32 devices in a mesh: dp: 8 (over z, y), mem: 4 (over x, core).
Axes of the slice: x: 2, y: 2, z: 4, core: 2. Of those that a mesh axis runs over, the one named last changes fastest.
Arguments:
- dec_input: bfloat16 [40, 128, 1024], P('dp'), may hold values from -6 to 6
- memory: bfloat16 [40, 1024, 1024], P('dp', 'mem'), may hold values from -6 to 6
- dec_len: int32 [40], P('dp'), may hold values from 1 to 128, as said below
- mem_len: int32 [40], P('dp'), may hold values from 1 to 1024, as said below
- self_in: bfloat16 [1024, 3, 1024], P(None, None, 'mem'), may hold values from -0.1875 to 0.1875
- self_in_bias: bfloat16 [2, 1024], P(None, 'mem'), may hold values from -3 to 3
- self_out: bfloat16 [1024, 1024], P('mem'), may hold values from -0.75 to 0.75
- cross_in: bfloat16 [1024, 3072], P('mem'), may hold values from -0.1875 to 0.1875
- cross_bias: bfloat16 [1024, 2], P('mem'), may hold values from -3 to 3
- cross_out: bfloat16 [1024, 1024], P('mem'), may hold values from -1.5 to 1.5
- fc_in: bfloat16 [1024, 4096], P(None, 'mem'), may hold values from -0.1875 to 0.1875
- fc_in_bias: bfloat16 [4096], P('mem'), may hold values from -3 to 3
- fc_out: bfloat16 [4096, 1024], P('mem'), may hold values from -0.09375 to 0.09375
- out_biases: bfloat16 [1024, 3], replicated, may hold values from -2 to 2
- norm_gains: bfloat16 [1024, 3], replicated, may hold values from 0.25 to 1.75
- norm_shifts: bfloat16 [1024, 3], replicated, may hold values from -2 to 2
- grad_out: bfloat16 [40, 128, 1024], P('dp'), may hold values from -6 to 6
Outputs:
- block_output: bfloat16 [40, 128, 1024], P('dp')
- input_grad: bfloat16 [40, 128, 1024], P('dp', None, 'mem')
- memory_grad: bfloat16 [40, 1024, 1024], P('dp', 'mem')
- self_in_grad: float32 [1024, 3, 1024], P(None, None, 'mem')
- self_in_bias_grad: float32 [2, 1024], P(None, 'mem')
- self_out_grad: float32 [1024, 1024], P('mem')
- cross_in_grad: float32 [1024, 3072], P(('dp', 'mem'))
- cross_bias_grad: float32 [1024, 2], P(('dp', 'mem'))
- cross_out_grad: float32 [1024, 1024], P(('dp', 'mem'))
- fc_in_grad: float32 [1024, 4096], P(None, 'mem')
- fc_in_bias_grad: float32 [4096], P('mem')
- fc_out_grad: float32 [4096, 1024], P('mem')
- out_biases_grad: float32 [1024, 3], P(('dp', 'mem'))
- gains_grad: float32 [1024, 3], P(('dp', 'mem'))
- shifts_grad: float32 [1024, 3], P(('dp', 'mem'))
The draws below stay inside these ranges and needn't reach their ends.
Inputs may be any that keep to these rules, and one draw needn't show every extreme that they name: `dec_len`: among the 5 items of each index of dp, one has length 128. `mem_len`: among the 5 items of each index of dp, one has length 1024.
All inputs are finite; a program needn't handle non-finite values.
Results may differ from the reference program's by a relative error of at most 0.03.
Values may be sent and summed in bfloat16 or wider, within the bound.
No kernel may reach another device: no remote copies, remote signals or barrier semaphores. Data moves between devices by JAX's collectives and lax.ppermute only.
A program may use at most 192 MiB of HBM per device.

```python
import jax
import jax.numpy as jnp
from jax import lax

D = 1024
HEAD_DIM = 64
FF = 4096
ITEMS_DEV = 5
DEC = 128
MEM_LEN = 1024
ITEMS = 40


def ragged_lengths(key, longest):
    blocks = ITEMS // ITEMS_DEV
    key_base, key_pick = jax.random.split(key)
    drawn = jax.random.randint(key_base, (blocks, ITEMS_DEV), 1, longest + 1)
    chosen = jax.random.randint(key_pick, (blocks, 1), 0, ITEMS_DEV)
    slot_ids = jnp.arange(ITEMS_DEV)[None, :]
    return jnp.where(slot_ids == chosen, longest, drawn).reshape(ITEMS).astype(jnp.int32)


def draw_dec_len(key, part):
    key = jax.random.fold_in(key, 11)
    return ragged_lengths(key, DEC)


def draw_mem_len(key, part):
    key = jax.random.fold_in(key, 23)
    return ragged_lengths(key, MEM_LEN)


def levels(own_key, shape, pieces, low, top_value):
    loudness = 1.0
    for dim, parts in pieces:
        draws = jax.random.uniform(jax.random.fold_in(jax.random.fold_in(own_key, 6), dim), (parts,), jnp.float32, low / len(pieces), top_value / len(pieces))
        loudness = loudness * jnp.repeat(jnp.exp(draws), shape[dim] // parts).reshape((-1,) + (1,) * (len(shape) - 1 - dim))
    return loudness


def scatter_about(stream_key, dims, spread, most, cuts=(), dtype=jnp.bfloat16):
    entries = jax.random.normal(stream_key, dims, jnp.float32) * spread
    if len(cuts) > 0:
        entries = levels(stream_key, dims, cuts, -0.22, 0.18) * entries
    return jnp.clip(entries, min=-most, max=most).astype(dtype)


def setup_inputs(seed: int = 0) -> dict:
    splits = jax.random.split(jax.random.key(seed), 18)
    dec_input = scatter_about(splits[0], (ITEMS, DEC, D), 1.0, 6.0, ((0, 8),))
    memory = scatter_about(splits[1], (ITEMS, MEM_LEN, D), 1.0, 6.0, ((0, 8), (1, 4)))
    dec_len = draw_dec_len(jax.random.fold_in(splits[17], 71), 0)
    mem_len = draw_mem_len(jax.random.fold_in(splits[17], 71), 0)
    self_in = scatter_about(splits[4], (D, 3, D), D ** -0.5, 0.1875, ((2, 4),))
    self_in_bias = scatter_about(splits[5], (2, D), 0.5, 3.0, ((1, 4),))
    self_out = scatter_about(splits[6], (D, D), (D // 16) ** -0.5, 0.75, ((0, 4),))
    cross_in = scatter_about(splits[7], (D, 3 * D), D ** -0.5, 0.1875, ((0, 4),))
    cross_bias = scatter_about(splits[8], (D, 2), 0.5, 3.0, ((0, 4),))
    cross_out = scatter_about(splits[9], (D, D), (D // 64) ** -0.5, 1.5, ((0, 4),))
    fc_in = scatter_about(splits[10], (D, FF), D ** -0.5, 0.1875, ((1, 4),))
    fc_in_bias = scatter_about(splits[11], (FF,), 0.5, 3.0, ((0, 4),))
    fc_out = scatter_about(splits[12], (FF, D), FF ** -0.5, 0.09375, ((0, 4),))
    out_biases = scatter_about(splits[13], (D, 3), 0.3, 2.0)
    norm_gains = jnp.clip(1.0 + 0.15 * jax.random.normal(splits[14], (D, 3), jnp.float32), 0.25, 1.75).astype(jnp.bfloat16)
    norm_shifts = scatter_about(splits[15], (D, 3), 0.3, 2.0)
    grad_out = scatter_about(splits[16], (ITEMS, DEC, D), 1.0, 6.0, ((0, 8),))
    return {"dec_input": dec_input, "memory": memory, "dec_len": dec_len, "mem_len": mem_len, "self_in": self_in, "self_in_bias": self_in_bias, "self_out": self_out, "cross_in": cross_in, "cross_bias": cross_bias, "cross_out": cross_out, "fc_in": fc_in, "fc_in_bias": fc_in_bias, "fc_out": fc_out, "out_biases": out_biases, "norm_gains": norm_gains, "norm_shifts": norm_shifts, "grad_out": grad_out}


MASKED = -1e+30
EPSILON = 1e-05

@jax.custom_vjp
def low(v):
    return lax.optimization_barrier(v.astype(jnp.bfloat16)).astype(jnp.float32)

@jax.custom_vjp
def low_back(v):
    return v

def low_keep(v):
    return (low(v), None)

def low_pass(kept, grad):
    return (grad,)

def back_keep(v):
    return (v, None)

def back_low(kept, grad):
    return (low(grad),)
low.defvjp(low_keep, low_pass)
low_back.defvjp(back_keep, back_low)

def matmul_high(left, right):
    return jnp.matmul(left, right, precision=lax.Precision.HIGHEST)

def einsum_high(form, left, right):
    return jnp.einsum(form, left, right, precision=lax.Precision.HIGHEST)

def norm_rows(resid, gain, shift):
    centre = resid - lax.optimization_barrier(jnp.mean(resid, axis=-1, keepdims=True))
    inverse = lax.rsqrt(lax.optimization_barrier(jnp.mean(centre * centre, axis=-1, keepdims=True)) + EPSILON)
    return centre * inverse * gain + shift

def layer_forward(params, dec_x, mem_x, dec_lengths, mem_lengths):
    self_in, self_in_bias, self_out, cross_in, cross_bias, cross_out, fc_in, fc_in_bias, fc_out, out_biases, norm_gains, norm_shifts = params
    item_count = dec_x.shape[0]
    model_width = dec_x.shape[2]
    heads_all = model_width // HEAD_DIM
    attn_scale = HEAD_DIM ** (-0.5)
    token_count = item_count * DEC
    flat_x = dec_x.reshape(token_count, model_width)
    query_self = low(low_back(matmul_high(flat_x, self_in[:, 0, :]) + self_in_bias[0]))
    key_self = low(low_back(matmul_high(flat_x, self_in[:, 1, :])))
    value_self = low(low_back(matmul_high(flat_x, self_in[:, 2, :]) + self_in_bias[1]))
    head_shape = (item_count, DEC, heads_all, HEAD_DIM)
    query_self = query_self.reshape(head_shape)
    key_self = key_self.reshape(head_shape)
    value_self = value_self.reshape(head_shape)
    positions = jnp.arange(DEC)
    causal = (positions[None, :] <= positions[:, None])[None, None]
    live_keys = (positions[None, :] < dec_lengths[:, None])[:, None, None, :]
    allowed = jnp.logical_and(causal, live_keys)
    raw_self = einsum_high('bihe,bjhe->bhij', query_self, key_self) * attn_scale
    scores_self = low_back(jnp.where(allowed, raw_self, MASKED))
    probs_self = jax.nn.softmax(scores_self, axis=-1)
    heads_self = einsum_high('bhij,bjhe->bihe', low(probs_self), value_self)
    heads_self = low(low_back(heads_self.reshape(token_count, model_width)))
    attended = low_back(matmul_high(heads_self, self_out)) + out_biases[:, 0]
    first = norm_rows(flat_x + attended, norm_gains[:, 0], norm_shifts[:, 0])
    first_low = low(first)
    flat_mem = mem_x.reshape(item_count * MEM_LEN, model_width)
    query_cross = low(low_back(matmul_high(first_low, cross_in[:, :model_width]) + cross_bias[:, 0]))
    key_cross = low(low_back(matmul_high(flat_mem, cross_in[:, model_width:2 * model_width])))
    value_cross = low(low_back(matmul_high(flat_mem, cross_in[:, 2 * model_width:]) + cross_bias[:, 1]))
    query_cross = query_cross.reshape(head_shape)
    mem_shape = (item_count, MEM_LEN, heads_all, HEAD_DIM)
    key_cross = key_cross.reshape(mem_shape)
    value_cross = value_cross.reshape(mem_shape)
    visible = (jnp.arange(MEM_LEN)[None, :] < mem_lengths[:, None])[:, None, None, :]
    raw_cross = einsum_high('bihe,bjhe->bhij', query_cross, key_cross) * attn_scale
    scores_cross = low_back(jnp.where(visible, raw_cross, MASKED))
    probs_cross = jax.nn.softmax(scores_cross, axis=-1)
    heads_cross = einsum_high('bhij,bjhe->bihe', low(probs_cross), value_cross)
    heads_cross = low(low_back(heads_cross.reshape(token_count, model_width)))
    crossed = low_back(matmul_high(heads_cross, cross_out)) + out_biases[:, 1]
    second = norm_rows(first + crossed, norm_gains[:, 1], norm_shifts[:, 1])
    second_low = low(second)
    pre_act = low_back(matmul_high(second_low, fc_in) + fc_in_bias)
    hidden = low(jax.nn.gelu(pre_act, approximate=False))
    fed = low_back(matmul_high(hidden, fc_out)) + out_biases[:, 2]
    final = norm_rows(second + fed, norm_gains[:, 2], norm_shifts[:, 2])
    return final.reshape(item_count, DEC, model_width)

def reference(dec_input, memory, dec_len, mem_len, self_in, self_in_bias, self_out, cross_in, cross_bias, cross_out, fc_in, fc_in_bias, fc_out, out_biases, norm_gains, norm_shifts, grad_out):
    params = tuple((weight.astype(jnp.float32) for weight in (self_in, self_in_bias, self_out, cross_in, cross_bias, cross_out, fc_in, fc_in_bias, fc_out, out_biases, norm_gains, norm_shifts)))
    blocks = ITEMS // ITEMS_DEV
    dec_blocks = dec_input.astype(jnp.float32).reshape(blocks, ITEMS_DEV, DEC, D)
    mem_blocks = memory.astype(jnp.float32).reshape(blocks, ITEMS_DEV, MEM_LEN, D)
    cot_blocks = grad_out.astype(jnp.float32).reshape(blocks, ITEMS_DEV, DEC, D)
    dec_lengths = dec_len.reshape(blocks, ITEMS_DEV)
    mem_lengths = mem_len.reshape(blocks, ITEMS_DEV)

    def one_block(totals, block):
        dec_x, mem_x, cotangent, dec_lens, mem_lens = block

        def apply_layer(weights, layer_in, layer_mem):
            return layer_forward(weights, layer_in, layer_mem, dec_lens, mem_lens)
        final, backward = jax.vjp(apply_layer, params, dec_x, mem_x)
        weight_grads, dec_grad, mem_grad = backward(cotangent)
        totals = jax.tree.map(jnp.add, totals, weight_grads)
        return (totals, (final.astype(jnp.bfloat16), dec_grad.astype(jnp.bfloat16), mem_grad.astype(jnp.bfloat16)))
    zeros = jax.tree.map(jnp.zeros_like, params)
    totals, (finals, dec_grads, mem_grads) = lax.scan(one_block, zeros, (dec_blocks, mem_blocks, cot_blocks, dec_lengths, mem_lengths))
    block_output = finals.reshape(ITEMS, DEC, D)
    input_grad = dec_grads.reshape(ITEMS, DEC, D)
    memory_grad = mem_grads.reshape(ITEMS, MEM_LEN, D)
    return (block_output, input_grad, memory_grad, totals[0], totals[1], totals[2], totals[3], totals[4], totals[5], totals[6], totals[7], totals[8], totals[9], totals[10], totals[11])
```

```python
import jax
import jax.numpy as jnp
from jax import lax
from jax.experimental import pallas as pl
from jax.experimental.pallas import tpu as pltpu
from jax.sharding import PartitionSpec as P

HEAD_DIM = 64
PAIR = 2 * HEAD_DIM
SCALE = HEAD_DIM ** (-0.5)
MASKED = -1e30
EPSILON = 1e-05
VMEM = 48 * 1024 * 1024

f32 = jnp.float32
bf16 = jnp.bfloat16


def to_low(values):
    return values.astype(bf16)


def nt(left, right):
    return lax.dot_general(left, right, (((1,), (1,)), ((), ())), preferred_element_type=f32)


def nn(left, right):
    return lax.dot_general(left, right, (((1,), (0,)), ((), ())), preferred_element_type=f32)


def tn(left, right):
    return lax.dot_general(left, right, (((0,), (0,)), ((), ())), preferred_element_type=f32)


def swap(values, axis, bit):
    pairs = [(i, i ^ bit) for i in range(lax.axis_size(axis))]
    return lax.ppermute(values, axis, pairs)


def has_bit(axis, bit):
    return (lax.axis_index(axis) & bit) != 0


def bits_of(axis):
    size, bits, bit = lax.axis_size(axis), [], 1
    while bit < size:
        bits.append(bit)
        bit *= 2
    return bits


def add_low(first, second):
    return to_low(first.astype(f32) + second.astype(f32))


def split_bit(values, axis, bit, dim):
    mine = has_bit(axis, bit).astype(jnp.int32)
    keep = lax.dynamic_index_in_dim(values, mine, dim, keepdims=False)
    send = lax.dynamic_index_in_dim(values, 1 - mine, dim, keepdims=False)
    return keep, send


def ordered(mine, theirs, axis, bit):
    second = has_bit(axis, bit)
    return jnp.where(second, theirs, mine), jnp.where(second, mine, theirs)


def mem_sum(partial):
    bits = bits_of("mem")
    half = partial.shape[1] // 2
    left, right = partial[:, :half], partial[:, half:]
    second = has_bit("mem", bits[0])
    keep = jnp.where(second, right, left)
    send = jnp.where(second, left, right)
    total = add_low(keep, swap(send, "mem", bits[0]))
    for bit in bits[1:]:
        total = add_low(total, swap(total, "mem", bit))
    low, high = ordered(total, swap(total, "mem", bits[0]), "mem", bits[0])
    return jnp.concatenate([low, high], axis=1)


def mem_rows_gather(shard):
    bits = bits_of("mem")
    values = shard[None]
    for bit in bits[1:]:
        low, high = ordered(values, swap(values, "mem", bit), "mem", bit)
        values = jnp.concatenate([low, high], axis=0)
    low, high = ordered(values, swap(values, "mem", bits[0]), "mem", bits[0])
    values = jnp.stack([low, high], axis=1)
    return values.reshape((-1,) + shard.shape[1:])


def dp_all_sum(values, order):
    for bit in order:
        halves = values.reshape((2, values.shape[0] // 2) + values.shape[1:])
        keep, send = split_bit(halves, "dp", bit, 0)
        values = add_low(keep, swap(send, "dp", bit))
    for bit in order[::-1]:
        low, high = ordered(values, swap(values, "dp", bit), "dp", bit)
        values = jnp.concatenate([low, high], axis=0)
    return values


def norm_parts(resid):
    centre = resid - jnp.mean(resid, axis=-1, keepdims=True)
    inverse = lax.rsqrt(jnp.mean(centre * centre, axis=-1, keepdims=True) + EPSILON)
    return (centre * inverse, inverse)


def norm_back(normed, inverse, gain, upstream):
    scaled = upstream * gain
    return inverse * (
        scaled
        - jnp.mean(scaled, axis=-1, keepdims=True)
        - normed * jnp.mean(scaled * normed, axis=-1, keepdims=True)
    )


def gelu_exact(pre_act):
    return jax.nn.gelu(pre_act, approximate=False)


def stacked(block, first_head):
    zero = jnp.zeros_like(block)
    return jnp.concatenate(
        [jnp.where(first_head, block, zero), jnp.where(first_head, zero, block)], axis=0
    )


def unstacked(both, first_head):
    rows = both.shape[0] // 2
    return jnp.where(first_head, both[:rows], both[rows:])


def first_lanes(rows):
    return lax.broadcasted_iota(jnp.int32, (rows, PAIR), 1) < HEAD_DIM


def row_sums(values, rows, first_head):
    lanes = lax.broadcasted_iota(jnp.int32, (16, PAIR), 1)
    which = lax.broadcasted_iota(jnp.int32, (16, PAIR), 0)
    pick = to_low((lanes // HEAD_DIM == which).astype(f32))
    high = to_low(values)
    low = to_low(values - high.astype(f32))
    sums = nt(pick, high) + nt(pick, low)
    return jnp.concatenate([sums[0:1], sums[1:2]], axis=1)


def cross_forward_kernel(len_ref, place_ref, q_ref, k_ref, v_ref, o_ref, stat_ref):
    item = pl.program_id(0)
    rows, steps = k_ref.shape[0], q_ref.shape[0]
    slot = place_ref[0] * rows + lax.broadcasted_iota(jnp.int32, (rows, 1), 0)
    visible = slot < len_ref[item]
    first_head = first_lanes(steps)
    for pair in range(q_ref.shape[1] // PAIR):
        lanes = slice(pair * PAIR, (pair + 1) * PAIR)
        query = stacked(q_ref[:, lanes] * SCALE, first_head)
        scores = jnp.where(visible, nt(k_ref[:, lanes], query), MASKED)
        top = jnp.max(scores, axis=0, keepdims=True)
        grown = jnp.exp(scores - top)
        total = jnp.sum(grown, axis=0, keepdims=True)
        weights = to_low(grown * (1.0 / total))
        o_ref[:, lanes] = to_low(unstacked(tn(weights, v_ref[:, lanes]), first_head))
        stat = top + jnp.log(total)
        stat_ref[0, 2 * pair : 2 * pair + 1, :] = stat[:, :steps]
        stat_ref[0, 2 * pair + 1 : 2 * pair + 2, :] = stat[:, steps:]


def cross_forward(lens, place, query, key, value, items):
    rows, width = key.shape[0] // items, key.shape[1]
    steps = query.shape[0] // items
    heads = width // HEAD_DIM
    block = lambda size: pl.BlockSpec((size, width), lambda i, *_: (i, 0))
    return pl.pallas_call(
        cross_forward_kernel,
        out_shape=(
            jax.ShapeDtypeStruct(query.shape, bf16),
            jax.ShapeDtypeStruct((items, heads, steps), f32),
        ),
        grid_spec=pltpu.PrefetchScalarGridSpec(
            num_scalar_prefetch=2,
            grid=(items,),
            in_specs=[block(steps), block(rows), block(rows)],
            out_specs=(block(steps), pl.BlockSpec((1, heads, steps), lambda i, *_: (i, 0, 0))),
        ),
        compiler_params=pltpu.CompilerParams(vmem_limit_bytes=VMEM),
        name="cross_forward",
    )(lens, place, query, key, value)


def merge_kernel(flip_ref, a_ref, sa_ref, b_ref, sb_ref, o_ref, stat_ref):
    flip = flip_ref[0] != 0
    mine, theirs = sa_ref[0], sb_ref[0]
    first, second = jnp.where(flip, theirs, mine), jnp.where(flip, mine, theirs)
    top = jnp.maximum(first, second)
    grown_first, grown_second = jnp.exp(first - top), jnp.exp(second - top)
    total = grown_first + grown_second
    stat_ref[0] = top + jnp.log(total)
    heads, width = first.shape[0], a_ref.shape[1]
    pick = lax.broadcasted_iota(jnp.int32, (heads, width), 1) // HEAD_DIM
    pick = to_low((pick == lax.broadcasted_iota(jnp.int32, (heads, width), 0)).astype(f32))

    def spread(share):
        high = to_low(share)
        return tn(high, pick) + tn(to_low(share - high.astype(f32)), pick)

    low_values = jnp.where(flip, b_ref[...], a_ref[...]).astype(f32)
    high_values = jnp.where(flip, a_ref[...], b_ref[...]).astype(f32)
    o_ref[...] = to_low(
        spread(grown_first / total) * low_values + spread(grown_second / total) * high_values
    )


def merge(flip, mine, stat_mine, theirs, stat_theirs):
    items, heads, steps = stat_mine.shape
    width = mine.shape[1]
    values = pl.BlockSpec((steps, width), lambda i, *_: (i, 0))
    stats = pl.BlockSpec((1, heads, steps), lambda i, *_: (i, 0, 0))
    return pl.pallas_call(
        merge_kernel,
        out_shape=(
            jax.ShapeDtypeStruct(mine.shape, bf16),
            jax.ShapeDtypeStruct(stat_mine.shape, f32),
        ),
        grid_spec=pltpu.PrefetchScalarGridSpec(
            num_scalar_prefetch=1,
            grid=(items,),
            in_specs=[values, stats, values, stats],
            out_specs=(values, stats),
        ),
        compiler_params=pltpu.CompilerParams(vmem_limit_bytes=VMEM),
        name="merge",
    )(flip, mine, stat_mine, theirs, stat_theirs)


def cross_backward_kernel(
    len_ref, place_ref, q_ref, k_ref, v_ref, o_ref, do_ref, stat_ref, dq_ref, dk_ref, dv_ref
):
    item = pl.program_id(0)
    rows, steps = k_ref.shape[0], q_ref.shape[0]
    slot = place_ref[0] * rows + lax.broadcasted_iota(jnp.int32, (rows, 1), 0)
    visible = slot < len_ref[item]
    first_head = first_lanes(steps)
    for pair in range(q_ref.shape[1] // PAIR):
        lanes = slice(pair * PAIR, (pair + 1) * PAIR)
        d_out = do_ref[:, lanes]
        dots = row_sums(d_out.astype(f32) * o_ref[:, lanes].astype(f32), steps, first_head)
        stat = jnp.concatenate(
            [stat_ref[0, 2 * pair : 2 * pair + 1, :], stat_ref[0, 2 * pair + 1 : 2 * pair + 2, :]],
            axis=1,
        )
        query = stacked(q_ref[:, lanes] * SCALE, first_head)
        d_both = stacked(d_out, first_head)
        key = k_ref[:, lanes]
        scores = jnp.where(visible, nt(key, query), MASKED)
        probs = jnp.exp(scores - stat)
        d_scores = to_low(probs * (nt(v_ref[:, lanes], d_both) - dots))
        dv_ref[:, lanes] = to_low(nn(to_low(probs), d_both))
        dk_ref[:, lanes] = to_low(nn(d_scores, query))
        dq_ref[:, lanes] = to_low(unstacked(tn(d_scores, key), first_head) * SCALE)


def cross_backward(lens, place, query, key, value, out, d_out, stat):
    items, heads, steps = stat.shape
    rows, width = key.shape[0] // items, key.shape[1]
    block = lambda size: pl.BlockSpec((size, width), lambda i, *_: (i, 0))
    stats = pl.BlockSpec((1, heads, steps), lambda i, *_: (i, 0, 0))
    return pl.pallas_call(
        cross_backward_kernel,
        out_shape=(
            jax.ShapeDtypeStruct(query.shape, bf16),
            jax.ShapeDtypeStruct(key.shape, bf16),
            jax.ShapeDtypeStruct(key.shape, bf16),
        ),
        grid_spec=pltpu.PrefetchScalarGridSpec(
            num_scalar_prefetch=2,
            grid=(items,),
            in_specs=[block(steps), block(rows), block(rows), block(steps), block(steps), stats],
            out_specs=(block(steps), block(rows), block(rows)),
        ),
        compiler_params=pltpu.CompilerParams(vmem_limit_bytes=VMEM),
        name="cross_backward",
    )(lens, place, query, key, value, out, d_out, stat)


def self_weights(len_ref, q_ref, k_ref, lanes, first_head, allowed):
    query = stacked(q_ref[:, lanes] * SCALE, first_head)
    scores = jnp.where(allowed, nt(k_ref[:, lanes], query), MASKED)
    top = jnp.max(scores, axis=0, keepdims=True)
    grown = jnp.exp(scores - top)
    total = jnp.sum(grown, axis=0, keepdims=True)
    return query, grown * (1.0 / total)


def self_allowed(len_ref, steps):
    keys = lax.broadcasted_iota(jnp.int32, (steps, 2 * steps), 0)
    queries = lax.broadcasted_iota(jnp.int32, (steps, 2 * steps), 1) % steps
    return jnp.logical_and(keys <= queries, keys < len_ref[pl.program_id(0)])


def self_forward_kernel(len_ref, q_ref, k_ref, v_ref, o_ref):
    steps = q_ref.shape[0]
    first_head = first_lanes(steps)
    allowed = self_allowed(len_ref, steps)
    for pair in range(q_ref.shape[1] // PAIR):
        lanes = slice(pair * PAIR, (pair + 1) * PAIR)
        _, probs = self_weights(len_ref, q_ref, k_ref, lanes, first_head, allowed)
        o_ref[:, lanes] = to_low(unstacked(tn(to_low(probs), v_ref[:, lanes]), first_head))


def self_backward_kernel(len_ref, q_ref, k_ref, v_ref, do_ref, dq_ref, dk_ref, dv_ref):
    steps = q_ref.shape[0]
    first_head = first_lanes(steps)
    allowed = self_allowed(len_ref, steps)
    for pair in range(q_ref.shape[1] // PAIR):
        lanes = slice(pair * PAIR, (pair + 1) * PAIR)
        query, probs = self_weights(len_ref, q_ref, k_ref, lanes, first_head, allowed)
        key = k_ref[:, lanes]
        d_both = stacked(do_ref[:, lanes], first_head)
        d_probs = nt(v_ref[:, lanes], d_both)
        dots = jnp.sum(probs * d_probs, axis=0, keepdims=True)
        d_scores = to_low(probs * (d_probs - dots))
        dv_ref[:, lanes] = to_low(nn(to_low(probs), d_both))
        dk_ref[:, lanes] = to_low(nn(d_scores, query))
        dq_ref[:, lanes] = to_low(unstacked(tn(d_scores, key), first_head) * SCALE)


def self_call(kernel, lens, arrays, outputs, name):
    items = lens.shape[0]
    tokens, width = arrays[0].shape
    block = pl.BlockSpec((tokens // items, width), lambda i, *_: (i, 0))
    return pl.pallas_call(
        kernel,
        out_shape=(jax.ShapeDtypeStruct((tokens, width), bf16),) * outputs,
        grid_spec=pltpu.PrefetchScalarGridSpec(
            num_scalar_prefetch=1,
            grid=(items,),
            in_specs=[block] * len(arrays),
            out_specs=(block,) * outputs,
        ),
        compiler_params=pltpu.CompilerParams(vmem_limit_bytes=VMEM),
        name=name,
    )(lens, *arrays)


def local(
    dec_input,
    memory,
    dec_len,
    mem_len,
    self_in,
    self_in_bias,
    self_out,
    cross_in,
    cross_bias,
    cross_out,
    fc_in,
    fc_in_bias,
    fc_out,
    out_biases,
    norm_gains,
    norm_shifts,
    grad_out,
):
    items, steps, width = dec_input.shape
    mem_rows = memory.shape[1]
    local_width = self_in.shape[2]
    tokens = items * steps
    mem_bits, dp_bits = bits_of("mem"), bits_of("dp")
    place = lax.axis_index("mem").astype(jnp.int32).reshape(1)
    biases = out_biases.astype(f32).T
    gains = norm_gains.astype(f32).T
    shifts = norm_shifts.astype(f32).T

    x_low = dec_input.reshape(tokens, width)
    mem_low = memory.reshape(items * mem_rows, width)

    weight_kv = mem_rows_gather(cross_in[:, width:])
    weight_query = mem_rows_gather(cross_in[:, :width])
    cross_shift = mem_rows_gather(cross_bias).astype(f32).T
    cross_back = mem_rows_gather(cross_out)

    weight_self = jnp.transpose(self_in, (1, 0, 2))
    bias_self = self_in_bias.astype(f32)
    query_self = to_low(nn(x_low, weight_self[0]) + bias_self[0])
    key_self = to_low(nn(x_low, weight_self[1]))
    value_self = to_low(nn(x_low, weight_self[2]) + bias_self[1])
    (heads_self,) = self_call(
        self_forward_kernel, dec_len, (query_self, key_self, value_self), 1, "self_forward"
    )
    arrived = mem_sum(to_low(nn(heads_self, self_out)))

    key_value = nn(mem_low, weight_kv)
    key_cross = to_low(key_value[:, :width])
    value_cross = to_low(key_value[:, width:] + cross_shift[1])

    normed_one, inverse_one = norm_parts(x_low.astype(f32) + arrived.astype(f32) + biases[0])
    first = normed_one * gains[0] + shifts[0]
    first_low = to_low(first)
    query_cross = to_low(nn(first_low, weight_query) + cross_shift[0])

    part, stat = cross_forward(mem_len, place, query_cross, key_cross, value_cross, items)
    half, half_heads = width // 2, width // HEAD_DIM // 2
    second_core = has_bit("mem", mem_bits[0])
    keep = jnp.where(second_core, part[:, half:], part[:, :half])
    send = jnp.where(second_core, part[:, :half], part[:, half:])
    stat_keep = jnp.where(second_core, stat[:, half_heads:], stat[:, :half_heads])
    stat_send = jnp.where(second_core, stat[:, :half_heads], stat[:, half_heads:])
    for bit in mem_bits:
        if bit != mem_bits[0]:
            send, stat_send = keep, stat_keep
        flip = has_bit("mem", bit).astype(jnp.int32).reshape(1)
        keep, stat_keep = merge(
            flip, keep, stat_keep, swap(send, "mem", bit), swap(stat_send, "mem", bit)
        )
    cross_heads = jnp.concatenate(
        ordered(keep, swap(keep, "mem", mem_bits[0]), "mem", mem_bits[0]), axis=1
    )
    stat = jnp.concatenate(
        ordered(stat_keep, swap(stat_keep, "mem", mem_bits[0]), "mem", mem_bits[0]), axis=1
    )

    normed_two, inverse_two = norm_parts(first + nn(cross_heads, cross_back) + biases[1])
    second = normed_two * gains[1] + shifts[1]
    second_low = to_low(second)

    pre_act = nn(second_low, fc_in) + fc_in_bias.astype(f32)
    hidden = to_low(gelu_exact(pre_act))
    fed = mem_sum(to_low(nn(hidden, fc_out)))
    normed_three, inverse_three = norm_parts(second + fed.astype(f32) + biases[2])
    final = normed_three * gains[2] + shifts[2]
    block_output = to_low(final).reshape(items, steps, width)

    upstream = grad_out.reshape(tokens, width).astype(f32)
    d_three = norm_back(normed_three, inverse_three, gains[2], upstream)
    gain_three = jnp.sum(upstream * normed_three, axis=0)
    shift_three = jnp.sum(upstream, axis=0)
    bias_three = jnp.sum(d_three, axis=0)
    d_three_low = to_low(d_three)
    gelu_back = jax.vjp(gelu_exact, pre_act)[1]
    d_pre_low = to_low(gelu_back(nt(d_three_low, fc_out))[0])
    arrived = mem_sum(to_low(nt(d_pre_low, fc_in)))
    d_fc_in_bias = jnp.sum(d_pre_low.astype(f32), axis=0)
    d_fc_out = to_low(tn(hidden, d_three_low))
    d_fc_in = to_low(tn(second_low, d_pre_low))

    d_second = d_three + arrived.astype(f32)
    d_two = norm_back(normed_two, inverse_two, gains[1], d_second)
    gain_two = jnp.sum(d_second * normed_two, axis=0)
    shift_two = jnp.sum(d_second, axis=0)
    bias_two = jnp.sum(d_two, axis=0)
    d_two_low = to_low(d_two)
    d_heads_cross = to_low(nt(d_two_low, cross_back))

    d_query_part, d_key_cross, d_value_cross = cross_backward(
        mem_len, place, query_cross, key_cross, value_cross, cross_heads, d_heads_cross, stat
    )
    d_query_cross = mem_sum(d_query_part)

    d_first = d_two + nt(d_query_cross, weight_query)
    d_one = norm_back(normed_one, inverse_one, gains[0], d_first)
    gain_one = jnp.sum(d_first * normed_one, axis=0)
    shift_one = jnp.sum(d_first, axis=0)
    bias_one = jnp.sum(d_one, axis=0)
    d_one_low = to_low(d_one)

    d_heads_self = to_low(nt(d_one_low, self_out))
    d_query, d_key, d_value = self_call(
        self_backward_kernel,
        dec_len,
        (query_self, key_self, value_self, d_heads_self),
        3,
        "self_backward",
    )
    partial_input = to_low(
        nt(d_query, weight_self[0]) + nt(d_key, weight_self[1]) + nt(d_value, weight_self[2])
    )
    pieces = partial_input.reshape((tokens,) + (2,) * len(mem_bits) + (local_width,))
    for bit in mem_bits:
        dim = pieces.ndim - 2
        keep, send = split_bit(pieces, "mem", bit, dim)
        pieces = add_low(keep, swap(send, "mem", bit))
    own = lax.dynamic_slice_in_dim(d_one, place[0] * local_width, local_width, 1)
    input_grad = to_low(own + pieces.astype(f32)).reshape(items, steps, local_width)

    order_one = dp_bits
    order_two = dp_bits[1:2] + dp_bits[:1] + dp_bits[2:]
    fed_rows = d_fc_in.shape[0]
    fc_grads = [
        dp_all_sum(
            jnp.concatenate([d_fc_in, d_fc_out.reshape(d_fc_in.shape)], axis=1)[rows], order
        )
        for rows, order in (
            (slice(None, fed_rows // 2), order_one),
            (slice(fed_rows // 2, None), order_two),
        )
    ]
    fc_grads = jnp.concatenate(fc_grads, axis=0).astype(f32)
    fc_in_grad = fc_grads[:, : fc_in.shape[1]]
    fc_out_grad = fc_grads[:, fc_in.shape[1] :].reshape(fc_out.shape)

    d_self = [to_low(tn(x_low, grad)) for grad in (d_query, d_key, d_value)]
    d_self_out = to_low(tn(heads_self, d_one_low))
    d_self_out = jnp.concatenate(
        [d_self_out[:, at : at + local_width] for at in range(0, width, local_width)], axis=0
    )
    self_one = dp_all_sum(jnp.concatenate(d_self[:2], axis=0), order_one)
    self_two = dp_all_sum(jnp.concatenate([d_self[2], d_self_out], axis=0), order_two)
    self_in_grad = jnp.stack(
        [self_one[:width], self_one[width:], self_two[:width]], axis=1
    ).astype(f32)
    self_out_grad = jnp.concatenate(
        [self_two[width + at : width + at + local_width] for at in range(0, width, local_width)],
        axis=1,
    ).astype(f32)

    small = [
        gain_one,
        gain_two,
        gain_three,
        shift_one,
        shift_two,
        shift_three,
        bias_one,
        bias_two,
        bias_three,
        jnp.sum(d_query_cross.astype(f32), axis=0),
        jnp.sum(d_heads_cross.astype(f32), axis=0),
    ]
    extra = [
        d_fc_in_bias,
        jnp.sum(d_query.astype(f32), axis=0),
        jnp.sum(d_heads_self.astype(f32), axis=0),
    ]
    rows = [jnp.pad(row, (0, width - row.shape[0])) for row in small + extra]
    rows = rows + [jnp.zeros_like(rows[0])] * (16 - len(rows))
    rows = jnp.stack(rows, axis=0)
    for bit in dp_bits:
        rows = rows + swap(rows, "dp", bit)
    shard = width // (lax.axis_size("dp") * lax.axis_size("mem"))
    spot = lax.axis_index("dp") * lax.axis_size("mem") + lax.axis_index("mem")
    owned = lax.dynamic_slice_in_dim(rows, spot * shard, shard, 1)
    gains_grad, shifts_grad, out_biases_grad = owned[0:3].T, owned[3:6].T, owned[6:9].T
    cross_bias_grad = owned[9:11].T
    fc_in_bias_grad = rows[11, : fc_in_bias.shape[0]]
    self_in_bias_grad = rows[12:14, :local_width]

    d_kv = to_low(tn(mem_low, jnp.concatenate([d_key_cross, d_value_cross], axis=1)))
    d_kv = d_kv.reshape((lax.axis_size("dp"),) + (2,) * len(mem_bits) + (shard, 2 * width))
    for bit in mem_bits:
        dim = d_kv.ndim - 3
        keep, send = split_bit(d_kv, "mem", bit, dim)
        d_kv = add_low(keep, swap(send, "mem", bit))
    col = lax.broadcasted_iota(jnp.int32, (width, width // lax.axis_size("mem")), 1)
    row = lax.broadcasted_iota(jnp.int32, (width, width // lax.axis_size("mem")), 0)
    wanted = (col // shard * lax.axis_size("mem") + place[0]) * shard + col % shard
    choose = to_low((row == wanted).astype(f32))
    d_q = to_low(tn(to_low(nn(first_low, choose)), d_query_cross))
    d_out = to_low(tn(to_low(nn(cross_heads, choose)), d_two_low))
    by_rows = lambda v: v.reshape(lax.axis_size("dp"), shard, -1)
    cross_rows = jnp.concatenate([by_rows(d_q), d_kv, by_rows(d_out)], axis=2)
    cross_rows = cross_rows.reshape((2,) * len(dp_bits) + cross_rows.shape[1:])
    for bit in dp_bits:
        dim = cross_rows.ndim - 3
        keep, send = split_bit(cross_rows, "dp", bit, dim)
        cross_rows = add_low(keep, swap(send, "dp", bit))
    cross_in_grad = cross_rows[:, : 3 * width].astype(f32)
    cross_out_grad = cross_rows[:, 3 * width :].astype(f32)

    memory_grad = to_low(
        nt(d_key_cross, weight_kv[:, :width]) + nt(d_value_cross, weight_kv[:, width:])
    ).reshape(items, mem_rows, width)

    return (
        block_output,
        input_grad,
        memory_grad,
        self_in_grad,
        self_in_bias_grad,
        self_out_grad,
        cross_in_grad,
        cross_bias_grad,
        cross_out_grad,
        fc_in_grad,
        fc_in_bias_grad,
        fc_out_grad,
        out_biases_grad,
        gains_grad,
        shifts_grad,
    )


def solution(mesh):
    placed = (
        P("dp", None, None),
        P("dp", "mem", None),
        P("dp"),
        P("dp"),
        P(None, None, "mem"),
        P(None, "mem"),
        P("mem", None),
        P("mem", None),
        P("mem", None),
        P("mem", None),
        P(None, "mem"),
        P("mem"),
        P("mem", None),
        P(),
        P(),
        P(),
        P("dp", None, None),
    )
    return jax.shard_map(
        local,
        mesh=mesh,
        in_specs=placed,
        out_specs=(
            P("dp", None, None),
            P("dp", None, "mem"),
            P("dp", "mem", None),
            P(None, None, "mem"),
            P(None, "mem"),
            P("mem", None),
            P(("dp", "mem"), None),
            P(("dp", "mem"), None),
            P(("dp", "mem"), None),
            P(None, "mem"),
            P("mem"),
            P("mem", None),
            P(("dp", "mem"), None),
            P(("dp", "mem"), None),
            P(("dp", "mem"), None),
        ),
        check_vma=False,
    )
```

```python
import functools

import jax
import jax.numpy as jnp
from jax import lax
from jax.experimental import pallas as pl
from jax.experimental.pallas import tpu as pltpu
from jax.sharding import PartitionSpec as P

HEAD_DIM = 64
PAIR = 2 * HEAD_DIM
CORE = 1
SCALE = HEAD_DIM ** (-0.5)
MASKED = -1e30
EPSILON = 1e-05
TILE = 256
MEGA = 1024 * 1024

f32 = jnp.float32
bf16 = jnp.bfloat16


def to_low(values):
    return values.astype(bf16)


def nt(left, right):
    return lax.dot_general(left, right, (((1,), (1,)), ((), ())), preferred_element_type=f32)


def nn(left, right):
    return lax.dot_general(left, right, (((1,), (0,)), ((), ())), preferred_element_type=f32)


def tn(left, right):
    return lax.dot_general(left, right, (((0,), (0,)), ((), ())), preferred_element_type=f32)


def col_sum(values):
    return jnp.sum(values, axis=0, keepdims=True)


def swap(values, axis, bit):
    pairs = [(i, i ^ bit) for i in range(lax.axis_size(axis))]
    return lax.ppermute(values, axis, pairs)


def core_swap(values):
    return swap(values, "mem", CORE)


def bits_of(axis):
    size, bits, bit = lax.axis_size(axis), [], 1
    while bit < size:
        bits.append(bit)
        bit *= 2
    return bits


def chip_bits():
    return bits_of("mem")[1:]


def bit_at(axis, bit):
    return (lax.axis_index(axis) // bit % 2).astype(jnp.int32)


def after(values, *others):
    return lax.optimization_barrier((values,) + others)[0]


def add_low(first, second):
    return to_low(first.astype(f32) + second.astype(f32))


def chip_swap(values):
    bits = chip_bits()
    for bit in bits[:-1]:
        values = add_low(values, swap(values, "mem", bit))
    return values, swap(values, "mem", bits[-1])


def relative(pieces, bits):
    for bit in bits:
        pieces = pieces | {r ^ bit: swap(piece, "mem", bit) for r, piece in pieces.items()}
    return pieces


def whole(shape):
    return pl.BlockSpec(shape, lambda *_: (0,) * len(shape))


HBM = pl.BlockSpec(memory_space=pl.ANY)


def call(
    kernel, info, inputs, outputs, scratch=(), grid=(1,), out_specs=None, mega=20, name=None
):
    arrays = [given[0] if isinstance(given, tuple) else given for given in inputs]
    specs = [given[1] if isinstance(given, tuple) else whole(given.shape) for given in inputs]
    return pl.pallas_call(
        kernel,
        out_shape=[jax.ShapeDtypeStruct(*out) for out in outputs],
        grid_spec=pltpu.PrefetchScalarGridSpec(
            num_scalar_prefetch=1,
            grid=grid,
            in_specs=specs,
            out_specs=out_specs or [whole(out[0]) for out in outputs],
            scratch_shapes=list(scratch),
        ),
        compiler_params=pltpu.CompilerParams(vmem_limit_bytes=mega * MEGA),
        cost_estimate=pl.CostEstimate(flops=1, bytes_accessed=1, transcendentals=0),
        name=name or kernel.__name__,
    )(info, *arrays)


def dp_position(bit):
    return DP_AT + bit.bit_length() - 1


def norm_parts(resid):
    centre = resid - jnp.mean(resid, axis=-1, keepdims=True)
    inverse = lax.rsqrt(jnp.mean(centre * centre, axis=-1, keepdims=True) + EPSILON)
    return (centre * inverse, inverse)


def norm_back(normed, inverse, gain, upstream):
    scaled = upstream * gain
    return inverse * (
        scaled
        - jnp.mean(scaled, axis=-1, keepdims=True)
        - normed * jnp.mean(scaled * normed, axis=-1, keepdims=True)
    )


def row(ref, at):
    return ref[at : at + 1, :]


def wide(ref):
    return ref[...].astype(f32)


def halves(core, mine, theirs):
    first = core == 0
    return jnp.where(first, mine, theirs), jnp.where(first, theirs, mine)


def dyn(start, size, unit=16):
    return pl.ds(pl.multiple_of(start, unit), size)


PLACE, CORE_AT, DP_AT, LENS = 0, 1, 3, 8
GAIN, SHIFT, BIAS, QUERY_BIAS = 0, 3, 6, 9


def assemble_kernel(ids, parts, s_ref, *refs):
    sources, outs, sem = refs[: len(ids)], refs[len(ids) : -1], refs[-1]
    rows = sources[0].shape[0]
    copies = []
    for source, r in zip(sources, ids):
        at = dyn((s_ref[PLACE] ^ r) * rows, rows)
        for out, start, step, to, width in parts:
            columns = pl.ds(pl.multiple_of(start + s_ref[CORE_AT] * step, 128), width)
            copies.append(
                pltpu.make_async_copy(
                    source.at[:, columns],
                    outs[out].at[at, pl.ds(to, width)],
                    sem.at[len(copies)],
                )
            )
    for copy in copies:
        copy.start()
    for copy in copies:
        copy.wait()


def assemble(info, pieces, parts, outputs, name):
    return call(
        functools.partial(assemble_kernel, tuple(pieces), parts),
        info,
        [(piece, HBM) for piece in pieces.values()],
        outputs,
        scratch=[pltpu.SemaphoreType.DMA((len(pieces) * len(parts),))],
        out_specs=[HBM] * len(outputs),
        name=name,
    )


def first_norm_kernel(
    s_ref, x_ref, mine_ref, came_ref, vec_ref, wq_ref, normed_ref, inv_ref, low_ref, keep_ref, send_ref
):
    resid = wide(x_ref) + (wide(mine_ref) + wide(came_ref)) + row(vec_ref, BIAS)
    normed, inverse = norm_parts(resid)
    normed_ref[...] = normed
    inv_ref[...] = inverse
    low = to_low(normed * row(vec_ref, GAIN) + row(vec_ref, SHIFT))
    low_ref[...] = low
    half = keep_ref.shape[1]
    left, right = (
        to_low(nn(low, wq_ref[:, part]) + vec_ref[QUERY_BIAS : QUERY_BIAS + 1, part])
        for part in (slice(0, half), slice(half, 2 * half))
    )
    keep_ref[...], send_ref[...] = halves(s_ref[CORE_AT], left, right)


def middle_kernel(
    s_ref,
    normed_ref,
    mine_ref,
    came_ref,
    vec_ref,
    bias_ref,
    bias_far_ref,
    back_hbm,
    in_hbm,
    in_far_hbm,
    out_hbm,
    out_far_hbm,
    heads_ref,
    normed_two_ref,
    inv_ref,
    low_ref,
    hidden_ref,
    hidden_far_ref,
    slope_ref,
    slope_far_ref,
    fed_ref,
    back,
    w_in,
    w_in_far,
    w_out,
    w_out_far,
    sem,
):
    loads = []
    for i, (source, target) in enumerate(
        (
            (back_hbm, back),
            (in_hbm, w_in),
            (in_far_hbm, w_in_far),
            (out_hbm, w_out),
            (out_far_hbm, w_out_far),
        )
    ):
        loads.append(pltpu.make_async_copy(source, target, sem.at[i]))
        loads[i].start()
    heads = jnp.concatenate(halves(s_ref[CORE_AT], mine_ref[...], came_ref[...]), axis=1)
    heads_ref[...] = heads
    first = normed_ref[...] * row(vec_ref, GAIN) + row(vec_ref, SHIFT)
    loads[0].wait()
    normed, inverse = norm_parts(first + nn(heads, back[...]) + row(vec_ref, BIAS + 1))
    normed_two_ref[...] = normed
    inv_ref[...] = inverse
    low = to_low(normed * row(vec_ref, GAIN + 1) + row(vec_ref, SHIFT + 1))
    low_ref[...] = low
    for i, (weight, shift, hidden, slope) in enumerate(
        ((w_in, bias_ref, hidden_ref, slope_ref), (w_in_far, bias_far_ref, hidden_far_ref, slope_far_ref))
    ):
        loads[1 + i].wait()
        for at in range(0, weight.shape[1], TILE):
            part = slice(at, at + TILE)
            pre = nn(low, weight[:, part]) + shift[:, part]
            share = 0.5 * (1.0 + lax.erf(pre * (0.5**0.5)))
            hidden[:, part] = to_low(pre * share)
            density = jnp.exp(-0.5 * pre * pre) * (1.0 / (2.0 * jnp.pi) ** 0.5)
            slope[:, part] = to_low(share + pre * density)
    loads[3].wait()
    loads[4].wait()
    for at in range(0, fed_ref.shape[1], TILE):
        part = slice(at, at + TILE)
        fed_ref[:, part] = to_low(
            nn(hidden_ref[...], w_out[:, part]) + nn(hidden_far_ref[...], w_out_far[:, part])
        )


def turn_kernel(
    s_ref,
    normed_two_ref,
    mine_ref,
    came_ref,
    vec_ref,
    grad_ref,
    slope_ref,
    slope_far_ref,
    in_hbm,
    in_far_hbm,
    out_hbm,
    out_far_hbm,
    final_ref,
    d_ref,
    d_low_ref,
    pre_ref,
    pre_far_ref,
    part_ref,
    sums_ref,
    pre_sums_ref,
    w_in,
    w_in_far,
    w_out,
    w_out_far,
    sem,
):
    loads = []
    for i, (source, target) in enumerate(
        ((out_hbm, w_out), (out_far_hbm, w_out_far), (in_hbm, w_in), (in_far_hbm, w_in_far))
    ):
        loads.append(pltpu.make_async_copy(source, target, sem.at[i]))
        loads[i].start()
    second = normed_two_ref[...] * row(vec_ref, GAIN + 1) + row(vec_ref, SHIFT + 1)
    resid = second + (wide(mine_ref) + wide(came_ref)) + row(vec_ref, BIAS + 2)
    normed, inverse = norm_parts(resid)
    gain = row(vec_ref, GAIN + 2)
    final_ref[...] = to_low(normed * gain + row(vec_ref, SHIFT + 2))
    upstream = wide(grad_ref)
    d_resid = norm_back(normed, inverse, gain, upstream)
    d_ref[...] = d_resid
    d_low = to_low(d_resid)
    d_low_ref[...] = d_low
    sums_ref[...] = jnp.zeros_like(sums_ref)
    sums_ref[0:1, :] = col_sum(upstream * normed)
    sums_ref[1:2, :] = col_sum(upstream)
    sums_ref[2:3, :] = col_sum(d_resid)
    pre_sums_ref[...] = jnp.zeros_like(pre_sums_ref)
    for i, (weight, slope, pre) in enumerate(
        ((w_out, slope_ref, pre_ref), (w_out_far, slope_far_ref, pre_far_ref))
    ):
        loads[i].wait()
        for at in range(0, weight.shape[0], TILE):
            part = slice(at, at + TILE)
            d_pre = to_low(nt(d_low, weight[part, :]) * slope[:, part].astype(f32))
            pre[:, part] = d_pre
            pre_sums_ref[i : i + 1, part] = col_sum(d_pre.astype(f32))
    loads[2].wait()
    loads[3].wait()
    for at in range(0, part_ref.shape[1], TILE):
        part = slice(at, at + TILE)
        part_ref[:, part] = to_low(
            nt(pre_ref[...], w_in[part, :]) + nt(pre_far_ref[...], w_in_far[part, :])
        )


def second_back_kernel(
    s_ref,
    d_three_ref,
    mine_ref,
    came_ref,
    normed_ref,
    inv_ref,
    vec_ref,
    back_ref,
    d_ref,
    d_low_ref,
    keep_ref,
    send_ref,
    sums_ref,
):
    upstream = d_three_ref[...] + (wide(mine_ref) + wide(came_ref))
    normed = normed_ref[...]
    d_resid = norm_back(normed, inv_ref[...], row(vec_ref, GAIN + 1), upstream)
    d_ref[...] = d_resid
    d_low = to_low(d_resid)
    d_low_ref[...] = d_low
    half = keep_ref.shape[1]
    left = to_low(nt(d_low, back_ref[:half, :]))
    right = to_low(nt(d_low, back_ref[half:, :]))
    keep_ref[...], send_ref[...] = halves(s_ref[CORE_AT], left, right)
    sums_ref[...] = jnp.zeros_like(sums_ref)
    sums_ref[0:1, :] = col_sum(upstream * normed)
    sums_ref[1:2, :] = col_sum(upstream)
    sums_ref[2:3, :] = col_sum(d_resid)
    sums_ref[3:4, :half] = col_sum(left.astype(f32))
    sums_ref[3:4, half:] = col_sum(right.astype(f32))


def split_sum_kernel(s_ref, mine_ref, came_ref, keep_ref, send_ref):
    rows = keep_ref.shape[0]
    for out, core in ((send_ref, 1 - s_ref[CORE_AT]), (keep_ref, s_ref[CORE_AT])):
        part = dyn(core * rows, rows)
        out[...] = add_low(mine_ref[part, :], came_ref[part, :])


def first_back_kernel(
    s_ref,
    d_two_ref,
    mine_ref,
    came_ref,
    normed_ref,
    inv_ref,
    vec_ref,
    wq_ref,
    d_low_ref,
    query_ref,
    sums_ref,
):
    d_query = jnp.concatenate(halves(s_ref[CORE_AT], mine_ref[...], came_ref[...]), axis=1)
    query_ref[...] = d_query
    upstream = d_two_ref[...] + nt(d_query, wq_ref[...])
    normed = normed_ref[...]
    d_resid = norm_back(normed, inv_ref[...], row(vec_ref, GAIN), upstream)
    d_low_ref[...] = to_low(d_resid)
    sums_ref[...] = jnp.zeros_like(sums_ref)
    sums_ref[0:1, :] = col_sum(upstream * normed)
    sums_ref[1:2, :] = col_sum(upstream)
    sums_ref[2:3, :] = col_sum(d_resid)
    sums_ref[3:4, :] = col_sum(d_query.astype(f32))


def stacked(block, first_head):
    zero = jnp.zeros_like(block)
    return jnp.concatenate(
        [jnp.where(first_head, block, zero), jnp.where(first_head, zero, block)], axis=0
    )


def unstacked(both, first_head):
    rows = both.shape[0] // 2
    return jnp.where(first_head, both[:rows], both[rows:])


def first_lanes(rows):
    return lax.broadcasted_iota(jnp.int32, (rows, PAIR), 1) < HEAD_DIM


def row_sums(values):
    lanes = lax.broadcasted_iota(jnp.int32, (16, PAIR), 1)
    which = lax.broadcasted_iota(jnp.int32, (16, PAIR), 0)
    pick = to_low((lanes // HEAD_DIM == which).astype(f32))
    high = to_low(values)
    low = to_low(values - high.astype(f32))
    sums = nt(pick, high) + nt(pick, low)
    return jnp.concatenate([sums[0:1], sums[1:2]], axis=1)


def shown(length, place, rows):
    spot = lax.broadcasted_iota(jnp.int32, (rows, 1), 0)
    return jnp.concatenate(
        [place * rows + spot < length, (place ^ CORE) * rows + spot < length], axis=0
    )


def join_rows(core, mine_ref, came_ref, both):
    rows = mine_ref.shape[0]
    both[dyn(core * rows, rows), :] = mine_ref[...]
    both[dyn((1 - core) * rows, rows), :] = came_ref[...]


def cross_forward_kernel(s_ref, mine_ref, came_ref, near_ref, far_ref, o_ref, stat_ref, both):
    item = pl.program_id(0)

    @pl.when(item == 0)
    def _():
        join_rows(s_ref[CORE_AT], mine_ref, came_ref, both)

    steps, width = o_ref.shape
    rows = dyn(item * steps, steps)
    visible = shown(s_ref[LENS + item], s_ref[PLACE], near_ref.shape[0])
    first_head = first_lanes(steps)
    for pair in range(width // PAIR):
        lanes = slice(pair * PAIR, (pair + 1) * PAIR)
        values = slice(width + pair * PAIR, width + (pair + 1) * PAIR)
        query = stacked(both[rows, lanes] * SCALE, first_head)
        key = jnp.concatenate([near_ref[:, lanes], far_ref[:, lanes]], axis=0)
        value = jnp.concatenate([near_ref[:, values], far_ref[:, values]], axis=0)
        scores = jnp.where(visible, nt(key, query), MASKED)
        top = jnp.max(scores, axis=0, keepdims=True)
        grown = jnp.exp(scores - top)
        total = jnp.sum(grown, axis=0, keepdims=True)
        weights = to_low(grown * (1.0 / total))
        o_ref[:, lanes] = to_low(unstacked(tn(weights, value), first_head))
        stat = top + jnp.log(total)
        stat_ref[0, 2 * pair : 2 * pair + 1, :] = stat[:, :steps]
        stat_ref[0, 2 * pair + 1 : 2 * pair + 2, :] = stat[:, steps:]


def cross_forward(info, items, mine, came, near, far):
    width, tokens = mine.shape[1], 2 * mine.shape[0]
    rows, steps = near.shape[0] // items, tokens // items
    heads = width // HEAD_DIM
    keys = pl.BlockSpec((rows, 2 * width), lambda i, *_: (i, 0))
    return call(
        cross_forward_kernel,
        info,
        [mine, came, (near, keys), (far, keys)],
        [((tokens, width), bf16), ((items, heads, steps), f32)],
        scratch=[pltpu.VMEM((tokens, width), bf16)],
        grid=(items,),
        mega=32,
        out_specs=[
            pl.BlockSpec((steps, width), lambda i, *_: (i, 0)),
            pl.BlockSpec((1, heads, steps), lambda i, *_: (i, 0, 0)),
        ],
    )


def merge_kernel(bit, s_ref, a_ref, sa_ref, b_ref, sb_ref, o_ref, stat_ref):
    flip = (s_ref[PLACE] & bit) != 0
    items, heads, steps = sa_ref.shape
    width = a_ref.shape[1]
    pick = lax.broadcasted_iota(jnp.int32, (heads, width), 1) // HEAD_DIM
    pick = to_low((pick == lax.broadcasted_iota(jnp.int32, (heads, width), 0)).astype(f32))

    def spread(share):
        high = to_low(share)
        return tn(high, pick) + tn(to_low(share - high.astype(f32)), pick)

    for item in range(items):
        rows = slice(item * steps, (item + 1) * steps)
        mine, theirs = sa_ref[item], sb_ref[item]
        first, second = jnp.where(flip, theirs, mine), jnp.where(flip, mine, theirs)
        top = jnp.maximum(first, second)
        grown_first, grown_second = jnp.exp(first - top), jnp.exp(second - top)
        total = grown_first + grown_second
        stat_ref[item] = top + jnp.log(total)
        low_values = jnp.where(flip, b_ref[rows, :], a_ref[rows, :]).astype(f32)
        high_values = jnp.where(flip, a_ref[rows, :], b_ref[rows, :]).astype(f32)
        o_ref[rows, :] = to_low(
            spread(grown_first / total) * low_values + spread(grown_second / total) * high_values
        )


def merge(info, bit, mine, stat_mine, theirs, stat_theirs):
    return call(
        functools.partial(merge_kernel, bit),
        info,
        [mine, stat_mine, theirs, stat_theirs],
        [(mine.shape, bf16), (stat_mine.shape, f32)],
        name="merge",
    )


def cross_backward_kernel(
    s_ref, q_ref, q_came_ref, do_mine_ref, do_came_ref, o_ref, stat_ref, near_ref, far_ref,
    dq_ref, dnear_ref, dfar_ref, q_both, do_both,
):
    item = pl.program_id(0)

    @pl.when(item == 0)
    def _():
        join_rows(s_ref[CORE_AT], q_ref, q_came_ref, q_both)
        join_rows(s_ref[CORE_AT], do_mine_ref, do_came_ref, do_both)

    steps, width = dq_ref.shape
    rows = near_ref.shape[0]
    tokens = dyn(item * steps, steps)
    visible = shown(s_ref[LENS + item], s_ref[PLACE], rows)
    first_head = first_lanes(steps)
    for pair in range(width // PAIR):
        lanes = slice(pair * PAIR, (pair + 1) * PAIR)
        values = slice(width + pair * PAIR, width + (pair + 1) * PAIR)
        d_out = do_both[tokens, lanes]
        dots = row_sums(d_out.astype(f32) * o_ref[:, lanes].astype(f32))
        stat = jnp.concatenate(
            [stat_ref[0, 2 * pair : 2 * pair + 1, :], stat_ref[0, 2 * pair + 1 : 2 * pair + 2, :]],
            axis=1,
        )
        query = stacked(q_both[tokens, lanes] * SCALE, first_head)
        d_both = stacked(d_out, first_head)
        key = jnp.concatenate([near_ref[:, lanes], far_ref[:, lanes]], axis=0)
        value = jnp.concatenate([near_ref[:, values], far_ref[:, values]], axis=0)
        scores = jnp.where(visible, nt(key, query), MASKED)
        probs = jnp.exp(scores - stat)
        d_scores = to_low(probs * (nt(value, d_both) - dots))
        d_value = to_low(nn(to_low(probs), d_both))
        d_key = to_low(nn(d_scores, query))
        dnear_ref[:, lanes] = d_key[:rows]
        dfar_ref[:, lanes] = d_key[rows:]
        dnear_ref[:, values] = d_value[:rows]
        dfar_ref[:, values] = d_value[rows:]
        dq_ref[:, lanes] = to_low(unstacked(tn(d_scores, key), first_head) * SCALE)


def cross_backward(info, queries, d_outs, out, stat, near, far):
    items, heads, steps = stat.shape
    tokens, width = out.shape
    rows = near.shape[0] // items
    keys = pl.BlockSpec((rows, 2 * width), lambda i, *_: (i, 0))
    block = pl.BlockSpec((steps, width), lambda i, *_: (i, 0))
    return call(
        cross_backward_kernel,
        info,
        list(queries)
        + list(d_outs)
        + [
            (out, block),
            (stat, pl.BlockSpec((1, heads, steps), lambda i, *_: (i, 0, 0))),
            (near, keys),
            (far, keys),
        ],
        [(out.shape, bf16), (near.shape, bf16), (far.shape, bf16)],
        scratch=[pltpu.VMEM((tokens, width), bf16)] * 2,
        grid=(items,),
        mega=32,
        out_specs=[block, keys, keys],
    )


def self_weights(query_block, key_block, first_head, allowed):
    query = stacked(query_block * SCALE, first_head)
    scores = jnp.where(allowed, nt(key_block, query), MASKED)
    top = jnp.max(scores, axis=0, keepdims=True)
    grown = jnp.exp(scores - top)
    total = jnp.sum(grown, axis=0, keepdims=True)
    return query, grown * (1.0 / total)


def self_parts(len_ref, items, tokens, width):
    steps = tokens // items
    keys = lax.broadcasted_iota(jnp.int32, (steps, 2 * steps), 0)
    queries = lax.broadcasted_iota(jnp.int32, (steps, 2 * steps), 1) % steps
    causal = keys <= queries
    for item in range(items):
        allowed = jnp.logical_and(causal, keys < len_ref[LENS + items + item])
        for pair in range(width // PAIR):
            yield (
                slice(item * steps, (item + 1) * steps),
                slice(pair * PAIR, (pair + 1) * PAIR),
                allowed,
            )


def self_forward_kernel(items, len_ref, q_ref, k_ref, v_ref, o_ref):
    tokens, width = q_ref.shape
    first_head = first_lanes(tokens // items)
    for rows, lanes, allowed in self_parts(len_ref, items, tokens, width):
        _, probs = self_weights(q_ref[rows, lanes], k_ref[rows, lanes], first_head, allowed)
        o_ref[rows, lanes] = to_low(unstacked(tn(to_low(probs), v_ref[rows, lanes]), first_head))


def self_backward_kernel(
    items, s_ref, q_ref, k_ref, v_ref, mine_ref, came_ref, out_ref,
    d_low_ref, dq_ref, dk_ref, dv_ref, sums_ref, do_both,
):
    tokens, width = q_ref.shape
    join_rows(s_ref[CORE_AT], mine_ref, came_ref, d_low_ref)
    do_both[...] = to_low(nt(d_low_ref[...], out_ref[...]))
    first_head = first_lanes(tokens // items)
    for rows, lanes, allowed in self_parts(s_ref, items, tokens, width):
        key = k_ref[rows, lanes]
        query, probs = self_weights(q_ref[rows, lanes], key, first_head, allowed)
        d_both = stacked(do_both[rows, lanes], first_head)
        d_probs = nt(v_ref[rows, lanes], d_both)
        dots = jnp.sum(probs * d_probs, axis=0, keepdims=True)
        d_scores = to_low(probs * (d_probs - dots))
        dv_ref[rows, lanes] = to_low(nn(to_low(probs), d_both))
        dk_ref[rows, lanes] = to_low(nn(d_scores, query))
        dq_ref[rows, lanes] = to_low(unstacked(tn(d_scores, key), first_head) * SCALE)
    sums_ref[...] = jnp.zeros_like(sums_ref)
    sums_ref[0:1, :] = col_sum(dq_ref[...].astype(f32))
    sums_ref[1:2, :] = col_sum(do_both[...].astype(f32))


def grad_half_kernel(count, s_ref, *refs):
    for at in range(0, refs[-1].shape[1], TILE):
        part = slice(at, at + TILE)
        total = tn(refs[0][...], refs[count][:, part])
        for i in range(1, count):
            total = total + tn(refs[i][...], refs[count + i][:, part])
        refs[-1][:, part] = to_low(total)


def grad_half(info, index, lefts, rights):
    rows, columns = lefts[0].shape[1] // 2, rights[0].shape[1]
    spec = lambda left: pl.BlockSpec((left.shape[0], rows), lambda i, s: (0, index(s)))
    return call(
        functools.partial(grad_half_kernel, len(lefts)),
        info,
        [(left, spec(left)) for left in lefts] + list(rights),
        [((rows, columns), bf16)],
        name="grad_half",
    )[0]


def self_grad_kernel(s_ref, x0_ref, x1_ref, d0_ref, d1_ref, q_ref, k_ref, v_ref, h_ref, *outs):
    width = q_ref.shape[1]
    for x_ref, d_ref, out in ((x0_ref, d0_ref, outs[0]), (x1_ref, d1_ref, outs[1])):
        for i, ref in enumerate((q_ref, k_ref, v_ref)):
            out[:, i * width : (i + 1) * width] = to_low(tn(x_ref[...], ref[...]))
        out[:, 3 * width :] = to_low(tn(d_ref[...], h_ref[...]))


def self_grad(info, first, second, x, d_low, query, key, value, heads):
    rows, tokens, width = x.shape[1] // 4, x.shape[0], query.shape[1]
    at = lambda index: pl.BlockSpec((tokens, rows), lambda i, s: (0, index(s)))
    return call(
        self_grad_kernel,
        info,
        [(x, at(first)), (x, at(second)), (d_low, at(first)), (d_low, at(second)), query, key, value, heads],
        [((rows, 4 * width), bf16)] * 2,
    )


def combine_kernel(s_ref, *refs):
    total = wide(refs[0])
    for ref in refs[1:-1]:
        total = total + wide(ref)
    refs[-1][...] = total.astype(refs[-1].dtype)


def combine(info, terms, rows, dtype=bf16):
    columns = terms[0][0].shape[1]
    tiles = 2 if rows >= 128 else 1
    at = lambda index: pl.BlockSpec((rows // tiles, columns), lambda i, s: (index(s) * tiles + i, 0))
    return call(
        combine_kernel,
        info,
        [(array, at(index)) for array, index in terms],
        [((rows, columns), dtype)],
        grid=(tiles,),
        out_specs=[pl.BlockSpec((rows // tiles, columns), lambda i, s: (i, 0))],
        name="combine",
    )[0]


def join_kernel(position, s_ref, mine_ref, came_ref, out_ref):
    @pl.when(pl.program_id(0) == s_ref[position])
    def _():
        out_ref[...] = mine_ref[...].astype(out_ref.dtype)

    @pl.when(pl.program_id(0) != s_ref[position])
    def _():
        out_ref[...] = came_ref[...].astype(out_ref.dtype)


def join(info, bit, mine, came, dtype=bf16):
    rows, columns = mine.shape
    return call(
        functools.partial(join_kernel, dp_position(bit)),
        info,
        [mine, came],
        [((2 * rows, columns), dtype)],
        grid=(2,),
        out_specs=[pl.BlockSpec((rows, columns), lambda i, s: (i, 0))],
        name="join",
    )[0]


class DpSum:
    def __init__(self, info, order, terms, step):
        self.info, self.order, self.step = info, list(order), step
        self.terms = [(term, lambda s: 0) for term in terms]
        self.rows = terms[0].shape[0]

    def wait(self, points):
        if points:
            array, index = self.terms[-1]
            self.terms[-1] = (after(array, *points), index)

    def send(self, *points):
        self.wait(points)
        bit = self.order[self.step]
        at = dp_position(bit)
        self.rows //= 2
        theirs = lambda index: lambda s: 2 * index(s) + 1 - s[at]
        mine = lambda index: lambda s: 2 * index(s) + s[at]
        sent = combine(self.info, [(term, theirs(index)) for term, index in self.terms], self.rows)
        self.terms = [(term, mine(index)) for term, index in self.terms]
        self.terms.append((swap(sent, "dp", bit), lambda s: 0))
        self.step += 1
        return sent

    def done(self):
        return self.step == len(self.order)

    def total(self, *points, dtype=bf16):
        self.wait(points)
        return combine(self.info, self.terms, self.rows, dtype)

    def start_gather(self, *points):
        self.values = self.total(*points)
        self.came = swap(self.values, "dp", self.order[-1])
        return self.values

    def gather(self, *points):
        bit = self.order.pop()
        came = after(self.came, *points) if points else self.came
        self.values = join(self.info, bit, self.values, came)
        self.came = swap(self.values, "dp", self.order[-1])
        return self.values

    def gathered(self):
        return len(self.order) == 1


def self_finish_kernel(first, second, s_ref, upper_ref, upper_came_ref, lower_ref, lower_came_ref, in_ref, out_ref):
    rows, width = upper_ref.shape[0], in_ref.shape[2]
    blocks = halves(s_ref[first], upper_ref[...], upper_came_ref[...])
    blocks = blocks + halves(s_ref[second], lower_ref[...], lower_came_ref[...])
    for at, block in enumerate(blocks):
        block = block.astype(f32)
        part = slice(at * rows, (at + 1) * rows)
        for i in range(3):
            in_ref[i, part, :] = block[:, i * width : (i + 1) * width]
        out_ref[:, part] = block[:, 3 * width :].T


def reversed_bits(index, count):
    return sum((index // (1 << i) % 2) << (count - 1 - i) for i in range(count))


def pick_rows_kernel(starts, s_ref, *refs):
    outs = len(starts)
    for k, (start, start_added) in enumerate(starts):
        rows = refs[-outs + k].shape[0]
        total = refs[0][dyn(start(s_ref), rows), :]
        if len(refs) - outs == 2:
            total = add_low(total, refs[1][dyn(start_added(s_ref), rows), :])
        refs[-outs + k][...] = total


def pick_rows(info, values, blocks, starts, rows, added=None):
    count = blocks.bit_length() - 1
    size, columns = values.shape[0] // blocks, values.shape[1]
    inputs = [(values, pl.BlockSpec((size, columns), lambda i, s: (i, 0)))]
    back = lambda height: pl.BlockSpec(
        (height, columns), lambda i, s: (reversed_bits(i, count), 0)
    )
    if added is not None:
        inputs.append((added, back(added.shape[0] // blocks)))
    return call(
        functools.partial(pick_rows_kernel, starts),
        info,
        inputs,
        [((rows * blocks, columns), bf16)] * len(starts),
        grid=(blocks,),
        out_specs=[back(rows)] * len(starts),
        name="pick_rows",
    )


def cross_rows_kernel(s_ref, q_ref, q_came_ref, o_ref, o_came_ref, kv_ref, kv_came_ref, out_ref):
    rows = q_ref.shape[0]
    left, right = halves(s_ref[CORE_AT], kv_ref[...], kv_came_ref[...])
    out_ref[:rows, :] = add_low(q_ref[...], q_came_ref[...])
    out_ref[rows : 2 * rows, :] = add_low(o_ref[...], o_came_ref[...])
    out_ref[2 * rows : 3 * rows, :] = left
    out_ref[3 * rows :, :] = right


def general_cross_rows(d_q, d_back, d_kv, shard):
    dp_size, mem_size = lax.axis_size("dp"), lax.axis_size("mem")
    width = d_q.shape[1]

    def split(values, axis, bit, dim):
        mine = bit_at(axis, bit)
        entry = lambda at: lax.dynamic_index_in_dim(values, at, dim, keepdims=False)
        return entry(mine), entry(1 - mine)

    mem_dims = (2,) * len(bits_of("mem"))
    own = []
    for grad in (d_q, d_back):
        grad = grad.reshape((dp_size,) + mem_dims + (shard, width))
        for bit in chip_bits()[::-1]:
            grad = split(grad, "mem", bit, 1)[0]
        keep, send = split(grad, "mem", CORE, 1)
        own.append(add_low(keep, core_swap(send)))
    grad = d_kv.reshape((dp_size,) + mem_dims + (shard, width))
    for bit in chip_bits()[::-1]:
        keep, send = split(grad, "mem", bit, 1)
        grad = add_low(keep, swap(send, "mem", bit))
    keep, send = split(grad, "mem", CORE, 1)
    own = jnp.stack(own + list(halves(bit_at("mem", CORE), keep, core_swap(send))), axis=1)
    own = own.reshape((2,) * len(bits_of("dp")) + own.shape[1:])
    for bit in bits_of("dp")[::-1]:
        keep, send = split(own, "dp", bit, 0)
        own = add_low(keep, swap(send, "dp", bit))
    return own.astype(f32)


def local(
    dec_input,
    memory,
    dec_len,
    mem_len,
    self_in,
    self_in_bias,
    self_out,
    cross_in,
    cross_bias,
    cross_out,
    fc_in,
    fc_in_bias,
    fc_out,
    out_biases,
    norm_gains,
    norm_shifts,
    grad_out,
):
    items, steps, width = dec_input.shape
    mem_rows = memory.shape[1]
    local_width, hidden_width = self_in.shape[2], fc_in.shape[1]
    tokens = items * steps
    half, share = width // 2, tokens // 2
    dp_size, mem_size = lax.axis_size("dp"), lax.axis_size("mem")
    dp_bits = bits_of("dp")
    place = lax.axis_index("mem").astype(jnp.int32)
    core = bit_at("mem", CORE)
    numbers = [place, core, place * 0] + [bit_at("dp", bit) for bit in dp_bits]
    info = jnp.stack(numbers + [place * 0] * (LENS - len(numbers)))
    info = jnp.concatenate([info, mem_len, dec_len])

    x_low = dec_input.reshape(tokens, width)
    mem_low = memory.reshape(items * mem_rows, width)
    own_rows = pl.BlockSpec((share, width), lambda i, s: (s[CORE_AT], 0))
    columns = lambda values, at, size: lax.dynamic_slice_in_dim(values, at, size, 1)

    kv_pieces = relative({0: cross_in[:, width:]}, chip_bits())
    mem_far = core_swap(mem_low)
    bias_pieces = relative({0: cross_bias.T}, chip_bits())

    weight_self = jnp.transpose(self_in, (1, 0, 2))
    bias_self = self_in_bias.astype(f32)
    query_self = to_low(nn(x_low, weight_self[0]) + bias_self[0])
    key_self = to_low(nn(x_low, weight_self[1]))
    value_self = to_low(nn(x_low, weight_self[2]) + bias_self[1])
    (heads_self,) = call(
        functools.partial(self_forward_kernel, items),
        info,
        [query_self, key_self, value_self],
        [((tokens, local_width), bf16)],
        name="self_forward",
    )
    part_of = lambda core: lax.dynamic_slice_in_dim(heads_self, core * share, share, 0)
    came = core_swap(to_low(nn(part_of(1 - core), self_out)))
    attended = to_low(nn(part_of(core), self_out) + came.astype(f32))
    attended, attended_came = chip_swap(attended)

    kv_pieces = {r: after(v, attended) if r else v for r, v in kv_pieces.items()}
    query_pieces = {0: after(cross_in[:, :width], *kv_pieces.values())}
    query_pieces = relative(query_pieces, chip_bits())
    low_weight = [((width, width), bf16)]
    (weight_kv,) = assemble(
        info,
        relative(kv_pieces, [CORE]),
        ((0, 0, half, 0, half), (0, width, half, half, half)),
        low_weight,
        "weight_kv",
    )
    kv_near, kv_far = nn(mem_low, weight_kv), nn(mem_far, weight_kv)
    query_pieces = {r: after(v, kv_near) if r else v for r, v in query_pieces.items()}
    (weight_query,) = assemble(
        info, relative(query_pieces, [CORE]), ((0, 0, 0, 0, width),), low_weight, "weight_query"
    )
    bias_pieces = {r: after(v, attended) if r else v for r, v in bias_pieces.items()}
    bias_pieces = relative(bias_pieces, [CORE])
    block = jnp.arange(width)[None, :] // local_width
    cross_shift = sum(
        jnp.where(block == (place ^ r), jnp.tile(v, (1, mem_size)).astype(f32), 0.0)
        for r, v in bias_pieces.items()
    )
    value_shift = lax.dynamic_slice_in_dim(cross_shift[1], core * half, half, 0)
    value_shift = jnp.concatenate([jnp.zeros((half,), f32), value_shift])
    vectors = jnp.concatenate(
        [
            norm_gains.astype(f32).T,
            norm_shifts.astype(f32).T,
            out_biases.astype(f32).T,
            cross_shift[:1],
            jnp.zeros((6, width), f32),
        ],
        axis=0,
    )
    kv_near, kv_far = to_low(kv_near + value_shift), to_low(kv_far + value_shift)
    fc_in_far, fc_out_far = core_swap(after(fc_in, attended)), core_swap(after(fc_out, attended))
    fc_bias = fc_in_bias[None].astype(f32)
    fc_bias_far = core_swap(fc_in_bias)[None].astype(f32)

    token_f32, token_low = ((share, width), f32), ((share, width), bf16)
    token_half, one_each = ((share, half), bf16), ((share, 1), f32)
    normed_one, inverse_one, first_low, query_keep, query_send = call(
        first_norm_kernel,
        info,
        [(x_low, own_rows), attended, after(attended_came, kv_near, kv_far), vectors, weight_query],
        [token_f32, one_each, token_low, token_half, token_half],
    )
    query_came = core_swap(query_send)
    back_pieces = relative({0: after(cross_out, attended_came)}, chip_bits())
    back_pieces = {r: after(v, first_low) if r else v for r, v in back_pieces.items()}
    query_came = after(query_came, *back_pieces.values())
    (cross_back,) = assemble(
        info,
        relative(back_pieces, [CORE]),
        ((0, 0, 0, 0, width),),
        low_weight,
        "cross_back",
    )

    out, stat = cross_forward(info, items, query_keep, query_came, kv_near, kv_far)
    for bit in chip_bits():
        out, stat = merge(info, bit, out, stat, swap(out, "mem", bit), swap(stat, "mem", bit))
    part_of_out = lambda core: lax.dynamic_slice_in_dim(out, core * share, share, 0)
    out_keep, out_came = part_of_out(core), core_swap(part_of_out(1 - core))

    units_low = ((share, hidden_width), bf16)
    weight = pltpu.VMEM((width, hidden_width), bf16)
    weight_out = pltpu.VMEM((hidden_width, width), bf16)
    cross_heads, normed_two, inverse_two, second_low, hidden, hidden_far, slope, slope_far, fed = call(
        middle_kernel,
        info,
        [normed_one, out_keep, out_came, vectors, fc_bias, fc_bias_far]
        + [(v, HBM) for v in (cross_back, fc_in, fc_in_far, fc_out, fc_out_far)],
        [token_low, token_f32, one_each, token_low] + [units_low] * 4 + [token_low],
        scratch=[
            pltpu.VMEM((width, width), bf16),
            weight,
            weight,
            weight_out,
            weight_out,
            pltpu.SemaphoreType.DMA((5,)),
        ],
        mega=44,
    )
    fed, fed_came = chip_swap(fed)
    second_other, hidden_other = core_swap(second_low), core_swap(hidden_far)
    final_low, d_three, d_three_low, d_pre, d_pre_far, d_fed, sums_three, pre_sums = call(
        turn_kernel,
        info,
        [normed_two, fed, fed_came, vectors, (grad_out.reshape(tokens, width), own_rows)]
        + [slope, slope_far]
        + [(v, HBM) for v in (fc_in, fc_in_far, fc_out, fc_out_far)],
        [token_low, token_f32, token_low, units_low, units_low, token_low]
        + [((8, width), f32), ((8, hidden_width), f32)],
        scratch=[weight, weight, weight_out, weight_out, pltpu.SemaphoreType.DMA((4,))],
        mega=44,
    )
    d_fed, d_fed_came = chip_swap(d_fed)

    order_one = dp_bits
    order_two = dp_bits[1:2] + dp_bits[:1] + dp_bits[2:]
    at_one, at_two = dp_position(order_one[0]), dp_position(order_two[0])
    d_three_other, d_pre_other = core_swap(d_three_low), core_swap(d_pre_far)
    fc_in_args = ([second_low, second_other], [d_pre, d_pre_other])
    fc_out_args = ([hidden, hidden_other], [d_three_low, d_three_other])
    fc_in_send = grad_half(info, lambda s: 1 - s[at_one], *fc_in_args)
    fc_in_came = swap(fc_in_send, "dp", order_one[0])
    fc_out_send = grad_half(info, lambda s: 1 - s[at_two], *fc_out_args)
    fc_out_came = swap(fc_out_send, "dp", order_two[0])
    fc_in_keep = grad_half(info, lambda s: s[at_one], *fc_in_args)
    fc_out_keep = grad_half(info, lambda s: s[at_two], *fc_out_args)
    fc_one = DpSum(info, order_one, [fc_in_keep, fc_in_came], 1)
    fc_two = DpSum(info, order_two, [fc_out_keep, fc_out_came], 1)

    d_fed_came = after(d_fed_came, fc_in_send, fc_out_send, fc_in_keep, fc_out_keep)
    d_two, d_two_low, d_keep, d_send, sums_two = call(
        second_back_kernel,
        info,
        [d_three, d_fed, d_fed_came, normed_two, inverse_two, vectors, cross_back],
        [token_f32, token_low, token_half, token_half, ((8, width), f32)],
    )
    d_came = core_swap(d_send)

    d_query_part, d_near, d_far = cross_backward(
        info, (query_keep, query_came), (d_keep, d_came), out, stat, kv_near, kv_far
    )
    d_query_part, d_query_came = chip_swap(d_query_part)
    last = (fc_one.send(d_query_part), fc_two.send(d_query_part))

    d_kv = to_low(tn(mem_low, after(d_near, *last)) + tn(mem_far, d_far))
    d_query_came = after(d_query_came, d_kv)
    d_query_keep, d_query_send = call(
        split_sum_kernel, info, [d_query_part, d_query_came], [token_half, token_half]
    )
    d_query_send_came = core_swap(d_query_send)
    last = (fc_one.send(d_query_send), fc_two.send(d_query_send))
    d_query_send_came = after(d_query_send_came, *last)
    d_one_low, d_query_cross, sums_one = call(
        first_back_kernel,
        info,
        [d_two, d_query_keep, d_query_send_came, normed_one, inverse_one]
        + [vectors, weight_query],
        [token_low, token_low, ((8, width), f32)],
    )
    d_one_came = core_swap(d_one_low)

    local_low = ((tokens, local_width), bf16)
    d_one_all, d_query, d_key, d_value, sums_self = call(
        functools.partial(self_backward_kernel, items),
        info,
        [query_self, key_self, value_self, d_one_low, d_one_came, self_out],
        [((tokens, width), bf16), local_low, local_low, local_low, ((8, local_width), f32)],
        scratch=[pltpu.VMEM((tokens, local_width), bf16)],
        name="self_backward",
    )

    self_args = (x_low, d_one_all, d_query, d_key, d_value, heads_self)
    self_one_send, self_two_send = self_grad(
        info, lambda s: 1 - s[at_one], lambda s: 3 - s[at_two], *self_args
    )
    self_one_came = swap(self_one_send, "dp", order_one[0])
    self_two_came = swap(self_two_send, "dp", order_two[0])
    last = (self_one_send, self_two_send)
    self_one_keep, self_two_keep = self_grad(
        info, lambda s: s[at_one], lambda s: 2 + s[at_two], after(x_low, *last), *self_args[1:]
    )
    self_one = DpSum(info, order_one, [self_one_keep, self_one_came], 1)
    self_two = DpSum(info, order_two, [self_two_keep, self_two_came], 1)
    last = (self_one_keep, self_two_keep)
    while not fc_one.done():
        last = (fc_one.send(*last), fc_two.send(*last))
    last = (fc_one.start_gather(*last), fc_two.start_gather(*last))

    shard = width // (dp_size * mem_size)
    d_q = to_low(tn(first_low, d_query_cross))
    d_back = to_low(tn(cross_heads, after(d_two_low, d_near)))
    simple = shard % 16 == 0 and mem_size == 4
    if simple:
        own = lambda s: s[PLACE] * shard
        other = lambda s: (s[PLACE] ^ CORE) * shard
        chip = lambda s: s[PLACE] // 2 * 2 * shard
        other_chip = lambda s: (1 - s[PLACE] // 2) * 2 * shard
        in_chip = lambda s: s[CORE_AT] * shard
        other_in_chip = lambda s: (1 - s[CORE_AT]) * shard
        (d_kv_send,) = pick_rows(
            info, after(d_kv, d_query_came), dp_size, [(other_chip, None)], 2 * shard
        )
        d_kv_came = swap(d_kv_send, "mem", chip_bits()[0])
        d_q_keep, d_q_send = pick_rows(info, d_q, dp_size, [(own, None), (other, None)], shard)
        d_back_keep, d_back_send = pick_rows(
            info, d_back, dp_size, [(own, None), (other, None)], shard
        )
        d_kv_keep, d_kv_send = pick_rows(
            info,
            d_kv,
            dp_size,
            [(own, in_chip), (other, other_in_chip)],
            shard,
            after(d_kv_came, *last),
        )
        rows = pl.BlockSpec((shard, width), lambda i, s: (i, 0))
        pieces = [d_q_keep, core_swap(d_q_send), d_back_keep, core_swap(d_back_send)]
        pieces = pieces + [d_kv_keep, core_swap(d_kv_send)]
        (cross_rows,) = call(
            cross_rows_kernel,
            info,
            [(piece, rows) for piece in pieces],
            [((4 * shard * dp_size, width), bf16)],
            grid=(dp_size,),
            out_specs=[pl.BlockSpec((4 * shard, width), lambda i, s: (i, 0))],
            name="cross_rows",
        )
        cross_sum = DpSum(info, dp_bits, [cross_rows], 0)
        last = (cross_sum.send(),)

    last = (self_one.send(*last), self_two.send(*last))

    partial = to_low(
        nt(after(d_query, *last), weight_self[0])
        + nt(d_key, weight_self[1])
        + nt(d_value, weight_self[2])
    )
    chips = range(mem_size // 2)
    by_core = lambda core: jnp.concatenate(
        [columns(partial, (2 * i + core) * local_width, local_width) for i in chips], axis=1
    )
    partial = add_low(by_core(core), core_swap(by_core(1 - core)))
    input_grad = columns(d_one_all, place * local_width, local_width).astype(f32)
    for i in chips:
        piece = columns(partial, (place // 2 ^ i) * local_width, local_width)
        input_grad = input_grad + (swap(piece, "mem", 2 * i) if i else piece).astype(f32)
    input_grad = to_low(input_grad).reshape(items, steps, local_width)

    padded = lambda v: jnp.pad(v, ((0, 0), (0, width - v.shape[1])))
    small = jnp.concatenate([sums_one, sums_two, sums_three, padded(pre_sums)], axis=0)
    small_came = core_swap(small)
    rows = small[:24] + small_came[:24]
    rows = jnp.concatenate(
        [rows[at : at + 1] for at in (0, 8, 16, 1, 9, 17, 2, 10, 18, 3, 11)]
        + [small[24:25] + small_came[25:26], padded(sums_self[:2]), rows[4:6]],
        axis=0,
    )
    rows_came = swap(rows, "dp", dp_bits[0])

    last = (input_grad,)
    while not self_one.done():
        last = (self_one.send(*last), self_two.send(*last))
    last = (fc_one.gather(*last), fc_two.gather(*last))
    if simple:
        last = (cross_sum.send(*last),)
    last = (self_one.start_gather(*last), self_two.start_gather(*last))
    for bit in dp_bits[1:]:
        rows = rows + after(rows_came, *last)
        rows_came = swap(rows, "dp", bit)
        last = (rows,)
    while not fc_one.gathered():
        last = (fc_one.gather(*last), fc_two.gather(*last))
    if simple:
        while not cross_sum.done():
            last = (cross_sum.send(*last),)
    while not self_one.gathered():
        last = (self_one.gather(*last), self_two.gather(*last))
    fc_in_grad, fc_out_grad = (
        join(info, fc.order[0], fc.values, after(fc.came, *last), f32) for fc in (fc_one, fc_two)
    )
    last = (fc_in_grad, fc_out_grad)
    quarter = pl.BlockSpec(self_one.values.shape, lambda i, s: (0, 0))
    self_in_grad, self_out_grad = call(
        functools.partial(self_finish_kernel, at_one, at_two),
        info,
        [self_one.values, after(self_one.came, *last), self_two.values, self_two.came],
        [((3, width, local_width), f32), ((local_width, width), f32)],
        name="self_finish",
    )
    self_in_grad = jnp.transpose(self_in_grad, (1, 0, 2))
    rows = rows + after(rows_came, *last)
    spot = (lax.axis_index("dp") * mem_size + place) * shard
    owned = columns(rows, spot, shard)
    gains_grad, shifts_grad, out_biases_grad = owned[0:3].T, owned[3:6].T, owned[6:9].T
    cross_bias_grad = owned[9:11].T
    fc_in_bias_grad = rows[11, :hidden_width]
    self_in_bias_grad = rows[12:14, :local_width]
    if simple:
        cross_rows = cross_sum.total(*last, dtype=f32)
        q_rows, back_rows, left, right = (
            cross_rows[at * shard : (at + 1) * shard] for at in range(4)
        )
    else:
        q_rows, back_rows, left, right = general_cross_rows(d_q, d_back, d_kv, shard)
    cross_in_grad = jnp.concatenate(
        [q_rows, left[:, :half], right[:, :half], left[:, half:], right[:, half:]], axis=1
    )
    cross_out_grad = back_rows

    came = core_swap(to_low(nt(after(d_far, *last), weight_kv)))
    memory_grad = to_low(nt(d_near, weight_kv) + came.astype(f32)).reshape(memory.shape)

    final_all = halves(core, final_low, core_swap(final_low))
    block_output = jnp.concatenate(final_all, axis=0).reshape(items, steps, width)

    return (
        block_output,
        input_grad,
        memory_grad,
        self_in_grad,
        self_in_bias_grad,
        self_out_grad,
        cross_in_grad,
        cross_bias_grad,
        cross_out_grad,
        fc_in_grad,
        fc_in_bias_grad,
        fc_out_grad,
        out_biases_grad,
        gains_grad,
        shifts_grad,
    )


def solution(mesh):
    placed = (
        P("dp", None, None),
        P("dp", "mem", None),
        P("dp"),
        P("dp"),
        P(None, None, "mem"),
        P(None, "mem"),
        P("mem", None),
        P("mem", None),
        P("mem", None),
        P("mem", None),
        P(None, "mem"),
        P("mem"),
        P("mem", None),
        P(),
        P(),
        P(),
        P("dp", None, None),
    )
    return jax.shard_map(
        local,
        mesh=mesh,
        in_specs=placed,
        out_specs=(
            P("dp", None, None),
            P("dp", None, "mem"),
            P("dp", "mem", None),
            P(None, None, "mem"),
            P(None, "mem"),
            P("mem", None),
            P(("dp", "mem"), None),
            P(("dp", "mem"), None),
            P(("dp", "mem"), None),
            P(None, "mem"),
            P("mem"),
            P("mem", None),
            P(("dp", "mem"), None),
            P(("dp", "mem"), None),
            P(("dp", "mem"), None),
        ),
        check_vma=False,
    )
```

```python
import functools

import jax
import jax.numpy as jnp
from jax import lax
from jax.experimental import pallas as pl
from jax.experimental.pallas import tpu as pltpu
from jax.sharding import PartitionSpec as P

HEAD_DIM = 64
PAIR = 2 * HEAD_DIM
CORE = 1
SCALE = HEAD_DIM ** (-0.5)
MASKED = -1e30
EPSILON = 1e-05
TILE = 256
MEGA = 1024 * 1024

f32 = jnp.float32
bf16 = jnp.bfloat16


def to_low(values):
    return values.astype(bf16)


def nt(left, right):
    return lax.dot_general(left, right, (((1,), (1,)), ((), ())), preferred_element_type=f32)


def nn(left, right):
    return lax.dot_general(left, right, (((1,), (0,)), ((), ())), preferred_element_type=f32)


def tn(left, right):
    return lax.dot_general(left, right, (((0,), (0,)), ((), ())), preferred_element_type=f32)


def col_sum(values):
    return jnp.sum(values, axis=0, keepdims=True)


def swap(values, axis, bit):
    pairs = [(i, i ^ bit) for i in range(lax.axis_size(axis))]
    return lax.ppermute(values, axis, pairs)


def core_swap(values):
    return swap(values, "mem", CORE)


def bits_of(axis):
    size, bits, bit = lax.axis_size(axis), [], 1
    while bit < size:
        bits.append(bit)
        bit *= 2
    return bits


def chip_bits():
    return bits_of("mem")[1:]


def bit_at(axis, bit):
    return (lax.axis_index(axis) // bit % 2).astype(jnp.int32)


def after(values, *others):
    return lax.optimization_barrier((values,) + others)[0]


def add_low(first, second):
    return to_low(first.astype(f32) + second.astype(f32))


def chip_swap(values):
    bits = chip_bits()
    for bit in bits[:-1]:
        values = add_low(values, swap(values, "mem", bit))
    return values, swap(values, "mem", bits[-1])


def relative(pieces, bits):
    for bit in bits:
        pieces = pieces | {r ^ bit: swap(piece, "mem", bit) for r, piece in pieces.items()}
    return pieces


def whole(shape):
    return pl.BlockSpec(shape, lambda *_: (0,) * len(shape))


HBM = pl.BlockSpec(memory_space=pl.ANY)


def call(
    kernel, info, inputs, outputs, scratch=(), grid=(1,), out_specs=None, mega=8, cost=0.0, name=None
):
    arrays = [given[0] if isinstance(given, tuple) else given for given in inputs]
    specs = [given[1] if isinstance(given, tuple) else whole(given.shape) for given in inputs]
    return pl.pallas_call(
        kernel,
        out_shape=[jax.ShapeDtypeStruct(*out) for out in outputs],
        grid_spec=pltpu.PrefetchScalarGridSpec(
            num_scalar_prefetch=1,
            grid=grid,
            in_specs=specs,
            out_specs=out_specs or [whole(out[0]) for out in outputs],
            scratch_shapes=list(scratch),
        ),
        compiler_params=pltpu.CompilerParams(vmem_limit_bytes=mega * MEGA),
        cost_estimate=pl.CostEstimate(
            flops=1 + int(cost * 1.1e9), bytes_accessed=1, transcendentals=0
        ),
        name=name or kernel.__name__,
    )(info, *arrays)


def dp_position(bit):
    return DP_AT + bit.bit_length() - 1


def norm_parts(resid):
    centre = resid - jnp.mean(resid, axis=-1, keepdims=True)
    inverse = lax.rsqrt(jnp.mean(centre * centre, axis=-1, keepdims=True) + EPSILON)
    return (centre * inverse, inverse)


def norm_back(normed, inverse, gain, upstream):
    scaled = upstream * gain
    return inverse * (
        scaled
        - jnp.mean(scaled, axis=-1, keepdims=True)
        - normed * jnp.mean(scaled * normed, axis=-1, keepdims=True)
    )


def row(ref, at):
    return ref[at : at + 1, :]


def wide(ref):
    return ref[...].astype(f32)


def halves(core, mine, theirs):
    first = core == 0
    return jnp.where(first, mine, theirs), jnp.where(first, theirs, mine)


def dyn(start, size, unit=16):
    return pl.ds(pl.multiple_of(start, unit), size)


PLACE, CORE_AT, DP_AT, LENS = 0, 1, 3, 8
GAIN, SHIFT, BIAS, QUERY_BIAS = 0, 3, 6, 9


def assemble_kernel(ids, parts, s_ref, *refs):
    sources, outs, sem = refs[: len(ids)], refs[len(ids) : -1], refs[-1]
    rows = sources[0].shape[0]
    copies = []
    for source, r in zip(sources, ids):
        at = dyn((s_ref[PLACE] ^ r) * rows, rows)
        for out, start, step, to, width in parts:
            columns = pl.ds(pl.multiple_of(start + s_ref[CORE_AT] * step, 128), width)
            copies.append(
                pltpu.make_async_copy(
                    source.at[:, columns],
                    outs[out].at[at, pl.ds(to, width)],
                    sem.at[len(copies)],
                )
            )
    for copy in copies:
        copy.start()
    for copy in copies:
        copy.wait()


def assemble(info, pieces, parts, outputs, name):
    return call(
        functools.partial(assemble_kernel, tuple(pieces), parts),
        info,
        [(piece, HBM) for piece in pieces.values()],
        outputs,
        scratch=[pltpu.SemaphoreType.DMA((len(pieces) * len(parts),))],
        out_specs=[HBM] * len(outputs),
        name=name,
    )


def first_norm_kernel(
    s_ref, x_ref, mine_ref, came_ref, vec_ref, wq_ref, normed_ref, inv_ref, low_ref, keep_ref, send_ref
):
    resid = wide(x_ref) + (wide(mine_ref) + wide(came_ref)) + row(vec_ref, BIAS)
    normed, inverse = norm_parts(resid)
    normed_ref[...] = normed
    inv_ref[...] = inverse
    low = to_low(normed * row(vec_ref, GAIN) + row(vec_ref, SHIFT))
    low_ref[...] = low
    half = keep_ref.shape[1]
    left, right = (
        to_low(nn(low, wq_ref[:, part]) + vec_ref[QUERY_BIAS : QUERY_BIAS + 1, part])
        for part in (slice(0, half), slice(half, 2 * half))
    )
    keep_ref[...], send_ref[...] = halves(s_ref[CORE_AT], left, right)


def middle_kernel(
    s_ref,
    normed_ref,
    mine_ref,
    came_ref,
    vec_ref,
    bias_ref,
    bias_far_ref,
    back_hbm,
    in_hbm,
    in_far_hbm,
    out_hbm,
    out_far_hbm,
    heads_ref,
    normed_two_ref,
    inv_ref,
    low_ref,
    hidden_ref,
    hidden_far_ref,
    slope_ref,
    slope_far_ref,
    fed_ref,
    back,
    w_in,
    w_in_far,
    w_out,
    w_out_far,
    sem,
):
    loads = []
    for i, (source, target) in enumerate(
        (
            (back_hbm, back),
            (in_hbm, w_in),
            (in_far_hbm, w_in_far),
            (out_hbm, w_out),
            (out_far_hbm, w_out_far),
        )
    ):
        loads.append(pltpu.make_async_copy(source, target, sem.at[i]))
        loads[i].start()
    heads = jnp.concatenate(halves(s_ref[CORE_AT], mine_ref[...], came_ref[...]), axis=1)
    heads_ref[...] = heads
    first = normed_ref[...] * row(vec_ref, GAIN) + row(vec_ref, SHIFT)
    loads[0].wait()
    normed, inverse = norm_parts(first + nn(heads, back[...]) + row(vec_ref, BIAS + 1))
    normed_two_ref[...] = normed
    inv_ref[...] = inverse
    low = to_low(normed * row(vec_ref, GAIN + 1) + row(vec_ref, SHIFT + 1))
    low_ref[...] = low
    for i, (weight, shift, hidden, slope) in enumerate(
        ((w_in, bias_ref, hidden_ref, slope_ref), (w_in_far, bias_far_ref, hidden_far_ref, slope_far_ref))
    ):
        loads[1 + i].wait()
        for at in range(0, weight.shape[1], TILE):
            part = slice(at, at + TILE)
            pre = nn(low, weight[:, part]) + shift[:, part]
            share = 0.5 * (1.0 + lax.erf(pre * (0.5**0.5)))
            hidden[:, part] = to_low(pre * share)
            density = jnp.exp(-0.5 * pre * pre) * (1.0 / (2.0 * jnp.pi) ** 0.5)
            slope[:, part] = to_low(share + pre * density)
    loads[3].wait()
    loads[4].wait()
    for at in range(0, fed_ref.shape[1], TILE):
        part = slice(at, at + TILE)
        fed_ref[:, part] = to_low(
            nn(hidden_ref[...], w_out[:, part]) + nn(hidden_far_ref[...], w_out_far[:, part])
        )


def turn_kernel(
    s_ref,
    normed_two_ref,
    mine_ref,
    came_ref,
    vec_ref,
    grad_ref,
    slope_ref,
    slope_far_ref,
    in_hbm,
    in_far_hbm,
    out_hbm,
    out_far_hbm,
    final_ref,
    d_ref,
    d_low_ref,
    pre_ref,
    pre_far_ref,
    part_ref,
    sums_ref,
    pre_sums_ref,
    w_in,
    w_in_far,
    w_out,
    w_out_far,
    sem,
):
    loads = []
    for i, (source, target) in enumerate(
        ((out_hbm, w_out), (out_far_hbm, w_out_far), (in_hbm, w_in), (in_far_hbm, w_in_far))
    ):
        loads.append(pltpu.make_async_copy(source, target, sem.at[i]))
        loads[i].start()
    second = normed_two_ref[...] * row(vec_ref, GAIN + 1) + row(vec_ref, SHIFT + 1)
    resid = second + (wide(mine_ref) + wide(came_ref)) + row(vec_ref, BIAS + 2)
    normed, inverse = norm_parts(resid)
    gain = row(vec_ref, GAIN + 2)
    final_ref[...] = to_low(normed * gain + row(vec_ref, SHIFT + 2))
    upstream = wide(grad_ref)
    d_resid = norm_back(normed, inverse, gain, upstream)
    d_ref[...] = d_resid
    d_low = to_low(d_resid)
    d_low_ref[...] = d_low
    sums_ref[...] = jnp.zeros_like(sums_ref)
    sums_ref[0:1, :] = col_sum(upstream * normed)
    sums_ref[1:2, :] = col_sum(upstream)
    sums_ref[2:3, :] = col_sum(d_resid)
    pre_sums_ref[...] = jnp.zeros_like(pre_sums_ref)
    for i, (weight, slope, pre) in enumerate(
        ((w_out, slope_ref, pre_ref), (w_out_far, slope_far_ref, pre_far_ref))
    ):
        loads[i].wait()
        for at in range(0, weight.shape[0], TILE):
            part = slice(at, at + TILE)
            d_pre = to_low(nt(d_low, weight[part, :]) * slope[:, part].astype(f32))
            pre[:, part] = d_pre
            pre_sums_ref[i : i + 1, part] = col_sum(d_pre.astype(f32))
    loads[2].wait()
    loads[3].wait()
    for at in range(0, part_ref.shape[1], TILE):
        part = slice(at, at + TILE)
        part_ref[:, part] = to_low(
            nt(pre_ref[...], w_in[part, :]) + nt(pre_far_ref[...], w_in_far[part, :])
        )


def second_back_kernel(
    s_ref,
    d_three_ref,
    mine_ref,
    came_ref,
    normed_ref,
    inv_ref,
    vec_ref,
    back_ref,
    d_ref,
    d_low_ref,
    keep_ref,
    send_ref,
    sums_ref,
):
    upstream = d_three_ref[...] + (wide(mine_ref) + wide(came_ref))
    normed = normed_ref[...]
    d_resid = norm_back(normed, inv_ref[...], row(vec_ref, GAIN + 1), upstream)
    d_ref[...] = d_resid
    d_low = to_low(d_resid)
    d_low_ref[...] = d_low
    half = keep_ref.shape[1]
    left = to_low(nt(d_low, back_ref[:half, :]))
    right = to_low(nt(d_low, back_ref[half:, :]))
    keep_ref[...], send_ref[...] = halves(s_ref[CORE_AT], left, right)
    sums_ref[...] = jnp.zeros_like(sums_ref)
    sums_ref[0:1, :] = col_sum(upstream * normed)
    sums_ref[1:2, :] = col_sum(upstream)
    sums_ref[2:3, :] = col_sum(d_resid)
    sums_ref[3:4, :half] = col_sum(left.astype(f32))
    sums_ref[3:4, half:] = col_sum(right.astype(f32))


def split_sum_kernel(s_ref, mine_ref, came_ref, keep_ref, send_ref):
    rows = keep_ref.shape[0]
    for out, core in ((send_ref, 1 - s_ref[CORE_AT]), (keep_ref, s_ref[CORE_AT])):
        part = dyn(core * rows, rows)
        out[...] = add_low(mine_ref[part, :], came_ref[part, :])


def first_back_kernel(
    s_ref,
    d_two_ref,
    mine_ref,
    came_ref,
    normed_ref,
    inv_ref,
    vec_ref,
    wq_ref,
    left_ref,
    right_ref,
    query_ref,
    sums_ref,
):
    d_query = jnp.concatenate(halves(s_ref[CORE_AT], mine_ref[...], came_ref[...]), axis=1)
    query_ref[...] = d_query
    upstream = d_two_ref[...] + nt(d_query, wq_ref[...])
    normed = normed_ref[...]
    d_resid = norm_back(normed, inv_ref[...], row(vec_ref, GAIN), upstream)
    half = left_ref.shape[1]
    left_ref[...] = to_low(d_resid[:, :half])
    right_ref[...] = to_low(d_resid[:, half:])
    sums_ref[...] = jnp.zeros_like(sums_ref)
    sums_ref[0:1, :] = col_sum(upstream * normed)
    sums_ref[1:2, :] = col_sum(upstream)
    sums_ref[2:3, :] = col_sum(d_resid)
    sums_ref[3:4, :] = col_sum(d_query.astype(f32))


def stacked(block, first_head):
    zero = jnp.zeros_like(block)
    return jnp.concatenate(
        [jnp.where(first_head, block, zero), jnp.where(first_head, zero, block)], axis=0
    )


def unstacked(both, first_head):
    rows = both.shape[0] // 2
    return jnp.where(first_head, both[:rows], both[rows:])


def first_lanes(rows):
    return lax.broadcasted_iota(jnp.int32, (rows, PAIR), 1) < HEAD_DIM


def row_sums(values):
    lanes = lax.broadcasted_iota(jnp.int32, (16, PAIR), 1)
    which = lax.broadcasted_iota(jnp.int32, (16, PAIR), 0)
    pick = to_low((lanes // HEAD_DIM == which).astype(f32))
    high = to_low(values)
    low = to_low(values - high.astype(f32))
    sums = nt(pick, high) + nt(pick, low)
    return jnp.concatenate([sums[0:1], sums[1:2]], axis=1)


def shown(length, place, rows):
    spot = lax.broadcasted_iota(jnp.int32, (rows, 1), 0)
    return jnp.concatenate(
        [place * rows + spot < length, (place ^ CORE) * rows + spot < length], axis=0
    )


def join_rows(core, mine_ref, came_ref, both):
    rows = mine_ref.shape[0]
    both[dyn(core * rows, rows), :] = mine_ref[...]
    both[dyn((1 - core) * rows, rows), :] = came_ref[...]


def cross_forward_kernel(s_ref, mine_ref, came_ref, near_ref, far_ref, o_ref, stat_ref, both):
    item = pl.program_id(0)

    @pl.when(item == 0)
    def _():
        join_rows(s_ref[CORE_AT], mine_ref, came_ref, both)

    steps, width = o_ref.shape
    rows = dyn(item * steps, steps)
    visible = shown(s_ref[LENS + item], s_ref[PLACE], near_ref.shape[0])
    first_head = first_lanes(steps)
    for pair in range(width // PAIR):
        lanes = slice(pair * PAIR, (pair + 1) * PAIR)
        values = slice(width + pair * PAIR, width + (pair + 1) * PAIR)
        query = stacked(both[rows, lanes] * SCALE, first_head)
        key = jnp.concatenate([near_ref[:, lanes], far_ref[:, lanes]], axis=0)
        value = jnp.concatenate([near_ref[:, values], far_ref[:, values]], axis=0)
        scores = jnp.where(visible, nt(key, query), MASKED)
        top = jnp.max(scores, axis=0, keepdims=True)
        grown = jnp.exp(scores - top)
        total = jnp.sum(grown, axis=0, keepdims=True)
        weights = to_low(grown * (1.0 / total))
        o_ref[:, lanes] = to_low(unstacked(tn(weights, value), first_head))
        stat = top + jnp.log(total)
        stat_ref[0, 2 * pair : 2 * pair + 1, :] = stat[:, :steps]
        stat_ref[0, 2 * pair + 1 : 2 * pair + 2, :] = stat[:, steps:]


def cross_forward(info, items, mine, came, near, far):
    width, tokens = mine.shape[1], 2 * mine.shape[0]
    rows, steps = near.shape[0] // items, tokens // items
    heads = width // HEAD_DIM
    keys = pl.BlockSpec((rows, 2 * width), lambda i, *_: (i, 0))
    return call(
        cross_forward_kernel,
        info,
        [mine, came, (near, keys), (far, keys)],
        [((tokens, width), bf16), ((items, heads, steps), f32)],
        scratch=[pltpu.VMEM((tokens, width), bf16)],
        grid=(items,),
        mega=16,
        out_specs=[
            pl.BlockSpec((steps, width), lambda i, *_: (i, 0)),
            pl.BlockSpec((1, heads, steps), lambda i, *_: (i, 0, 0)),
        ],
    )


def merge_kernel(bit, s_ref, a_ref, sa_ref, b_ref, sb_ref, o_ref, stat_ref):
    flip = (s_ref[PLACE] & bit) != 0
    items, heads, steps = sa_ref.shape
    width = a_ref.shape[1]
    pick = lax.broadcasted_iota(jnp.int32, (heads, width), 1) // HEAD_DIM
    pick = to_low((pick == lax.broadcasted_iota(jnp.int32, (heads, width), 0)).astype(f32))

    def spread(share):
        high = to_low(share)
        return tn(high, pick) + tn(to_low(share - high.astype(f32)), pick)

    for item in range(items):
        rows = slice(item * steps, (item + 1) * steps)
        mine, theirs = sa_ref[item], sb_ref[item]
        first, second = jnp.where(flip, theirs, mine), jnp.where(flip, mine, theirs)
        top = jnp.maximum(first, second)
        grown_first, grown_second = jnp.exp(first - top), jnp.exp(second - top)
        total = grown_first + grown_second
        stat_ref[item] = top + jnp.log(total)
        low_values = jnp.where(flip, b_ref[rows, :], a_ref[rows, :]).astype(f32)
        high_values = jnp.where(flip, a_ref[rows, :], b_ref[rows, :]).astype(f32)
        o_ref[rows, :] = to_low(
            spread(grown_first / total) * low_values + spread(grown_second / total) * high_values
        )


def merge(info, bit, mine, stat_mine, theirs, stat_theirs):
    return call(
        functools.partial(merge_kernel, bit),
        info,
        [mine, stat_mine, theirs, stat_theirs],
        [(mine.shape, bf16), (stat_mine.shape, f32)],
        name="merge",
    )


def cross_backward_kernel(
    s_ref, q_ref, q_came_ref, do_mine_ref, do_came_ref, o_ref, stat_ref, near_ref, far_ref,
    dq_ref, dnear_ref, dfar_ref, q_both, do_both,
):
    item = pl.program_id(0)

    @pl.when(item == 0)
    def _():
        join_rows(s_ref[CORE_AT], q_ref, q_came_ref, q_both)
        join_rows(s_ref[CORE_AT], do_mine_ref, do_came_ref, do_both)

    steps, width = dq_ref.shape
    rows = near_ref.shape[0]
    tokens = dyn(item * steps, steps)
    visible = shown(s_ref[LENS + item], s_ref[PLACE], rows)
    first_head = first_lanes(steps)
    for pair in range(width // PAIR):
        lanes = slice(pair * PAIR, (pair + 1) * PAIR)
        values = slice(width + pair * PAIR, width + (pair + 1) * PAIR)
        d_out = do_both[tokens, lanes]
        dots = row_sums(d_out.astype(f32) * o_ref[:, lanes].astype(f32))
        stat = jnp.concatenate(
            [stat_ref[0, 2 * pair : 2 * pair + 1, :], stat_ref[0, 2 * pair + 1 : 2 * pair + 2, :]],
            axis=1,
        )
        query = stacked(q_both[tokens, lanes] * SCALE, first_head)
        d_both = stacked(d_out, first_head)
        key = jnp.concatenate([near_ref[:, lanes], far_ref[:, lanes]], axis=0)
        value = jnp.concatenate([near_ref[:, values], far_ref[:, values]], axis=0)
        scores = jnp.where(visible, nt(key, query), MASKED)
        probs = jnp.exp(scores - stat)
        d_scores = to_low(probs * (nt(value, d_both) - dots))
        d_value = to_low(nn(to_low(probs), d_both))
        d_key = to_low(nn(d_scores, query))
        dnear_ref[:, lanes] = d_key[:rows]
        dfar_ref[:, lanes] = d_key[rows:]
        dnear_ref[:, values] = d_value[:rows]
        dfar_ref[:, values] = d_value[rows:]
        dq_ref[:, lanes] = to_low(unstacked(tn(d_scores, key), first_head) * SCALE)


def cross_backward(info, queries, d_outs, out, stat, near, far):
    items, heads, steps = stat.shape
    tokens, width = out.shape
    rows = near.shape[0] // items
    keys = pl.BlockSpec((rows, 2 * width), lambda i, *_: (i, 0))
    block = pl.BlockSpec((steps, width), lambda i, *_: (i, 0))
    return call(
        cross_backward_kernel,
        info,
        list(queries)
        + list(d_outs)
        + [
            (out, block),
            (stat, pl.BlockSpec((1, heads, steps), lambda i, *_: (i, 0, 0))),
            (near, keys),
            (far, keys),
        ],
        [(out.shape, bf16), (near.shape, bf16), (far.shape, bf16)],
        scratch=[pltpu.VMEM((tokens, width), bf16)] * 2,
        grid=(items,),
        mega=16,
        out_specs=[block, keys, keys],
    )


def self_weights(query_block, key_block, first_head, allowed):
    query = stacked(query_block * SCALE, first_head)
    scores = jnp.where(allowed, nt(key_block, query), MASKED)
    top = jnp.max(scores, axis=0, keepdims=True)
    grown = jnp.exp(scores - top)
    total = jnp.sum(grown, axis=0, keepdims=True)
    return query, grown * (1.0 / total)


def self_parts(len_ref, items, tokens, width):
    steps = tokens // items
    keys = lax.broadcasted_iota(jnp.int32, (steps, 2 * steps), 0)
    queries = lax.broadcasted_iota(jnp.int32, (steps, 2 * steps), 1) % steps
    causal = keys <= queries
    for item in range(items):
        allowed = jnp.logical_and(causal, keys < len_ref[LENS + items + item])
        for pair in range(width // PAIR):
            yield (
                slice(item * steps, (item + 1) * steps),
                slice(pair * PAIR, (pair + 1) * PAIR),
                allowed,
            )


def self_forward_kernel(items, len_ref, q_ref, k_ref, v_ref, o_ref):
    tokens, width = q_ref.shape
    first_head = first_lanes(tokens // items)
    for rows, lanes, allowed in self_parts(len_ref, items, tokens, width):
        _, probs = self_weights(q_ref[rows, lanes], k_ref[rows, lanes], first_head, allowed)
        o_ref[rows, lanes] = to_low(unstacked(tn(to_low(probs), v_ref[rows, lanes]), first_head))


def self_backward_kernel(
    items, s_ref, q_ref, k_ref, v_ref, left_ref, right_ref, left_came, right_came, out_ref,
    d_low_ref, dq_ref, dk_ref, dv_ref, sums_ref, do_both,
):
    tokens, width = q_ref.shape
    half = left_ref.shape[1]
    for at, mine, came in ((0, left_ref, left_came), (half, right_ref, right_came)):
        part = slice(at, at + half)
        rows = mine.shape[0]
        d_low_ref[dyn(s_ref[CORE_AT] * rows, rows), part] = mine[...]
        d_low_ref[dyn((1 - s_ref[CORE_AT]) * rows, rows), part] = came[...]
    do_both[...] = to_low(nt(d_low_ref[...], out_ref[...]))
    first_head = first_lanes(tokens // items)
    for rows, lanes, allowed in self_parts(s_ref, items, tokens, width):
        key = k_ref[rows, lanes]
        query, probs = self_weights(q_ref[rows, lanes], key, first_head, allowed)
        d_both = stacked(do_both[rows, lanes], first_head)
        d_probs = nt(v_ref[rows, lanes], d_both)
        dots = jnp.sum(probs * d_probs, axis=0, keepdims=True)
        d_scores = to_low(probs * (d_probs - dots))
        dv_ref[rows, lanes] = to_low(nn(to_low(probs), d_both))
        dk_ref[rows, lanes] = to_low(nn(d_scores, query))
        dq_ref[rows, lanes] = to_low(unstacked(tn(d_scores, key), first_head) * SCALE)
    sums_ref[...] = jnp.zeros_like(sums_ref)
    sums_ref[0:1, :] = col_sum(dq_ref[...].astype(f32))
    sums_ref[1:2, :] = col_sum(do_both[...].astype(f32))


def grad_half_kernel(count, s_ref, *refs):
    for at in range(0, refs[-1].shape[1], TILE):
        part = slice(at, at + TILE)
        total = tn(refs[0][...], refs[count][:, part])
        for i in range(1, count):
            total = total + tn(refs[i][...], refs[count + i][:, part])
        refs[-1][:, part] = to_low(total)


def grad_half(info, index, lefts, rights):
    rows, columns = lefts[0].shape[1] // 2, rights[0].shape[1]
    spec = lambda left: pl.BlockSpec((left.shape[0], rows), lambda i, s: (0, index(s)))
    return call(
        functools.partial(grad_half_kernel, len(lefts)),
        info,
        [(left, spec(left)) for left in lefts] + list(rights),
        [((rows, columns), bf16)],
        cost=5.0,
        name="grad_half",
    )[0]


def self_grad_kernel(s_ref, x0_ref, x1_ref, d0_ref, d1_ref, q_ref, k_ref, v_ref, h_ref, *outs):
    width = q_ref.shape[1]
    for x_ref, d_ref, out in ((x0_ref, d0_ref, outs[0]), (x1_ref, d1_ref, outs[1])):
        for i, ref in enumerate((q_ref, k_ref, v_ref)):
            out[:, i * width : (i + 1) * width] = to_low(tn(x_ref[...], ref[...]))
        out[:, 3 * width :] = to_low(tn(d_ref[...], h_ref[...]))


def self_grad(info, first, second, x, d_low, query, key, value, heads):
    rows, tokens, width = x.shape[1] // 4, x.shape[0], query.shape[1]
    at = lambda index: pl.BlockSpec((tokens, rows), lambda i, s: (0, index(s)))
    return call(
        self_grad_kernel,
        info,
        [(x, at(first)), (x, at(second)), (d_low, at(first)), (d_low, at(second)), query, key, value, heads],
        [((rows, 4 * width), bf16)] * 2,
    )


def put_wide(out, at, values):
    rows = values.shape[0]
    high = to_low(values)
    out[at : at + rows, :] = high
    out[at + rows : at + 2 * rows, :] = to_low(values - high.astype(f32))


def get_wide(ref, at, rows):
    return ref[at : at + rows, :].astype(f32) + ref[at + rows : at + 2 * rows, :].astype(f32)


def split_kernel(positions, joint, s_ref, *refs):
    count = len(positions)
    mine, came, outs = refs[:count], refs[count : 2 * count], refs[2 * count :]
    sends, keeps = outs[:-count], outs[-count:]
    rows = keeps[0].shape[0]
    for k, position in enumerate(positions):
        base = 2 * rows * k if joint[0] else 0
        for send in (True, False):
            half = 1 - s_ref[position] if send else s_ref[position]
            total = add_low(
                mine[k][dyn(half * rows, rows), :], came[k][dyn(base + half * rows, rows), :]
            )
            if not send:
                keeps[k][...] = total
            elif joint[1]:
                sends[0][k * rows : (k + 1) * rows, :] = total
            else:
                sends[k][...] = total


def split(info, bits, mine, came, joint):
    rows, columns = mine[0].shape[0] // 2, mine[0].shape[1]
    sends = [2 * rows] if joint[1] else [rows] * len(bits)
    return call(
        functools.partial(split_kernel, [dp_position(bit) for bit in bits], joint),
        info,
        list(mine) + list(came),
        [((size, columns), bf16) for size in sends + [rows] * len(bits)],
        name="split_sums",
    )


def total_kernel(joint, extra, s_ref, *refs):
    mine, came, outs = refs[:2], refs[2:4], refs[4 + extra :]
    rows = mine[0].shape[0]
    for k in range(2):
        base = rows * k if joint[0] else 0
        total = add_low(mine[k][...], came[k][base : base + rows, :])
        if joint[1]:
            outs[0][k * rows : (k + 1) * rows, :] = total
        else:
            outs[k][...] = total
    if extra:
        put_wide(outs[0], 2 * rows, refs[4][...])


def total_pair(info, mine, came, joint, extra=None):
    rows, columns = mine[0].shape
    extras = [] if extra is None else [extra]
    more = 2 * sum(v.shape[0] for v in extras)
    outputs = [2 * rows + more] if joint[1] else [rows, rows]
    return call(
        functools.partial(total_kernel, joint, len(extras)),
        info,
        list(mine) + list(came) + extras,
        [((size, columns), bf16) for size in outputs],
        name="total_sums",
    )


def join_pair_kernel(positions, given, extra, s_ref, *refs):
    mine, came, outs = refs[:given], refs[given : 2 * given], refs[2 * given :]
    rows = mine[-1].shape[0] if given == 2 else (mine[0].shape[0] - 2 * extra) // 2
    for k, position in enumerate(positions):
        part = slice(0, rows) if given == 2 else slice(k * rows, (k + 1) * rows)
        own, other = mine[k % given][part, :], came[k % given][part, :]
        base = 2 * rows * k if len(outs) == 1 else 0
        out = outs[k % len(outs)]
        out[dyn(base + s_ref[position] * rows, rows), :] = own
        out[dyn(base + (1 - s_ref[position]) * rows, rows), :] = other
    if extra:
        at = mine[0].shape[0] - 2 * extra
        total = get_wide(mine[0], at, extra) + get_wide(came[0], at, extra)
        put_wide(outs[0], outs[0].shape[0] - 2 * extra, total)


def join_pair(info, bits, mine, came, joint, extra=0):
    given, columns = len(mine), mine[0].shape[1]
    rows = 2 * mine[1].shape[0] if given == 2 else mine[0].shape[0] - 2 * extra
    more = 2 * extra
    outputs = [(2 * rows + more, columns)] if joint else [(rows + more, columns), (rows, columns)]
    return call(
        functools.partial(
            join_pair_kernel, [dp_position(bit) for bit in bits], given, extra
        ),
        info,
        list(mine) + list(came),
        [(shape, bf16) for shape in outputs],
        cost=4.0,
        name="join_pair",
    )


def join_kernel(position, s_ref, mine_ref, came_ref, out_ref):
    @pl.when(pl.program_id(1) == s_ref[position])
    def _():
        out_ref[...] = mine_ref[...].astype(out_ref.dtype)

    @pl.when(pl.program_id(1) != s_ref[position])
    def _():
        out_ref[...] = came_ref[...].astype(out_ref.dtype)


def join(info, bit, mine, came, rows):
    columns = mine.shape[1]
    spec = pl.BlockSpec((rows, columns), lambda i, j, s: (0, 0))
    return call(
        functools.partial(join_kernel, dp_position(bit)),
        info,
        [(mine, spec), (came, spec)],
        [((2 * rows, columns), f32)],
        grid=(1, 2),
        out_specs=[pl.BlockSpec((rows, columns), lambda i, j, s: (j, 0))],
        name="join",
    )[0]


class PairSum:
    def __init__(self, info, orders, keeps, cames):
        self.info, self.step = info, 1
        self.bits = list(zip(*orders))
        self.back = self.bits[::-1]
        self.mine, self.came, self.extra = tuple(keeps), tuple(cames), None
        self.joint, self.gathering = False, False

    def pending(self):
        return self.came

    def arrived(self, came):
        self.came = came

    def exchange(self, values, bits):
        if len(values) == 1:
            self.came = (swap(values[0], "dp", bits[0]),)
        else:
            self.came = tuple(swap(value, "dp", bit) for value, bit in zip(values, bits))

    def advance(self):
        same = lambda bits: bits[0] == bits[1]
        came = self.came if len(self.came) == 2 else self.came * 2
        if self.step < len(self.bits):
            bits = self.bits[self.step]
            joint = (self.joint, same(bits))
            result = split(self.info, bits, self.mine, came, joint)
            sent, self.mine, self.joint = tuple(result[:-2]), tuple(result[-2:]), joint[1]
            self.step += 1
            self.exchange(sent, bits)
            return sent
        if not self.gathering:
            joint = (self.joint, same(self.back[0]))
            self.values = total_pair(self.info, self.mine, came, joint, self.extra)
            self.gathering = True
        else:
            bits = self.back.pop(0)
            extra = 0 if self.extra is None else self.extra.shape[0]
            joint = same(self.back[0])
            self.values = join_pair(self.info, bits, self.values, self.came, joint, extra)
        self.exchange(self.values, self.back[0])
        return tuple(self.values)

    def gathered(self):
        return self.gathering and len(self.back) == 1

    def whole(self, *points):
        self.came = tuple(after(came, *points) for came in self.came)
        rows = self.values[1].shape[0]
        parts = zip(self.back[0], self.values, self.came)
        return [join(self.info, bit, mine, came, rows) for bit, mine, came in parts]

    def extra_sum(self):
        extra = self.extra.shape[0]
        at = self.values[0].shape[0] - 2 * extra
        total = self.values[0][at:].astype(f32) + self.came[0][at:].astype(f32)
        return total[:extra] + total[extra:]


class BlockSum:
    def __init__(self, info, keep, came):
        self.info, self.order = info, bits_of("dp")[1:]
        self.mine, self.came = keep, (came,)

    def pending(self):
        return self.came

    def arrived(self, came):
        self.came = came

    def summed(self):
        return not self.order

    def advance(self):
        bit = self.order.pop(0)
        sent, self.mine = split(self.info, [bit], [self.mine], self.came, (False, False))
        self.came = (swap(sent, "dp", bit),)
        return (sent,)

    def total(self):
        return self.mine.astype(f32) + self.came[0].astype(f32)


def take_turns(flows, *points):
    if not flows:
        return ()
    came = lax.optimization_barrier((tuple(flow.pending() for flow in flows), points))[0]
    for flow, values in zip(flows, came):
        flow.arrived(values)
    return sum((flow.advance() for flow in flows), ())


def self_finish_kernel(first, second, s_ref, upper_ref, upper_came_ref, lower_ref, lower_came_ref, in_ref, out_ref):
    rows, width = upper_ref.shape[0], in_ref.shape[2]
    blocks = halves(s_ref[first], upper_ref[...], upper_came_ref[...])
    blocks = blocks + halves(s_ref[second], lower_ref[...], lower_came_ref[...])
    for at, block in enumerate(blocks):
        block = block.astype(f32)
        part = slice(at * rows, (at + 1) * rows)
        for i in range(3):
            in_ref[i, part, :] = block[:, i * width : (i + 1) * width]
        out_ref[:, part] = block[:, 3 * width :].T


def reversed_bits(index, count):
    return sum((index // (1 << i) % 2) << (count - 1 - i) for i in range(count))


def cross_grad_kernel(blocks, s_ref, *refs):
    scratch = refs[10]
    count = blocks.bit_length() - 1
    for k in range(2):
        left, right = refs[2 * k], refs[2 * k + 1]
        keep, first, second = refs[4 + 3 * k : 7 + 3 * k]
        rows, half = keep.shape[0] // blocks, first.shape[1]
        for at in range(0, right.shape[1], TILE):
            part = slice(at, at + TILE)
            scratch[...] = to_low(tn(left[...], right[:, part]))
            size = scratch.shape[0] // blocks
            send, column = (first, at) if at < half else (second, at - half)
            sent = slice(column, column + TILE)
            for block in range(blocks):
                turned = reversed_bits(block, count)
                to = slice(turned * rows, (turned + 1) * rows)
                own = dyn(block * size + s_ref[PLACE] * rows, rows)
                other = dyn(block * size + (s_ref[PLACE] ^ CORE) * rows, rows)
                keep[to, part] = scratch[own, :]
                send[to, sent] = scratch[other, :]


def cross_grad(info, blocks, shard, pairs):
    width = pairs[0][0].shape[1]
    rows = blocks * shard
    outputs = [((rows, width), bf16), ((rows, width // 2), bf16), ((rows, width // 2), bf16)]
    return call(
        functools.partial(cross_grad_kernel, blocks),
        info,
        [array for pair in pairs for array in pair],
        outputs * 2,
        scratch=[pltpu.VMEM((width, TILE), bf16)],
        name="cross_grad",
    )


def input_part_kernel(s_ref, q_ref, k_ref, v_ref, weight_ref, keep_ref, send_ref):
    width = q_ref.shape[1]
    for out, core in ((send_ref, 1 - s_ref[CORE_AT]), (keep_ref, s_ref[CORE_AT])):
        for i in range(out.shape[1] // width):
            rows = dyn((2 * i + core) * width, width)
            total = nt(q_ref[...], weight_ref[0, rows, :])
            total = total + nt(k_ref[...], weight_ref[1, rows, :])
            total = total + nt(v_ref[...], weight_ref[2, rows, :])
            out[:, i * width : (i + 1) * width] = to_low(total)


def input_sum_kernel(s_ref, mine_ref, came_ref, d_ref, keep_ref, send_ref):
    width = keep_ref.shape[1]
    chip = s_ref[PLACE] // 2
    other = dyn((1 - chip) * width, width, 128)
    send_ref[...] = add_low(mine_ref[:, other], came_ref[:, other])
    own = dyn(chip * width, width, 128)
    keep_ref[...] = (
        mine_ref[:, own].astype(f32)
        + came_ref[:, own].astype(f32)
        + d_ref[:, dyn(s_ref[PLACE] * width, width, 128)].astype(f32)
    )


def memory_kernel(s_ref, d_ref, weight_ref, *refs):
    total = nt(d_ref[...], weight_ref[...])
    if len(refs) == 2:
        total = total + wide(refs[0])
    refs[-1][...] = to_low(total)


def memory_part(info, items, d_ref, weight, *came):
    rows = pl.BlockSpec((d_ref.shape[0] // items, d_ref.shape[1]), lambda i, s: (i, 0))
    return call(
        memory_kernel,
        info,
        [(d_ref, rows), weight] + [(array, rows) for array in came],
        [(d_ref.shape, bf16)],
        grid=(items,),
        out_specs=[rows],
        mega=12,
        name="memory_grad",
    )[0]


def stack_kernel(s_ref, one_ref, two_ref, three_ref, pre_ref, out_ref):
    out_ref[...] = jnp.zeros_like(out_ref)
    out_ref[0:8, :], out_ref[8:16, :], out_ref[16:24, :] = one_ref[...], two_ref[...], three_ref[...]
    out_ref[24:32, : pre_ref.shape[1]] = pre_ref[...]


SMALL = (0, 8, 16, 1, 9, 17, 2, 10, 18, 3, 11)


def small_kernel(s_ref, mine_ref, came_ref, self_ref, out_ref):
    out_ref[...] = jnp.zeros_like(out_ref)
    for to, at in enumerate(SMALL):
        out_ref[to : to + 1, :] = mine_ref[at : at + 1, :] + came_ref[at : at + 1, :]
    to = len(SMALL)
    out_ref[to : to + 1, :] = mine_ref[24:25, :] + came_ref[25:26, :]
    out_ref[to + 1 : to + 3, : self_ref.shape[1]] = self_ref[0:2, :]


def other_chip_kernel(blocks, s_ref, values, out):
    size, rows, count = values.shape[0] // blocks, out.shape[0] // blocks, blocks.bit_length() - 1
    for block in range(blocks):
        to = reversed_bits(block, count) * rows
        start = block * size + (1 - s_ref[PLACE] // 2) * rows
        out[to : to + rows, :] = values[dyn(start, rows), :]


def chip_rows_kernel(blocks, s_ref, values, came, keep, first, second):
    size, rows, count = values.shape[0] // blocks, keep.shape[0] // blocks, blocks.bit_length() - 1
    half = first.shape[1]
    for block in range(blocks):
        turned = reversed_bits(block, count)
        to = slice(turned * rows, (turned + 1) * rows)
        own = values[dyn(block * size + s_ref[PLACE] * rows, rows), :]
        keep[to, :] = add_low(own, came[dyn((2 * turned + s_ref[CORE_AT]) * rows, rows), :])
        other = values[dyn(block * size + (s_ref[PLACE] ^ CORE) * rows, rows), :]
        other = add_low(other, came[dyn((2 * turned + 1 - s_ref[CORE_AT]) * rows, rows), :])
        first[to, :] = other[:, :half]
        second[to, :] = other[:, half:]


def cross_rows_kernel(blocks, s_ref, *refs):
    send, keep = refs[9:]
    rows = refs[0].shape[0] // blocks
    for block in range(blocks):
        part = slice(block * rows, (block + 1) * rows)
        came = [
            jnp.concatenate([refs[3 * k + 1][part, :], refs[3 * k + 2][part, :]], axis=1)
            for k in range(3)
        ]
        values = [add_low(refs[0][part, :], came[0]), add_low(refs[3][part, :], came[1])]
        values.extend(halves(s_ref[CORE_AT], refs[6][part, :], came[2]))
        base = 4 * rows * (block % (blocks // 2))
        mine = s_ref[DP_AT] == block // (blocks // 2)
        for out, chosen in ((keep, mine), (send, jnp.logical_not(mine))):

            @pl.when(chosen)
            def _():
                for i, value in enumerate(values):
                    out[base + i * rows : base + (i + 1) * rows, :] = value


def general_cross_rows(d_q, d_back, d_kv, shard):
    dp_size, mem_size = lax.axis_size("dp"), lax.axis_size("mem")
    width = d_q.shape[1]

    def split(values, axis, bit, dim):
        mine = bit_at(axis, bit)
        entry = lambda at: lax.dynamic_index_in_dim(values, at, dim, keepdims=False)
        return entry(mine), entry(1 - mine)

    mem_dims = (2,) * len(bits_of("mem"))
    own = []
    for grad in (d_q, d_back):
        grad = grad.reshape((dp_size,) + mem_dims + (shard, width))
        for bit in chip_bits()[::-1]:
            grad = split(grad, "mem", bit, 1)[0]
        keep, send = split(grad, "mem", CORE, 1)
        own.append(add_low(keep, core_swap(send)))
    grad = d_kv.reshape((dp_size,) + mem_dims + (shard, width))
    for bit in chip_bits()[::-1]:
        keep, send = split(grad, "mem", bit, 1)
        grad = add_low(keep, swap(send, "mem", bit))
    keep, send = split(grad, "mem", CORE, 1)
    own = jnp.stack(own + list(halves(bit_at("mem", CORE), keep, core_swap(send))), axis=1)
    own = own.reshape((2,) * len(bits_of("dp")) + own.shape[1:])
    for bit in bits_of("dp")[::-1]:
        keep, send = split(own, "dp", bit, 0)
        own = add_low(keep, swap(send, "dp", bit))
    return own.astype(f32)


def local(
    dec_input,
    memory,
    dec_len,
    mem_len,
    self_in,
    self_in_bias,
    self_out,
    cross_in,
    cross_bias,
    cross_out,
    fc_in,
    fc_in_bias,
    fc_out,
    out_biases,
    norm_gains,
    norm_shifts,
    grad_out,
):
    items, steps, width = dec_input.shape
    mem_rows = memory.shape[1]
    local_width, hidden_width = self_in.shape[2], fc_in.shape[1]
    tokens = items * steps
    half, share = width // 2, tokens // 2
    dp_size, mem_size = lax.axis_size("dp"), lax.axis_size("mem")
    dp_bits = bits_of("dp")
    place = lax.axis_index("mem").astype(jnp.int32)
    core = bit_at("mem", CORE)
    numbers = [place, core, place * 0] + [bit_at("dp", bit) for bit in dp_bits]
    info = jnp.stack(numbers + [place * 0] * (LENS - len(numbers)))
    info = jnp.concatenate([info, mem_len, dec_len])

    x_low = dec_input.reshape(tokens, width)
    mem_low = memory.reshape(items * mem_rows, width)
    own_rows = pl.BlockSpec((share, width), lambda i, s: (s[CORE_AT], 0))
    columns = lambda values, at, size: lax.dynamic_slice_in_dim(values, at, size, 1)

    cross_pieces = relative({0: cross_in}, chip_bits())
    mem_far = core_swap(mem_low)
    bias_pieces = relative({0: cross_bias.T}, chip_bits())

    weight_self = jnp.transpose(self_in, (1, 0, 2))
    bias_self = self_in_bias.astype(f32)
    query_self = to_low(nn(x_low, weight_self[0]) + bias_self[0])
    key_self = to_low(nn(x_low, weight_self[1]))
    value_self = to_low(nn(x_low, weight_self[2]) + bias_self[1])
    (heads_self,) = call(
        functools.partial(self_forward_kernel, items),
        info,
        [query_self, key_self, value_self],
        [((tokens, local_width), bf16)],
        name="self_forward",
    )
    part_of = lambda core: lax.dynamic_slice_in_dim(heads_self, core * share, share, 0)
    came = core_swap(to_low(nn(part_of(1 - core), self_out)))
    attended = to_low(nn(part_of(core), self_out) + came.astype(f32))
    attended, attended_came = chip_swap(attended)

    points = (attended,) + tuple(bias_pieces.values())
    cross_pieces = {r: after(v, *points) if r else v for r, v in cross_pieces.items()}
    low_weight = [((width, width), bf16)]
    weight_kv, weight_query = assemble(
        info,
        relative(cross_pieces, [CORE]),
        ((0, width, half, 0, half), (0, 2 * width, half, half, half), (1, 0, 0, 0, width)),
        low_weight * 2,
        "cross_weights",
    )
    bias_pieces = relative(bias_pieces, [CORE])
    block = jnp.arange(width)[None, :] // local_width
    cross_shift = sum(
        jnp.where(block == (place ^ r), jnp.tile(v, (1, mem_size)).astype(f32), 0.0)
        for r, v in bias_pieces.items()
    )
    value_shift = lax.dynamic_slice_in_dim(cross_shift[1], core * half, half, 0)
    value_shift = jnp.concatenate([jnp.zeros((half,), f32), value_shift])
    vectors = jnp.concatenate(
        [
            norm_gains.astype(f32).T,
            norm_shifts.astype(f32).T,
            out_biases.astype(f32).T,
            cross_shift[:1],
            jnp.zeros((6, width), f32),
        ],
        axis=0,
    )
    kv_near = to_low(nn(mem_low, weight_kv) + value_shift)
    kv_far = to_low(nn(mem_far, weight_kv) + value_shift)
    fc_in_far, fc_out_far = core_swap(after(fc_in, attended)), core_swap(after(fc_out, attended))
    fc_bias = fc_in_bias[None].astype(f32)
    fc_bias_far = core_swap(fc_in_bias)[None].astype(f32)

    token_f32, token_low = ((share, width), f32), ((share, width), bf16)
    token_half, one_each = ((share, half), bf16), ((share, 1), f32)
    normed_one, inverse_one, first_low, query_keep, query_send = call(
        first_norm_kernel,
        info,
        [(x_low, own_rows), attended, after(attended_came, kv_near, kv_far), vectors, weight_query],
        [token_f32, one_each, token_low, token_half, token_half],
    )
    back_pieces = relative({0: after(cross_out, kv_near)}, chip_bits())
    back_pieces = {r: after(v, first_low) if r else v for r, v in back_pieces.items()}
    query_came = core_swap(query_send)
    (cross_back,) = assemble(
        info,
        relative(back_pieces, [CORE]),
        ((0, 0, 0, 0, width),),
        low_weight,
        "cross_back",
    )

    out, stat = cross_forward(info, items, query_keep, query_came, kv_near, kv_far)
    out = after(out, *back_pieces.values())
    for bit in chip_bits():
        out, stat = merge(info, bit, out, stat, swap(out, "mem", bit), swap(stat, "mem", bit))
    part_of_out = lambda core: lax.dynamic_slice_in_dim(out, core * share, share, 0)
    out_keep, out_came = part_of_out(core), core_swap(part_of_out(1 - core))

    units_low = ((share, hidden_width), bf16)
    weight = pltpu.VMEM((width, hidden_width), bf16)
    weight_out = pltpu.VMEM((hidden_width, width), bf16)
    cross_heads, normed_two, inverse_two, second_low, hidden, hidden_far, slope, slope_far, fed = call(
        middle_kernel,
        info,
        [normed_one, out_keep, out_came, vectors, fc_bias, fc_bias_far]
        + [(v, HBM) for v in (cross_back, fc_in, fc_in_far, fc_out, fc_out_far)],
        [token_low, token_f32, one_each, token_low] + [units_low] * 4 + [token_low],
        scratch=[
            pltpu.VMEM((width, width), bf16),
            weight,
            weight,
            weight_out,
            weight_out,
            pltpu.SemaphoreType.DMA((5,)),
        ],
        mega=32,
    )
    fed, fed_came = chip_swap(fed)
    second_other, hidden_other = core_swap(second_low), core_swap(hidden_far)
    final_low, d_three, d_three_low, d_pre, d_pre_far, d_fed, sums_three, pre_sums = call(
        turn_kernel,
        info,
        [normed_two, fed, fed_came, vectors, (grad_out.reshape(tokens, width), own_rows)]
        + [slope, slope_far]
        + [(v, HBM) for v in (fc_in, fc_in_far, fc_out, fc_out_far)],
        [token_low, token_f32, token_low, units_low, units_low, token_low]
        + [((8, width), f32), ((8, hidden_width), f32)],
        scratch=[weight, weight, weight_out, weight_out, pltpu.SemaphoreType.DMA((4,))],
        mega=32,
    )
    d_fed, d_fed_came = chip_swap(d_fed)

    order_one = dp_bits
    order_two = dp_bits[1:2] + dp_bits[:1] + dp_bits[2:]
    at_one, at_two = dp_position(order_one[0]), dp_position(order_two[0])
    d_three_other, d_pre_other = core_swap(d_three_low), core_swap(d_pre_far)
    fc_in_args = ([second_low, second_other], [d_pre, d_pre_other])
    fc_out_args = ([hidden, hidden_other], [d_three_low, d_three_other])
    upright = hidden_width == width
    if not upright:
        fc_in_args = fc_in_args[::-1]
    fc_in_send = grad_half(info, lambda s: 1 - s[at_one], *fc_in_args)
    fc_in_came = swap(fc_in_send, "dp", order_one[0])
    fc_out_send = grad_half(info, lambda s: 1 - s[at_two], *fc_out_args)
    fc_out_came = swap(fc_out_send, "dp", order_two[0])
    fc_in_keep = grad_half(info, lambda s: s[at_one], *fc_in_args)
    fc_out_keep = grad_half(info, lambda s: s[at_two], *fc_out_args)
    orders = (order_one, order_two)
    fc_sum = PairSum(
        info, orders, (fc_in_keep, fc_out_keep), (fc_in_came, fc_out_came)
    )

    d_fed_came = after(d_fed_came, fc_in_send, fc_out_send, fc_in_keep, fc_out_keep)
    d_two, d_two_low, d_keep, d_send, sums_two = call(
        second_back_kernel,
        info,
        [d_three, d_fed, d_fed_came, normed_two, inverse_two, vectors, cross_back],
        [token_f32, token_low, token_half, token_half, ((8, width), f32)],
    )
    d_came = core_swap(d_send)

    d_query_part, d_near, d_far = cross_backward(
        info, (query_keep, query_came), (d_keep, d_came), out, stat, kv_near, kv_far
    )
    d_query_part, d_query_came = chip_swap(d_query_part)
    flows_fc = [fc_sum]
    last = take_turns(flows_fc, d_query_part)

    d_kv = to_low(tn(mem_low, after(d_near, *last)) + tn(mem_far, d_far))
    shard = width // (dp_size * mem_size)
    simple = shard % 16 == 0 and mem_size == 4
    d_query_came = after(d_query_came, *take_turns(flows_fc, d_kv))
    if simple:
        (d_kv_send,) = call(
            functools.partial(other_chip_kernel, dp_size),
            info,
            [d_kv],
            [((width // 2, width), bf16)],
            name="other_chip",
        )
        d_kv_came = swap(d_kv_send, "mem", chip_bits()[0])
        d_query_came = after(d_query_came, d_kv_send)
    d_query_keep, d_query_send = call(
        split_sum_kernel, info, [d_query_part, d_query_came], [token_half, token_half]
    )
    d_query_send_came = core_swap(d_query_send)
    d_one_left, d_one_right, d_query_cross, sums_one = call(
        first_back_kernel,
        info,
        [d_two, d_query_keep, d_query_send_came, normed_one, inverse_one]
        + [vectors, weight_query],
        [token_half, token_half, token_low, ((8, width), f32)],
    )

    local_low = ((tokens, local_width), bf16)
    d_one_all, d_query, d_key, d_value, sums_self = call(
        functools.partial(self_backward_kernel, items),
        info,
        [query_self, key_self, value_self, d_one_left, d_one_right]
        + [core_swap(d_one_left), core_swap(d_one_right), self_out],
        [((tokens, width), bf16), local_low, local_low, local_low, ((8, local_width), f32)],
        scratch=[pltpu.VMEM((tokens, local_width), bf16)],
        name="self_backward",
    )

    self_args = (x_low, d_one_all, d_query, d_key, d_value, heads_self)
    self_one_send, self_two_send = self_grad(
        info, lambda s: 1 - s[at_one], lambda s: 3 - s[at_two], *self_args
    )
    self_one_came = swap(self_one_send, "dp", order_one[0])
    self_two_came = swap(self_two_send, "dp", order_two[0])
    last = (self_one_send, self_two_send)

    (small,) = call(
        stack_kernel,
        info,
        [sums_one, sums_two, after(sums_three, *last), pre_sums],
        [((32, width), f32)],
    )
    small_came = core_swap(small)
    self_one_keep, self_two_keep = self_grad(
        info, lambda s: s[at_one], lambda s: 2 + s[at_two], after(x_low, *last), *self_args[1:]
    )
    self_sum = PairSum(
        info, orders, (self_one_keep, self_two_keep), (self_one_came, self_two_came)
    )
    flows_self = [self_sum]
    last = (self_one_keep, self_two_keep)
    (fc_sum.extra,) = call(
        small_kernel, info, [small, after(small_came, *last), sums_self], [((16, width), f32)]
    )
    flows_self = [self_sum]

    chips = mem_size // 2
    shares = ((tokens, chips * local_width), bf16)
    partial, partial_send = call(
        input_part_kernel,
        info,
        [after(d_query, *last), d_key, d_value, weight_self],
        [shares, shares],
    )
    partial_came = core_swap(partial_send)

    if simple:
        q_keep, q_first, q_second, back_keep, back_first, back_second = cross_grad(
            info,
            dp_size,
            shard,
            [(after(first_low, *last), d_query_cross), (cross_heads, d_two_low)],
        )
        cross_parts = [q_keep, core_swap(q_first), core_swap(q_second)]
        cross_parts += [back_keep, core_swap(back_first), core_swap(back_second)]
        last = (q_keep,)
    last = take_turns(flows_fc, *last, partial)
    last = last + take_turns(flows_self, *last)
    if simple:
        rows = dp_size * shard
        d_kv_keep, d_kv_first, d_kv_second = call(
            functools.partial(chip_rows_kernel, dp_size),
            info,
            [d_kv, after(d_kv_came, *last)],
            [((rows, width), bf16), ((rows, half), bf16), ((rows, half), bf16)],
            name="chip_rows",
        )
        cross_parts += [d_kv_keep, core_swap(d_kv_first), core_swap(d_kv_second)]
        cross_send, cross_keep = call(
            functools.partial(cross_rows_kernel, dp_size),
            info,
            cross_parts,
            [((2 * rows, width), bf16)] * 2,
            name="cross_rows",
        )
        cross_sum = BlockSum(info, cross_keep, swap(cross_send, "dp", dp_bits[0]))
        last = last + (cross_send,)
    if chips == 2:
        input_grad, partial_send = call(
            input_sum_kernel,
            info,
            [partial, after(partial_came, *last), d_one_all],
            [((tokens, local_width), f32), local_low],
        )
        input_came = [swap(partial_send, "mem", chip_bits()[0])]
    else:
        partial = add_low(partial, partial_came)
        piece = lambda i: columns(partial, (place // 2 ^ i) * local_width, local_width)
        input_grad = columns(d_one_all, place * local_width, local_width).astype(f32)
        input_grad = input_grad + piece(0).astype(f32)
        input_came = [swap(piece(i), "mem", 2 * i) for i in range(1, chips)]
    flows_side = [cross_sum] if simple else []
    d_mem_far = memory_part(info, items, after(d_far, *last), weight_kv)
    last = take_turns(flows_self + flows_fc, *last, d_mem_far)
    last = last + take_turns(flows_side, *last)
    memory_grad = d_mem_came = None
    while not all(flow.gathered() for flow in flows_self + flows_fc):
        last = take_turns([flow for flow in flows_self + flows_fc if not flow.gathered()], *last)
        if d_mem_came is None:
            d_mem_came = core_swap(after(d_mem_far, *last))
        elif memory_grad is None:
            memory_grad = memory_part(info, items, after(d_near, *last), weight_kv, d_mem_came)
            last = last + (memory_grad,)
        last = last + take_turns([flow for flow in flows_side if not flow.summed()], *last)
    fc_in_grad, fc_out_grad = fc_sum.whole(*last)
    input_came = [after(came, *last) for came in input_came]
    for came in input_came:
        input_grad = input_grad + came.astype(f32)
    input_grad = to_low(input_grad).reshape(items, steps, local_width)
    final_came = core_swap(after(final_low, *last))
    block_output = jnp.concatenate(halves(core, final_low, final_came), axis=0)
    block_output = block_output.reshape(items, steps, width)
    if not upright:
        fc_in_grad = fc_in_grad.T
    last = (fc_in_grad, fc_out_grad)
    self_in_grad, self_out_grad = call(
        functools.partial(self_finish_kernel, at_one, at_two),
        info,
        [self_sum.values[0], after(self_sum.came[0], *last)]
        + [self_sum.values[1], self_sum.came[1]],
        [((3, width, local_width), f32), ((local_width, width), f32)],
        name="self_finish",
    )
    self_in_grad = jnp.transpose(self_in_grad, (1, 0, 2))
    rows = fc_sum.extra_sum()
    spot = (lax.axis_index("dp") * mem_size + place) * shard
    owned = columns(rows, spot, shard)
    gains_grad, shifts_grad, out_biases_grad = owned[0:3].T, owned[3:6].T, owned[6:9].T
    cross_bias_grad = owned[9:11].T
    fc_in_bias_grad = rows[11, :hidden_width]
    self_in_bias_grad = rows[12:14, :local_width]
    if simple:
        cross_sum.arrived((after(cross_sum.pending()[0], *last),))
        cross_rows = cross_sum.total()
        q_rows, back_rows, left, right = (
            cross_rows[at * shard : (at + 1) * shard] for at in range(4)
        )
    else:
        d_q = to_low(tn(first_low, d_query_cross))
        d_back = to_low(tn(cross_heads, d_two_low))
        q_rows, back_rows, left, right = general_cross_rows(d_q, d_back, d_kv, shard)
    cross_in_grad = jnp.concatenate(
        [q_rows, left[:, :half], right[:, :half], left[:, half:], right[:, half:]], axis=1
    )
    cross_out_grad = back_rows

    return (
        block_output,
        input_grad,
        memory_grad.reshape(memory.shape),
        self_in_grad,
        self_in_bias_grad,
        self_out_grad,
        cross_in_grad,
        cross_bias_grad,
        cross_out_grad,
        fc_in_grad,
        fc_in_bias_grad,
        fc_out_grad,
        out_biases_grad,
        gains_grad,
        shifts_grad,
    )


def solution(mesh):
    placed = (
        P("dp", None, None),
        P("dp", "mem", None),
        P("dp"),
        P("dp"),
        P(None, None, "mem"),
        P(None, "mem"),
        P("mem", None),
        P("mem", None),
        P("mem", None),
        P("mem", None),
        P(None, "mem"),
        P("mem"),
        P("mem", None),
        P(),
        P(),
        P(),
        P("dp", None, None),
    )
    return jax.shard_map(
        local,
        mesh=mesh,
        in_specs=placed,
        out_specs=(
            P("dp", None, None),
            P("dp", None, "mem"),
            P("dp", "mem", None),
            P(None, None, "mem"),
            P(None, "mem"),
            P("mem", None),
            P(("dp", "mem"), None),
            P(("dp", "mem"), None),
            P(("dp", "mem"), None),
            P(None, "mem"),
            P("mem"),
            P("mem", None),
            P(("dp", "mem"), None),
            P(("dp", "mem"), None),
            P(("dp", "mem"), None),
        ),
        check_vma=False,
    )
```

```python
import functools

import jax
import jax.numpy as jnp
from jax import lax
from jax.experimental import pallas as pl
from jax.experimental.pallas import tpu as pltpu
from jax.sharding import PartitionSpec as P

HEAD_DIM = 64
PAIR = 2 * HEAD_DIM
CORE = 1
SCALE = HEAD_DIM ** (-0.5)
MASKED = -1e30
EPSILON = 1e-05
TILE = 256
MEGA = 1024 * 1024

f32 = jnp.float32
bf16 = jnp.bfloat16


def to_low(values):
    return values.astype(bf16)


def nt(left, right):
    return lax.dot_general(left, right, (((1,), (1,)), ((), ())), preferred_element_type=f32)


def nn(left, right):
    return lax.dot_general(left, right, (((1,), (0,)), ((), ())), preferred_element_type=f32)


def tn(left, right):
    return lax.dot_general(left, right, (((0,), (0,)), ((), ())), preferred_element_type=f32)


def col_sum(values):
    return jnp.sum(values, axis=0, keepdims=True)


def swap(values, axis, bit):
    pairs = [(i, i ^ bit) for i in range(lax.axis_size(axis))]
    return lax.ppermute(values, axis, pairs)


def core_swap(values):
    return swap(values, "mem", CORE)


def bits_of(axis):
    size, bits, bit = lax.axis_size(axis), [], 1
    while bit < size:
        bits.append(bit)
        bit *= 2
    return bits


def chip_bits():
    return bits_of("mem")[1:]


def bit_at(axis, bit):
    return (lax.axis_index(axis) // bit % 2).astype(jnp.int32)


def after(values, *others):
    return lax.optimization_barrier((values,) + others)[0]


def add_low(first, second):
    return to_low(first.astype(f32) + second.astype(f32))


def chip_swap(values):
    bits = chip_bits()
    for bit in bits[:-1]:
        values = add_low(values, swap(values, "mem", bit))
    return values, swap(values, "mem", bits[-1])


def relative(pieces, bits):
    for bit in bits:
        pieces = pieces | {r ^ bit: swap(piece, "mem", bit) for r, piece in pieces.items()}
    return pieces


def whole(shape):
    return pl.BlockSpec(shape, lambda *_: (0,) * len(shape))


HBM = pl.BlockSpec(memory_space=pl.ANY)


def call(
    kernel, info, inputs, outputs, scratch=(), grid=(1,), out_specs=None, mega=8, cost=0.0, name=None
):
    arrays = [given[0] if isinstance(given, tuple) else given for given in inputs]
    specs = [given[1] if isinstance(given, tuple) else whole(given.shape) for given in inputs]
    return pl.pallas_call(
        kernel,
        out_shape=[jax.ShapeDtypeStruct(*out) for out in outputs],
        grid_spec=pltpu.PrefetchScalarGridSpec(
            num_scalar_prefetch=1,
            grid=grid,
            in_specs=specs,
            out_specs=out_specs or [whole(out[0]) for out in outputs],
            scratch_shapes=list(scratch),
        ),
        compiler_params=pltpu.CompilerParams(vmem_limit_bytes=mega * MEGA),
        cost_estimate=pl.CostEstimate(
            flops=1 + int(cost * 1.1e9), bytes_accessed=1, transcendentals=0
        ),
        name=name or kernel.__name__,
    )(info, *arrays)


def dp_position(bit):
    return DP_AT + bit.bit_length() - 1


def norm_parts(resid):
    centre = resid - jnp.mean(resid, axis=-1, keepdims=True)
    inverse = lax.rsqrt(jnp.mean(centre * centre, axis=-1, keepdims=True) + EPSILON)
    return (centre * inverse, inverse)


def norm_back(normed, inverse, gain, upstream):
    scaled = upstream * gain
    return inverse * (
        scaled
        - jnp.mean(scaled, axis=-1, keepdims=True)
        - normed * jnp.mean(scaled * normed, axis=-1, keepdims=True)
    )


def row(ref, at):
    return ref[at : at + 1, :]


def wide(ref):
    return ref[...].astype(f32)


def halves(core, mine, theirs):
    first = core == 0
    return jnp.where(first, mine, theirs), jnp.where(first, theirs, mine)


def dyn(start, size, unit=16):
    return pl.ds(pl.multiple_of(start, unit), size)


PLACE, CORE_AT, DP_AT, LENS = 0, 1, 3, 8
GAIN, SHIFT, BIAS, QUERY_BIAS = 0, 3, 6, 9


def assemble_kernel(ids, parts, s_ref, *refs):
    sources, outs, sem = refs[: len(ids)], refs[len(ids) : -1], refs[-1]
    rows = sources[0].shape[0]
    copies = []
    for source, r in zip(sources, ids):
        at = dyn((s_ref[PLACE] ^ r) * rows, rows)
        for out, start, step, to, width in parts:
            columns = pl.ds(pl.multiple_of(start + s_ref[CORE_AT] * step, 128), width)
            copies.append(
                pltpu.make_async_copy(
                    source.at[:, columns],
                    outs[out].at[at, pl.ds(to, width)],
                    sem.at[len(copies)],
                )
            )
    for copy in copies:
        copy.start()
    for copy in copies:
        copy.wait()


def assemble(info, pieces, parts, outputs, name):
    return call(
        functools.partial(assemble_kernel, tuple(pieces), parts),
        info,
        [(piece, HBM) for piece in pieces.values()],
        outputs,
        scratch=[pltpu.SemaphoreType.DMA((len(pieces) * len(parts),))],
        out_specs=[HBM] * len(outputs),
        name=name,
    )


def first_norm_kernel(
    s_ref, x_ref, mine_ref, came_ref, vec_ref, wq_ref, normed_ref, inv_ref, low_ref, keep_ref, send_ref
):
    resid = wide(x_ref) + (wide(mine_ref) + wide(came_ref)) + row(vec_ref, BIAS)
    normed, inverse = norm_parts(resid)
    normed_ref[...] = normed
    inv_ref[...] = inverse
    low = to_low(normed * row(vec_ref, GAIN) + row(vec_ref, SHIFT))
    low_ref[...] = low
    half = keep_ref.shape[1]
    left, right = (
        to_low(nn(low, wq_ref[:, part]) + vec_ref[QUERY_BIAS : QUERY_BIAS + 1, part])
        for part in (slice(0, half), slice(half, 2 * half))
    )
    keep_ref[...], send_ref[...] = halves(s_ref[CORE_AT], left, right)


def middle_kernel(
    s_ref,
    normed_ref,
    mine_ref,
    came_ref,
    vec_ref,
    bias_ref,
    bias_far_ref,
    back_hbm,
    in_hbm,
    in_far_hbm,
    out_hbm,
    out_far_hbm,
    heads_ref,
    normed_two_ref,
    inv_ref,
    low_ref,
    hidden_ref,
    hidden_far_ref,
    slope_ref,
    slope_far_ref,
    fed_ref,
    back,
    w_in,
    w_in_far,
    w_out,
    w_out_far,
    sem,
):
    loads = []
    for i, (source, target) in enumerate(
        (
            (back_hbm, back),
            (in_hbm, w_in),
            (in_far_hbm, w_in_far),
            (out_hbm, w_out),
            (out_far_hbm, w_out_far),
        )
    ):
        loads.append(pltpu.make_async_copy(source, target, sem.at[i]))
        loads[i].start()
    heads = jnp.concatenate(halves(s_ref[CORE_AT], mine_ref[...], came_ref[...]), axis=1)
    heads_ref[...] = heads
    first = normed_ref[...] * row(vec_ref, GAIN) + row(vec_ref, SHIFT)
    loads[0].wait()
    normed, inverse = norm_parts(first + nn(heads, back[...]) + row(vec_ref, BIAS + 1))
    normed_two_ref[...] = normed
    inv_ref[...] = inverse
    low = to_low(normed * row(vec_ref, GAIN + 1) + row(vec_ref, SHIFT + 1))
    low_ref[...] = low
    for i, (weight, shift, hidden, slope) in enumerate(
        ((w_in, bias_ref, hidden_ref, slope_ref), (w_in_far, bias_far_ref, hidden_far_ref, slope_far_ref))
    ):
        loads[1 + i].wait()
        for at in range(0, weight.shape[1], TILE):
            part = slice(at, at + TILE)
            pre = nn(low, weight[:, part]) + shift[:, part]
            share = 0.5 * (1.0 + lax.erf(pre * (0.5**0.5)))
            hidden[:, part] = to_low(pre * share)
            density = jnp.exp(-0.5 * pre * pre) * (1.0 / (2.0 * jnp.pi) ** 0.5)
            slope[:, part] = to_low(share + pre * density)
    loads[3].wait()
    loads[4].wait()
    for at in range(0, fed_ref.shape[1], TILE):
        part = slice(at, at + TILE)
        fed_ref[:, part] = to_low(
            nn(hidden_ref[...], w_out[:, part]) + nn(hidden_far_ref[...], w_out_far[:, part])
        )


def turn_kernel(
    s_ref,
    normed_two_ref,
    mine_ref,
    came_ref,
    vec_ref,
    grad_ref,
    slope_ref,
    slope_far_ref,
    in_hbm,
    in_far_hbm,
    out_hbm,
    out_far_hbm,
    final_ref,
    d_ref,
    d_low_ref,
    pre_ref,
    pre_far_ref,
    part_ref,
    sums_ref,
    pre_sums_ref,
    w_in,
    w_in_far,
    w_out,
    w_out_far,
    sem,
):
    loads = []
    for i, (source, target) in enumerate(
        ((out_hbm, w_out), (out_far_hbm, w_out_far), (in_hbm, w_in), (in_far_hbm, w_in_far))
    ):
        loads.append(pltpu.make_async_copy(source, target, sem.at[i]))
        loads[i].start()
    second = normed_two_ref[...] * row(vec_ref, GAIN + 1) + row(vec_ref, SHIFT + 1)
    resid = second + (wide(mine_ref) + wide(came_ref)) + row(vec_ref, BIAS + 2)
    normed, inverse = norm_parts(resid)
    gain = row(vec_ref, GAIN + 2)
    final_ref[...] = to_low(normed * gain + row(vec_ref, SHIFT + 2))
    upstream = wide(grad_ref)
    d_resid = norm_back(normed, inverse, gain, upstream)
    d_ref[...] = d_resid
    d_low = to_low(d_resid)
    d_low_ref[...] = d_low
    sums_ref[...] = jnp.zeros_like(sums_ref)
    sums_ref[0:1, :] = col_sum(upstream * normed)
    sums_ref[1:2, :] = col_sum(upstream)
    sums_ref[2:3, :] = col_sum(d_resid)
    pre_sums_ref[...] = jnp.zeros_like(pre_sums_ref)
    for i, (weight, slope, pre) in enumerate(
        ((w_out, slope_ref, pre_ref), (w_out_far, slope_far_ref, pre_far_ref))
    ):
        loads[i].wait()
        for at in range(0, weight.shape[0], TILE):
            part = slice(at, at + TILE)
            d_pre = to_low(nt(d_low, weight[part, :]) * slope[:, part].astype(f32))
            pre[:, part] = d_pre
            pre_sums_ref[i : i + 1, part] = col_sum(d_pre.astype(f32))
    loads[2].wait()
    loads[3].wait()
    for at in range(0, part_ref.shape[1], TILE):
        part = slice(at, at + TILE)
        part_ref[:, part] = to_low(
            nt(pre_ref[...], w_in[part, :]) + nt(pre_far_ref[...], w_in_far[part, :])
        )


def second_back_kernel(
    s_ref,
    d_three_ref,
    mine_ref,
    came_ref,
    normed_ref,
    inv_ref,
    vec_ref,
    back_ref,
    d_ref,
    d_low_ref,
    keep_ref,
    send_ref,
    sums_ref,
):
    upstream = d_three_ref[...] + (wide(mine_ref) + wide(came_ref))
    normed = normed_ref[...]
    d_resid = norm_back(normed, inv_ref[...], row(vec_ref, GAIN + 1), upstream)
    d_ref[...] = d_resid
    d_low = to_low(d_resid)
    d_low_ref[...] = d_low
    half = keep_ref.shape[1]
    left = to_low(nt(d_low, back_ref[:half, :]))
    right = to_low(nt(d_low, back_ref[half:, :]))
    keep_ref[...], send_ref[...] = halves(s_ref[CORE_AT], left, right)
    sums_ref[...] = jnp.zeros_like(sums_ref)
    sums_ref[0:1, :] = col_sum(upstream * normed)
    sums_ref[1:2, :] = col_sum(upstream)
    sums_ref[2:3, :] = col_sum(d_resid)
    sums_ref[3:4, :half] = col_sum(left.astype(f32))
    sums_ref[3:4, half:] = col_sum(right.astype(f32))


def split_sum_kernel(s_ref, mine_ref, came_ref, keep_ref, send_ref):
    rows = keep_ref.shape[0]
    for out, core in ((send_ref, 1 - s_ref[CORE_AT]), (keep_ref, s_ref[CORE_AT])):
        part = dyn(core * rows, rows)
        out[...] = add_low(mine_ref[part, :], came_ref[part, :])


def first_back_kernel(
    s_ref,
    d_two_ref,
    mine_ref,
    came_ref,
    normed_ref,
    inv_ref,
    vec_ref,
    wq_ref,
    left_ref,
    right_ref,
    query_ref,
    sums_ref,
):
    d_query = jnp.concatenate(halves(s_ref[CORE_AT], mine_ref[...], came_ref[...]), axis=1)
    query_ref[...] = d_query
    upstream = d_two_ref[...] + nt(d_query, wq_ref[...])
    normed = normed_ref[...]
    d_resid = norm_back(normed, inv_ref[...], row(vec_ref, GAIN), upstream)
    half = left_ref.shape[1]
    left_ref[...] = to_low(d_resid[:, :half])
    right_ref[...] = to_low(d_resid[:, half:])
    sums_ref[...] = jnp.zeros_like(sums_ref)
    sums_ref[0:1, :] = col_sum(upstream * normed)
    sums_ref[1:2, :] = col_sum(upstream)
    sums_ref[2:3, :] = col_sum(d_resid)
    sums_ref[3:4, :] = col_sum(d_query.astype(f32))


def stacked(block, first_head):
    zero = jnp.zeros_like(block)
    return jnp.concatenate(
        [jnp.where(first_head, block, zero), jnp.where(first_head, zero, block)], axis=0
    )


def unstacked(both, first_head):
    rows = both.shape[0] // 2
    return jnp.where(first_head, both[:rows], both[rows:])


def first_lanes(rows):
    return lax.broadcasted_iota(jnp.int32, (rows, PAIR), 1) < HEAD_DIM


def row_sums(values):
    lanes = lax.broadcasted_iota(jnp.int32, (16, PAIR), 1)
    which = lax.broadcasted_iota(jnp.int32, (16, PAIR), 0)
    pick = to_low((lanes // HEAD_DIM == which).astype(f32))
    high = to_low(values)
    low = to_low(values - high.astype(f32))
    sums = nt(pick, high) + nt(pick, low)
    return jnp.concatenate([sums[0:1], sums[1:2]], axis=1)


def shown(length, place, rows):
    spot = lax.broadcasted_iota(jnp.int32, (rows, 1), 0)
    return jnp.concatenate(
        [place * rows + spot < length, (place ^ CORE) * rows + spot < length], axis=0
    )


def join_rows(core, mine_ref, came_ref, both):
    rows = mine_ref.shape[0]
    both[dyn(core * rows, rows), :] = mine_ref[...]
    both[dyn((1 - core) * rows, rows), :] = came_ref[...]


def cross_forward_kernel(s_ref, mine_ref, came_ref, near_ref, far_ref, o_ref, stat_ref, both):
    item = pl.program_id(0)

    @pl.when(item == 0)
    def _():
        join_rows(s_ref[CORE_AT], mine_ref, came_ref, both)

    steps, width = o_ref.shape
    rows = dyn(item * steps, steps)
    visible = shown(s_ref[LENS + item], s_ref[PLACE], near_ref.shape[0])
    first_head = first_lanes(steps)
    for pair in range(width // PAIR):
        lanes = slice(pair * PAIR, (pair + 1) * PAIR)
        values = slice(width + pair * PAIR, width + (pair + 1) * PAIR)
        query = stacked(both[rows, lanes] * SCALE, first_head)
        key = jnp.concatenate([near_ref[:, lanes], far_ref[:, lanes]], axis=0)
        value = jnp.concatenate([near_ref[:, values], far_ref[:, values]], axis=0)
        scores = jnp.where(visible, nt(key, query), MASKED)
        top = jnp.max(scores, axis=0, keepdims=True)
        grown = jnp.exp(scores - top)
        total = jnp.sum(grown, axis=0, keepdims=True)
        weights = to_low(grown * (1.0 / total))
        o_ref[:, lanes] = to_low(unstacked(tn(weights, value), first_head))
        stat = top + jnp.log(total)
        stat_ref[0, 2 * pair : 2 * pair + 1, :] = stat[:, :steps]
        stat_ref[0, 2 * pair + 1 : 2 * pair + 2, :] = stat[:, steps:]


def cross_forward(info, items, mine, came, near, far):
    width, tokens = mine.shape[1], 2 * mine.shape[0]
    rows, steps = near.shape[0] // items, tokens // items
    heads = width // HEAD_DIM
    keys = pl.BlockSpec((rows, 2 * width), lambda i, *_: (i, 0))
    return call(
        cross_forward_kernel,
        info,
        [mine, came, (near, keys), (far, keys)],
        [((tokens, width), bf16), ((items, heads, steps), f32)],
        scratch=[pltpu.VMEM((tokens, width), bf16)],
        grid=(items,),
        mega=14,
        out_specs=[
            pl.BlockSpec((steps, width), lambda i, *_: (i, 0)),
            pl.BlockSpec((1, heads, steps), lambda i, *_: (i, 0, 0)),
        ],
    )


def merge_kernel(bit, s_ref, a_ref, sa_ref, b_ref, sb_ref, o_ref, stat_ref):
    flip = (s_ref[PLACE] & bit) != 0
    items, heads, steps = sa_ref.shape
    width = a_ref.shape[1]
    pick = lax.broadcasted_iota(jnp.int32, (heads, width), 1) // HEAD_DIM
    pick = to_low((pick == lax.broadcasted_iota(jnp.int32, (heads, width), 0)).astype(f32))

    def spread(share):
        high = to_low(share)
        return tn(high, pick) + tn(to_low(share - high.astype(f32)), pick)

    for item in range(items):
        rows = slice(item * steps, (item + 1) * steps)
        mine, theirs = sa_ref[item], sb_ref[item]
        first, second = jnp.where(flip, theirs, mine), jnp.where(flip, mine, theirs)
        top = jnp.maximum(first, second)
        grown_first, grown_second = jnp.exp(first - top), jnp.exp(second - top)
        total = grown_first + grown_second
        stat_ref[item] = top + jnp.log(total)
        low_values = jnp.where(flip, b_ref[rows, :], a_ref[rows, :]).astype(f32)
        high_values = jnp.where(flip, a_ref[rows, :], b_ref[rows, :]).astype(f32)
        o_ref[rows, :] = to_low(
            spread(grown_first / total) * low_values + spread(grown_second / total) * high_values
        )


def merge(info, bit, mine, stat_mine, theirs, stat_theirs):
    return call(
        functools.partial(merge_kernel, bit),
        info,
        [mine, stat_mine, theirs, stat_theirs],
        [(mine.shape, bf16), (stat_mine.shape, f32)],
        name="merge",
    )


def cross_backward_kernel(
    s_ref, q_ref, q_came_ref, do_mine_ref, do_came_ref, o_ref, stat_ref, near_ref, far_ref,
    dq_ref, dnear_ref, dfar_ref, q_both, do_both,
):
    item = pl.program_id(0)

    @pl.when(item == 0)
    def _():
        join_rows(s_ref[CORE_AT], q_ref, q_came_ref, q_both)
        join_rows(s_ref[CORE_AT], do_mine_ref, do_came_ref, do_both)

    steps, width = dq_ref.shape
    rows = near_ref.shape[0]
    tokens = dyn(item * steps, steps)
    visible = shown(s_ref[LENS + item], s_ref[PLACE], rows)
    first_head = first_lanes(steps)
    for pair in range(width // PAIR):
        lanes = slice(pair * PAIR, (pair + 1) * PAIR)
        values = slice(width + pair * PAIR, width + (pair + 1) * PAIR)
        d_out = do_both[tokens, lanes]
        dots = row_sums(d_out.astype(f32) * o_ref[:, lanes].astype(f32))
        stat = jnp.concatenate(
            [stat_ref[0, 2 * pair : 2 * pair + 1, :], stat_ref[0, 2 * pair + 1 : 2 * pair + 2, :]],
            axis=1,
        )
        query = stacked(q_both[tokens, lanes] * SCALE, first_head)
        d_both = stacked(d_out, first_head)
        key = jnp.concatenate([near_ref[:, lanes], far_ref[:, lanes]], axis=0)
        value = jnp.concatenate([near_ref[:, values], far_ref[:, values]], axis=0)
        scores = jnp.where(visible, nt(key, query), MASKED)
        probs = jnp.exp(scores - stat)
        d_scores = to_low(probs * (nt(value, d_both) - dots))
        d_value = to_low(nn(to_low(probs), d_both))
        d_key = to_low(nn(d_scores, query))
        dnear_ref[:, lanes] = d_key[:rows]
        dfar_ref[:, lanes] = d_key[rows:]
        dnear_ref[:, values] = d_value[:rows]
        dfar_ref[:, values] = d_value[rows:]
        dq_ref[:, lanes] = to_low(unstacked(tn(d_scores, key), first_head) * SCALE)


def cross_backward(info, queries, d_outs, out, stat, near, far):
    items, heads, steps = stat.shape
    tokens, width = out.shape
    rows = near.shape[0] // items
    keys = pl.BlockSpec((rows, 2 * width), lambda i, *_: (i, 0))
    block = pl.BlockSpec((steps, width), lambda i, *_: (i, 0))
    return call(
        cross_backward_kernel,
        info,
        list(queries)
        + list(d_outs)
        + [
            (out, block),
            (stat, pl.BlockSpec((1, heads, steps), lambda i, *_: (i, 0, 0))),
            (near, keys),
            (far, keys),
        ],
        [(out.shape, bf16), (near.shape, bf16), (far.shape, bf16)],
        scratch=[pltpu.VMEM((tokens, width), bf16)] * 2,
        grid=(items,),
        mega=14,
        out_specs=[block, keys, keys],
    )


def self_weights(query_block, key_block, first_head, allowed):
    query = stacked(query_block * SCALE, first_head)
    scores = jnp.where(allowed, nt(key_block, query), MASKED)
    top = jnp.max(scores, axis=0, keepdims=True)
    grown = jnp.exp(scores - top)
    total = jnp.sum(grown, axis=0, keepdims=True)
    return query, grown * (1.0 / total)


def self_parts(len_ref, items, tokens, width):
    steps = tokens // items
    keys = lax.broadcasted_iota(jnp.int32, (steps, 2 * steps), 0)
    queries = lax.broadcasted_iota(jnp.int32, (steps, 2 * steps), 1) % steps
    causal = keys <= queries
    for item in range(items):
        allowed = jnp.logical_and(causal, keys < len_ref[LENS + items + item])
        for pair in range(width // PAIR):
            yield (
                slice(item * steps, (item + 1) * steps),
                slice(pair * PAIR, (pair + 1) * PAIR),
                allowed,
            )


def self_forward_kernel(items, len_ref, q_ref, k_ref, v_ref, o_ref):
    tokens, width = q_ref.shape
    first_head = first_lanes(tokens // items)
    for rows, lanes, allowed in self_parts(len_ref, items, tokens, width):
        _, probs = self_weights(q_ref[rows, lanes], k_ref[rows, lanes], first_head, allowed)
        o_ref[rows, lanes] = to_low(unstacked(tn(to_low(probs), v_ref[rows, lanes]), first_head))


def self_backward_kernel(
    items, s_ref, q_ref, k_ref, v_ref, left_ref, right_ref, left_came, right_came, out_ref,
    d_low_ref, dq_ref, dk_ref, dv_ref, sums_ref, do_both,
):
    tokens, width = q_ref.shape
    half = left_ref.shape[1]
    for at, mine, came in ((0, left_ref, left_came), (half, right_ref, right_came)):
        part = slice(at, at + half)
        rows = mine.shape[0]
        d_low_ref[dyn(s_ref[CORE_AT] * rows, rows), part] = mine[...]
        d_low_ref[dyn((1 - s_ref[CORE_AT]) * rows, rows), part] = came[...]
    do_both[...] = to_low(nt(d_low_ref[...], out_ref[...]))
    first_head = first_lanes(tokens // items)
    for rows, lanes, allowed in self_parts(s_ref, items, tokens, width):
        key = k_ref[rows, lanes]
        query, probs = self_weights(q_ref[rows, lanes], key, first_head, allowed)
        d_both = stacked(do_both[rows, lanes], first_head)
        d_probs = nt(v_ref[rows, lanes], d_both)
        dots = jnp.sum(probs * d_probs, axis=0, keepdims=True)
        d_scores = to_low(probs * (d_probs - dots))
        dv_ref[rows, lanes] = to_low(nn(to_low(probs), d_both))
        dk_ref[rows, lanes] = to_low(nn(d_scores, query))
        dq_ref[rows, lanes] = to_low(unstacked(tn(d_scores, key), first_head) * SCALE)
    sums_ref[...] = jnp.zeros_like(sums_ref)
    sums_ref[0:1, :] = col_sum(dq_ref[...].astype(f32))
    sums_ref[1:2, :] = col_sum(do_both[...].astype(f32))


def grad_half_kernel(count, s_ref, *refs):
    for at in range(0, refs[-1].shape[1], TILE):
        part = slice(at, at + TILE)
        total = tn(refs[0][...], refs[count][:, part])
        for i in range(1, count):
            total = total + tn(refs[i][...], refs[count + i][:, part])
        refs[-1][:, part] = to_low(total)


def grad_half(info, index, lefts, rights):
    rows, columns = lefts[0].shape[1] // 2, rights[0].shape[1]
    spec = lambda left: pl.BlockSpec((left.shape[0], rows), lambda i, s: (0, index(s)))
    return call(
        functools.partial(grad_half_kernel, len(lefts)),
        info,
        [(left, spec(left)) for left in lefts] + list(rights),
        [((rows, columns), bf16)],
        cost=5.0,
        name="grad_half",
    )[0]


def self_grad_kernel(s_ref, x0_ref, x1_ref, d0_ref, d1_ref, q_ref, k_ref, v_ref, h_ref, *outs):
    width = q_ref.shape[1]
    for x_ref, d_ref, out in ((x0_ref, d0_ref, outs[0]), (x1_ref, d1_ref, outs[1])):
        for i, ref in enumerate((q_ref, k_ref, v_ref)):
            out[:, i * width : (i + 1) * width] = to_low(tn(x_ref[...], ref[...]))
        out[:, 3 * width :] = to_low(tn(d_ref[...], h_ref[...]))


def self_grad(info, first, second, x, d_low, query, key, value, heads):
    rows, tokens, width = x.shape[1] // 4, x.shape[0], query.shape[1]
    at = lambda index: pl.BlockSpec((tokens, rows), lambda i, s: (0, index(s)))
    return call(
        self_grad_kernel,
        info,
        [(x, at(first)), (x, at(second)), (d_low, at(first)), (d_low, at(second)), query, key, value, heads],
        [((rows, 4 * width), bf16)] * 2,
    )


def put_wide(out, at, values):
    rows = values.shape[0]
    high = to_low(values)
    out[at : at + rows, :] = high
    out[at + rows : at + 2 * rows, :] = to_low(values - high.astype(f32))


def get_wide(ref, at, rows):
    return ref[at : at + rows, :].astype(f32) + ref[at + rows : at + 2 * rows, :].astype(f32)


def split_kernel(positions, joint, s_ref, *refs):
    count = len(positions)
    mine, came, outs = refs[:count], refs[count : 2 * count], refs[2 * count :]
    sends, keeps = outs[:-count], outs[-count:]
    rows = keeps[0].shape[0]
    for k, position in enumerate(positions):
        base = 2 * rows * k if joint[0] else 0
        for send in (True, False):
            half = 1 - s_ref[position] if send else s_ref[position]
            total = add_low(
                mine[k][dyn(half * rows, rows), :], came[k][dyn(base + half * rows, rows), :]
            )
            if not send:
                keeps[k][...] = total
            elif joint[1]:
                sends[0][k * rows : (k + 1) * rows, :] = total
            else:
                sends[k][...] = total


def split(info, bits, mine, came, joint):
    rows, columns = mine[0].shape[0] // 2, mine[0].shape[1]
    sends = [2 * rows] if joint[1] else [rows] * len(bits)
    return call(
        functools.partial(split_kernel, [dp_position(bit) for bit in bits], joint),
        info,
        list(mine) + list(came),
        [((size, columns), bf16) for size in sends + [rows] * len(bits)],
        name="split_sums",
    )


def total_kernel(joint, extra, s_ref, *refs):
    mine, came, outs = refs[:2], refs[2:4], refs[4 + extra :]
    rows = mine[0].shape[0]
    for k in range(2):
        base = rows * k if joint[0] else 0
        total = add_low(mine[k][...], came[k][base : base + rows, :])
        if joint[1]:
            outs[0][k * rows : (k + 1) * rows, :] = total
        else:
            outs[k][...] = total
    if extra:
        put_wide(outs[0], 2 * rows, refs[4][...])


def total_pair(info, mine, came, joint, extra=None):
    rows, columns = mine[0].shape
    extras = [] if extra is None else [extra]
    more = 2 * sum(v.shape[0] for v in extras)
    outputs = [2 * rows + more] if joint[1] else [rows, rows]
    return call(
        functools.partial(total_kernel, joint, len(extras)),
        info,
        list(mine) + list(came) + extras,
        [((size, columns), bf16) for size in outputs],
        name="total_sums",
    )


def join_pair_kernel(positions, given, extra, s_ref, *refs):
    mine, came, outs = refs[:given], refs[given : 2 * given], refs[2 * given :]
    joint = given < len(positions)
    rows = mine[0].shape[0] - 2 * extra
    rows = rows // 2 if joint else rows
    for k, position in enumerate(positions):
        part = slice(k * rows, (k + 1) * rows) if joint else slice(0, rows)
        own, other = mine[k % given][part, :], came[k % given][part, :]
        base = 2 * rows * k if len(outs) < len(positions) else 0
        out = outs[k % len(outs)]
        out[dyn(base + s_ref[position] * rows, rows), :] = own
        out[dyn(base + (1 - s_ref[position]) * rows, rows), :] = other
    if extra:
        at = mine[0].shape[0] - 2 * extra
        total = get_wide(mine[0], at, extra) + get_wide(came[0], at, extra)
        put_wide(outs[0], outs[0].shape[0] - 2 * extra, total)


def join_pair(info, bits, mine, came, joint, extra=0, cost=8.0):
    given, columns = len(mine), mine[0].shape[1]
    rows = mine[0].shape[0] - 2 * extra
    rows = (rows if given == len(bits) else rows // 2) * 2
    more = 2 * extra
    outputs = [len(bits) * rows + more] if joint else [rows + more] + [rows] * (len(bits) - 1)
    return call(
        functools.partial(
            join_pair_kernel, [dp_position(bit) for bit in bits], given, extra
        ),
        info,
        list(mine) + list(came),
        [((size, columns), bf16) for size in outputs],
        cost=cost,
        name="join_pair",
    )


def join_kernel(position, s_ref, mine_ref, came_ref, out_ref):
    @pl.when(pl.program_id(1) == s_ref[position])
    def _():
        out_ref[...] = mine_ref[...].astype(out_ref.dtype)

    @pl.when(pl.program_id(1) != s_ref[position])
    def _():
        out_ref[...] = came_ref[...].astype(out_ref.dtype)


def join(info, bit, mine, came, rows):
    columns = mine.shape[1]
    spec = pl.BlockSpec((rows, columns), lambda i, j, s: (0, 0))
    return call(
        functools.partial(join_kernel, dp_position(bit)),
        info,
        [(mine, spec), (came, spec)],
        [((2 * rows, columns), f32)],
        grid=(1, 2),
        out_specs=[pl.BlockSpec((rows, columns), lambda i, j, s: (j, 0))],
        name="join",
    )[0]


class PairSum:
    def __init__(self, info, orders, keeps, cames):
        self.info, self.step = info, 1
        self.bits = list(zip(*orders))
        self.back = self.bits[::-1]
        self.mine, self.came, self.extra = tuple(keeps), tuple(cames), None
        self.joint, self.gathering = False, False

    def pending(self):
        return self.came

    def arrived(self, came):
        self.came = came

    def exchange(self, values, bits):
        if len(values) == 1:
            self.came = (swap(values[0], "dp", bits[0]),)
        else:
            self.came = tuple(swap(value, "dp", bit) for value, bit in zip(values, bits))

    def advance(self):
        same = lambda bits: bits[0] == bits[1]
        came = self.came if len(self.came) == 2 else self.came * 2
        if self.step < len(self.bits):
            bits = self.bits[self.step]
            joint = (self.joint, same(bits))
            result = split(self.info, bits, self.mine, came, joint)
            sent, self.mine, self.joint = tuple(result[:-2]), tuple(result[-2:]), joint[1]
            self.step += 1
            self.exchange(sent, bits)
            return sent
        if not self.gathering:
            joint = (self.joint, same(self.back[0]))
            self.values = total_pair(self.info, self.mine, came, joint, self.extra)
            self.gathering = True
        else:
            bits = self.back.pop(0)
            extra = 0 if self.extra is None else self.extra.shape[0]
            joint = same(self.back[0])
            self.values = tuple(
                join_pair(
                    self.info,
                    bits,
                    self.values,
                    self.came,
                    joint,
                    extra,
                    0.0 if len(self.back) == 1 else 8.0,
                )
            )
        self.exchange(self.values, self.back[0])
        return tuple(self.values)

    def advance_one(self, k, *points):
        bit, last = self.back[0][k], self.back[1][k]
        extra = 0 if k or self.extra is None else self.extra.shape[0]
        mine, came = self.values[k], after(self.came[k], *points) if points else self.came[k]
        cost = 8.0 if k else 8.0
        (values,) = join_pair(self.info, [bit], [mine], [came], False, extra, cost)
        self.values = self.values[:k] + (values,) + self.values[k + 1 :]
        self.came = self.came[:k] + (swap(values, "dp", last),) + self.came[k + 1 :]
        if k:
            self.back.pop(0)
        return (values,)

    def gathered(self):
        return self.gathering and len(self.back) == 1

    def whole(self, k, *points):
        self.came = self.came[:k] + (after(self.came[k], *points),) + self.came[k + 1 :]
        rows = self.values[1].shape[0]
        return join(self.info, self.back[0][k], self.values[k], self.came[k], rows)

    def extra_sum(self):
        extra = self.extra.shape[0]
        at = self.values[0].shape[0] - 2 * extra
        total = self.values[0][at:].astype(f32) + self.came[0][at:].astype(f32)
        return total[:extra] + total[extra:]


class BlockSum:
    def __init__(self, info, keep, came):
        self.info, self.order = info, bits_of("dp")[1:]
        self.mine, self.came = keep, (came,)

    def pending(self):
        return self.came

    def arrived(self, came):
        self.came = came

    def summed(self):
        return not self.order

    def advance(self):
        bit = self.order.pop(0)
        sent, self.mine = split(self.info, [bit], [self.mine], self.came, (False, False))
        self.came = (swap(sent, "dp", bit),)
        return (sent,)

    def total(self):
        return self.mine.astype(f32) + self.came[0].astype(f32)


def take_turns(flows, *points):
    if not flows:
        return ()
    came = lax.optimization_barrier((tuple(flow.pending() for flow in flows), points))[0]
    for flow, values in zip(flows, came):
        flow.arrived(values)
    return sum((flow.advance() for flow in flows), ())


def self_finish_kernel(first, second, s_ref, upper_ref, upper_came_ref, lower_ref, lower_came_ref, in_ref, out_ref):
    rows, width = upper_ref.shape[0], in_ref.shape[2]
    blocks = halves(s_ref[first], upper_ref[...], upper_came_ref[...])
    blocks = blocks + halves(s_ref[second], lower_ref[...], lower_came_ref[...])
    for at, block in enumerate(blocks):
        block = block.astype(f32)
        part = slice(at * rows, (at + 1) * rows)
        for i in range(3):
            in_ref[i, part, :] = block[:, i * width : (i + 1) * width]
        out_ref[:, part] = block[:, 3 * width :].T


def second_order(bits):
    return bits[1:2] + bits[:1] + bits[2:]


def spot_of(block, blocks):
    order = [1 << i for i in range(blocks.bit_length() - 1)]
    return sum((block // bit % 2) << (len(order) - 1 - i) for i, bit in enumerate(order))


def cross_grad_kernel(blocks, s_ref, *refs):
    scratch = refs[10]
    for k in range(2):
        left, right = refs[2 * k], refs[2 * k + 1]
        keep, first, second = refs[4 + 3 * k : 7 + 3 * k]
        rows, half = keep.shape[0] // blocks, first.shape[1]
        for at in range(0, right.shape[1], TILE):
            part = slice(at, at + TILE)
            scratch[...] = to_low(tn(left[...], right[:, part]))
            size = scratch.shape[0] // blocks
            send, column = (first, at) if at < half else (second, at - half)
            sent = slice(column, column + TILE)
            for block in range(blocks):
                turned = spot_of(block, blocks)
                to = slice(turned * rows, (turned + 1) * rows)
                own = dyn(block * size + s_ref[PLACE] * rows, rows)
                other = dyn(block * size + (s_ref[PLACE] ^ CORE) * rows, rows)
                keep[to, part] = scratch[own, :]
                send[to, sent] = scratch[other, :]


def cross_grad(info, blocks, shard, pairs):
    width = pairs[0][0].shape[1]
    rows = blocks * shard
    outputs = [((rows, width), bf16), ((rows, width // 2), bf16), ((rows, width // 2), bf16)]
    return call(
        functools.partial(cross_grad_kernel, blocks),
        info,
        [array for pair in pairs for array in pair],
        outputs * 2,
        scratch=[pltpu.VMEM((width, TILE), bf16)],
        name="cross_grad",
    )


def input_part_kernel(s_ref, q_ref, k_ref, v_ref, weight_ref, keep_ref, send_ref):
    width = q_ref.shape[1]
    for out, core in ((send_ref, 1 - s_ref[CORE_AT]), (keep_ref, s_ref[CORE_AT])):
        for i in range(out.shape[1] // width):
            rows = dyn((2 * i + core) * width, width)
            total = nt(q_ref[...], weight_ref[0, rows, :])
            total = total + nt(k_ref[...], weight_ref[1, rows, :])
            total = total + nt(v_ref[...], weight_ref[2, rows, :])
            out[:, i * width : (i + 1) * width] = to_low(total)


def input_sum_kernel(s_ref, mine_ref, came_ref, d_ref, keep_ref, send_ref):
    width = keep_ref.shape[1]
    chip = s_ref[PLACE] // 2
    other = dyn((1 - chip) * width, width, 128)
    send_ref[...] = add_low(mine_ref[:, other], came_ref[:, other])
    own = dyn(chip * width, width, 128)
    keep_ref[...] = (
        mine_ref[:, own].astype(f32)
        + came_ref[:, own].astype(f32)
        + d_ref[:, dyn(s_ref[PLACE] * width, width, 128)].astype(f32)
    )


def memory_kernel(s_ref, d_ref, weight_ref, *refs):
    total = nt(d_ref[...], weight_ref[...])
    if len(refs) == 2:
        total = total + wide(refs[0])
    refs[-1][...] = to_low(total)


def memory_part(info, items, d_ref, weight, *came):
    rows = pl.BlockSpec((d_ref.shape[0] // items, d_ref.shape[1]), lambda i, s: (i, 0))
    return call(
        memory_kernel,
        info,
        [(d_ref, rows), weight] + [(array, rows) for array in came],
        [(d_ref.shape, bf16)],
        grid=(items,),
        out_specs=[rows],
        mega=12,
        name="memory_grad",
    )[0]


def stack_kernel(s_ref, one_ref, two_ref, three_ref, pre_ref, out_ref):
    out_ref[...] = jnp.zeros_like(out_ref)
    out_ref[0:8, :], out_ref[8:16, :], out_ref[16:24, :] = one_ref[...], two_ref[...], three_ref[...]
    out_ref[24:32, : pre_ref.shape[1]] = pre_ref[...]


SMALL = (0, 8, 16, 1, 9, 17, 2, 10, 18, 3, 11)


def small_kernel(s_ref, mine_ref, came_ref, self_ref, out_ref):
    out_ref[...] = jnp.zeros_like(out_ref)
    for to, at in enumerate(SMALL):
        out_ref[to : to + 1, :] = mine_ref[at : at + 1, :] + came_ref[at : at + 1, :]
    to = len(SMALL)
    out_ref[to : to + 1, :] = mine_ref[24:25, :] + came_ref[25:26, :]
    out_ref[to + 1 : to + 3, : self_ref.shape[1]] = self_ref[0:2, :]


def other_chip_kernel(blocks, s_ref, values, out):
    size, rows = values.shape[0] // blocks, out.shape[0] // blocks
    for block in range(blocks):
        to = spot_of(block, blocks) * rows
        start = block * size + (1 - s_ref[PLACE] // 2) * rows
        out[to : to + rows, :] = values[dyn(start, rows), :]


def chip_rows_kernel(blocks, s_ref, values, came, keep, first, second):
    size, rows = values.shape[0] // blocks, keep.shape[0] // blocks
    half = first.shape[1]
    for block in range(blocks):
        turned = spot_of(block, blocks)
        to = slice(turned * rows, (turned + 1) * rows)
        own = values[dyn(block * size + s_ref[PLACE] * rows, rows), :]
        keep[to, :] = add_low(own, came[dyn((2 * turned + s_ref[CORE_AT]) * rows, rows), :])
        other = values[dyn(block * size + (s_ref[PLACE] ^ CORE) * rows, rows), :]
        other = add_low(other, came[dyn((2 * turned + 1 - s_ref[CORE_AT]) * rows, rows), :])
        first[to, :] = other[:, :half]
        second[to, :] = other[:, half:]


def cross_rows_kernel(blocks, s_ref, *refs):
    send, keep = refs[9:]
    rows = refs[0].shape[0] // blocks
    for block in range(blocks):
        part = slice(block * rows, (block + 1) * rows)
        came = [
            jnp.concatenate([refs[3 * k + 1][part, :], refs[3 * k + 2][part, :]], axis=1)
            for k in range(3)
        ]
        values = [add_low(refs[0][part, :], came[0]), add_low(refs[3][part, :], came[1])]
        values.extend(halves(s_ref[CORE_AT], refs[6][part, :], came[2]))
        base = 4 * rows * (block % (blocks // 2))
        mine = s_ref[DP_AT] == block // (blocks // 2)
        for out, chosen in ((keep, mine), (send, jnp.logical_not(mine))):

            @pl.when(chosen)
            def _():
                for i, value in enumerate(values):
                    out[base + i * rows : base + (i + 1) * rows, :] = value


def general_cross_rows(d_q, d_back, d_kv, shard):
    dp_size, mem_size = lax.axis_size("dp"), lax.axis_size("mem")
    width = d_q.shape[1]

    def split(values, axis, bit, dim):
        mine = bit_at(axis, bit)
        entry = lambda at: lax.dynamic_index_in_dim(values, at, dim, keepdims=False)
        return entry(mine), entry(1 - mine)

    mem_dims = (2,) * len(bits_of("mem"))
    own = []
    for grad in (d_q, d_back):
        grad = grad.reshape((dp_size,) + mem_dims + (shard, width))
        for bit in chip_bits()[::-1]:
            grad = split(grad, "mem", bit, 1)[0]
        keep, send = split(grad, "mem", CORE, 1)
        own.append(add_low(keep, core_swap(send)))
    grad = d_kv.reshape((dp_size,) + mem_dims + (shard, width))
    for bit in chip_bits()[::-1]:
        keep, send = split(grad, "mem", bit, 1)
        grad = add_low(keep, swap(send, "mem", bit))
    keep, send = split(grad, "mem", CORE, 1)
    own = jnp.stack(own + list(halves(bit_at("mem", CORE), keep, core_swap(send))), axis=1)
    own = own.reshape((2,) * len(bits_of("dp")) + own.shape[1:])
    for bit in bits_of("dp")[::-1]:
        keep, send = split(own, "dp", bit, 0)
        own = add_low(keep, swap(send, "dp", bit))
    return own.astype(f32)


def local(
    dec_input,
    memory,
    dec_len,
    mem_len,
    self_in,
    self_in_bias,
    self_out,
    cross_in,
    cross_bias,
    cross_out,
    fc_in,
    fc_in_bias,
    fc_out,
    out_biases,
    norm_gains,
    norm_shifts,
    grad_out,
):
    items, steps, width = dec_input.shape
    mem_rows = memory.shape[1]
    local_width, hidden_width = self_in.shape[2], fc_in.shape[1]
    tokens = items * steps
    half, share = width // 2, tokens // 2
    dp_size, mem_size = lax.axis_size("dp"), lax.axis_size("mem")
    dp_bits = bits_of("dp")
    place = lax.axis_index("mem").astype(jnp.int32)
    core = bit_at("mem", CORE)
    numbers = [place, core, place * 0] + [bit_at("dp", bit) for bit in dp_bits]
    info = jnp.stack(numbers + [place * 0] * (LENS - len(numbers)))
    info = jnp.concatenate([info, mem_len, dec_len])

    x_low = dec_input.reshape(tokens, width)
    mem_low = memory.reshape(items * mem_rows, width)
    own_rows = pl.BlockSpec((share, width), lambda i, s: (s[CORE_AT], 0))
    columns = lambda values, at, size: lax.dynamic_slice_in_dim(values, at, size, 1)

    cross_pieces = relative({0: cross_in}, chip_bits())
    mem_far = core_swap(mem_low)
    bias_pieces = relative({0: cross_bias.T}, chip_bits())

    weight_self = jnp.transpose(self_in, (1, 0, 2))
    bias_self = self_in_bias.astype(f32)
    query_self = to_low(nn(x_low, weight_self[0]) + bias_self[0])
    key_self = to_low(nn(x_low, weight_self[1]))
    value_self = to_low(nn(x_low, weight_self[2]) + bias_self[1])
    (heads_self,) = call(
        functools.partial(self_forward_kernel, items),
        info,
        [query_self, key_self, value_self],
        [((tokens, local_width), bf16)],
        name="self_forward",
    )
    part_of = lambda core: lax.dynamic_slice_in_dim(heads_self, core * share, share, 0)
    came = core_swap(to_low(nn(part_of(1 - core), self_out)))
    attended = to_low(nn(part_of(core), self_out) + came.astype(f32))
    attended, attended_came = chip_swap(attended)

    points = (attended,) + tuple(bias_pieces.values())
    cross_pieces = {r: after(v, *points) if r else v for r, v in cross_pieces.items()}
    low_weight = [((width, width), bf16)]
    weight_kv, weight_query = assemble(
        info,
        relative(cross_pieces, [CORE]),
        ((0, width, half, 0, half), (0, 2 * width, half, half, half), (1, 0, 0, 0, width)),
        low_weight * 2,
        "cross_weights",
    )
    bias_pieces = relative(bias_pieces, [CORE])
    block = jnp.arange(width)[None, :] // local_width
    cross_shift = sum(
        jnp.where(block == (place ^ r), jnp.tile(v, (1, mem_size)).astype(f32), 0.0)
        for r, v in bias_pieces.items()
    )
    value_shift = lax.dynamic_slice_in_dim(cross_shift[1], core * half, half, 0)
    value_shift = jnp.concatenate([jnp.zeros((half,), f32), value_shift])
    vectors = jnp.concatenate(
        [
            norm_gains.astype(f32).T,
            norm_shifts.astype(f32).T,
            out_biases.astype(f32).T,
            cross_shift[:1],
            jnp.zeros((6, width), f32),
        ],
        axis=0,
    )
    kv_near = to_low(nn(mem_low, weight_kv) + value_shift)
    kv_far = to_low(nn(mem_far, weight_kv) + value_shift)
    fc_in_far, fc_out_far = core_swap(after(fc_in, attended)), core_swap(after(fc_out, attended))
    fc_bias = fc_in_bias[None].astype(f32)
    fc_bias_far = core_swap(fc_in_bias)[None].astype(f32)

    token_f32, token_low = ((share, width), f32), ((share, width), bf16)
    token_half, one_each = ((share, half), bf16), ((share, 1), f32)
    normed_one, inverse_one, first_low, query_keep, query_send = call(
        first_norm_kernel,
        info,
        [(x_low, own_rows), attended, after(attended_came, kv_near, kv_far), vectors, weight_query],
        [token_f32, one_each, token_low, token_half, token_half],
    )
    back_pieces = relative({0: after(cross_out, kv_near)}, chip_bits())
    back_pieces = {r: after(v, first_low) if r else v for r, v in back_pieces.items()}
    query_came = core_swap(query_send)
    (cross_back,) = assemble(
        info,
        relative(back_pieces, [CORE]),
        ((0, 0, 0, 0, width),),
        low_weight,
        "cross_back",
    )

    out, stat = cross_forward(info, items, query_keep, query_came, kv_near, kv_far)
    out = after(out, *back_pieces.values())
    for bit in chip_bits():
        out, stat = merge(info, bit, out, stat, swap(out, "mem", bit), swap(stat, "mem", bit))
    part_of_out = lambda core: lax.dynamic_slice_in_dim(out, core * share, share, 0)
    out_keep, out_came = part_of_out(core), core_swap(part_of_out(1 - core))

    units_low = ((share, hidden_width), bf16)
    weight = pltpu.VMEM((width, hidden_width), bf16)
    weight_out = pltpu.VMEM((hidden_width, width), bf16)
    cross_heads, normed_two, inverse_two, second_low, hidden, hidden_far, slope, slope_far, fed = call(
        middle_kernel,
        info,
        [normed_one, out_keep, out_came, vectors, fc_bias, fc_bias_far]
        + [(v, HBM) for v in (cross_back, fc_in, fc_in_far, fc_out, fc_out_far)],
        [token_low, token_f32, one_each, token_low] + [units_low] * 4 + [token_low],
        scratch=[
            pltpu.VMEM((width, width), bf16),
            weight,
            weight,
            weight_out,
            weight_out,
            pltpu.SemaphoreType.DMA((5,)),
        ],
        mega=20,
    )
    fed, fed_came = chip_swap(fed)
    second_other, hidden_other = core_swap(second_low), core_swap(hidden_far)
    final_low, d_three, d_three_low, d_pre, d_pre_far, d_fed, sums_three, pre_sums = call(
        turn_kernel,
        info,
        [normed_two, fed, fed_came, vectors, (grad_out.reshape(tokens, width), own_rows)]
        + [slope, slope_far]
        + [(v, HBM) for v in (fc_in, fc_in_far, fc_out, fc_out_far)],
        [token_low, token_f32, token_low, units_low, units_low, token_low]
        + [((8, width), f32), ((8, hidden_width), f32)],
        scratch=[weight, weight, weight_out, weight_out, pltpu.SemaphoreType.DMA((4,))],
        mega=20,
    )
    d_fed, d_fed_came = chip_swap(d_fed)

    order_one = dp_bits
    order_two = second_order(dp_bits)
    at_one, at_two = dp_position(order_one[0]), dp_position(order_two[0])
    d_three_other, d_pre_other = core_swap(d_three_low), core_swap(d_pre_far)
    fc_in_args = ([second_low, second_other], [d_pre, d_pre_other])
    fc_out_args = ([hidden, hidden_other], [d_three_low, d_three_other])
    upright = hidden_width == width
    if not upright:
        fc_in_args = fc_in_args[::-1]
    fc_in_send = grad_half(info, lambda s: 1 - s[at_one], *fc_in_args)
    fc_in_came = swap(fc_in_send, "dp", order_one[0])
    fc_out_send = grad_half(info, lambda s: 1 - s[at_two], *fc_out_args)
    fc_out_came = swap(fc_out_send, "dp", order_two[0])
    fc_in_keep = grad_half(info, lambda s: s[at_one], *fc_in_args)
    fc_out_keep = grad_half(info, lambda s: s[at_two], *fc_out_args)
    orders = (order_one, order_two)
    fc_sum = PairSum(
        info, orders, (fc_in_keep, fc_out_keep), (fc_in_came, fc_out_came)
    )

    d_fed_came = after(d_fed_came, fc_in_send, fc_out_send, fc_in_keep, fc_out_keep)
    d_two, d_two_low, d_keep, d_send, sums_two = call(
        second_back_kernel,
        info,
        [d_three, d_fed, d_fed_came, normed_two, inverse_two, vectors, cross_back],
        [token_f32, token_low, token_half, token_half, ((8, width), f32)],
    )
    d_came = core_swap(d_send)

    d_query_part, d_near, d_far = cross_backward(
        info, (query_keep, query_came), (d_keep, d_came), out, stat, kv_near, kv_far
    )
    d_query_part, d_query_came = chip_swap(d_query_part)
    flows_fc = [fc_sum]
    last = take_turns(flows_fc, d_query_part)

    d_kv = to_low(tn(mem_low, after(d_near, *last)) + tn(mem_far, d_far))
    shard = width // (dp_size * mem_size)
    simple = shard % 16 == 0 and mem_size == 4
    d_query_came = after(d_query_came, *take_turns(flows_fc, d_kv))
    if simple:
        (d_kv_send,) = call(
            functools.partial(other_chip_kernel, dp_size),
            info,
            [d_kv],
            [((width // 2, width), bf16)],
            name="other_chip",
        )
        d_kv_came = swap(d_kv_send, "mem", chip_bits()[0])
        d_query_came = after(d_query_came, d_kv_send)
    d_query_keep, d_query_send = call(
        split_sum_kernel, info, [d_query_part, d_query_came], [token_half, token_half]
    )
    d_query_send_came = core_swap(d_query_send)
    d_one_left, d_one_right, d_query_cross, sums_one = call(
        first_back_kernel,
        info,
        [d_two, d_query_keep, d_query_send_came, normed_one, inverse_one]
        + [vectors, weight_query],
        [token_half, token_half, token_low, ((8, width), f32)],
    )

    local_low = ((tokens, local_width), bf16)
    d_one_all, d_query, d_key, d_value, sums_self = call(
        functools.partial(self_backward_kernel, items),
        info,
        [query_self, key_self, value_self, d_one_left, d_one_right]
        + [core_swap(d_one_left), core_swap(d_one_right), self_out],
        [((tokens, width), bf16), local_low, local_low, local_low, ((8, local_width), f32)],
        scratch=[pltpu.VMEM((tokens, local_width), bf16)],
        name="self_backward",
    )

    self_args = (x_low, d_one_all, d_query, d_key, d_value, heads_self)
    self_one_send, self_two_send = self_grad(
        info, lambda s: 1 - s[at_one], lambda s: 3 - s[at_two], *self_args
    )
    self_one_came = swap(self_one_send, "dp", order_one[0])
    self_two_came = swap(self_two_send, "dp", order_two[0])
    last = (self_one_send, self_two_send)

    (small,) = call(
        stack_kernel,
        info,
        [sums_one, sums_two, after(sums_three, *last), pre_sums],
        [((32, width), f32)],
    )
    small_came = core_swap(small)
    self_one_keep, self_two_keep = self_grad(
        info, lambda s: s[at_one], lambda s: 2 + s[at_two], after(x_low, *last), *self_args[1:]
    )
    self_sum = PairSum(
        info, orders, (self_one_keep, self_two_keep), (self_one_came, self_two_came)
    )
    flows_self = [self_sum]
    last = (self_one_keep, self_two_keep)
    (fc_sum.extra,) = call(
        small_kernel, info, [small, after(small_came, *last), sums_self], [((16, width), f32)]
    )
    flows_self = [self_sum]

    chips = mem_size // 2
    shares = ((tokens, chips * local_width), bf16)
    partial, partial_send = call(
        input_part_kernel,
        info,
        [after(d_query, *last), d_key, d_value, weight_self],
        [shares, shares],
    )
    partial_came = core_swap(partial_send)

    if simple:
        q_keep, q_first, q_second, back_keep, back_first, back_second = cross_grad(
            info,
            dp_size,
            shard,
            [(after(first_low, *last), d_query_cross), (cross_heads, d_two_low)],
        )
        cross_parts = [q_keep, core_swap(q_first), core_swap(q_second)]
        cross_parts += [back_keep, core_swap(back_first), core_swap(back_second)]
        last = (q_keep,)
    last = take_turns(flows_fc, *last, partial)
    last = last + take_turns(flows_self, *last)
    if simple:
        rows = dp_size * shard
        d_kv_keep, d_kv_first, d_kv_second = call(
            functools.partial(chip_rows_kernel, dp_size),
            info,
            [d_kv, after(d_kv_came, *last)],
            [((rows, width), bf16), ((rows, half), bf16), ((rows, half), bf16)],
            name="chip_rows",
        )
        cross_parts += [d_kv_keep, core_swap(d_kv_first), core_swap(d_kv_second)]
        cross_send, cross_keep = call(
            functools.partial(cross_rows_kernel, dp_size),
            info,
            cross_parts,
            [((2 * rows, width), bf16)] * 2,
            name="cross_rows",
        )
        cross_sum = BlockSum(info, cross_keep, swap(cross_send, "dp", dp_bits[0]))
        last = last + (cross_send,)
    if chips == 2:
        input_grad, partial_send = call(
            input_sum_kernel,
            info,
            [partial, after(partial_came, *last), d_one_all],
            [((tokens, local_width), f32), local_low],
        )
        input_came = [swap(partial_send, "mem", chip_bits()[0])]
    else:
        partial = add_low(partial, partial_came)
        piece = lambda i: columns(partial, (place // 2 ^ i) * local_width, local_width)
        input_grad = columns(d_one_all, place * local_width, local_width).astype(f32)
        input_grad = input_grad + piece(0).astype(f32)
        input_came = [swap(piece(i), "mem", 2 * i) for i in range(1, chips)]
    flows_side = [cross_sum] if simple else []
    d_mem_far = memory_part(info, items, after(d_far, *last), weight_kv)
    last = take_turns(flows_self + flows_fc, *last, d_mem_far)
    last = last + take_turns(flows_side, *last)
    d_mem_came = None
    while len(fc_sum.back) > 2:
        last = take_turns(flows_self + flows_fc, *last)
    last = take_turns(flows_self, *last, *fc_sum.came) + fc_sum.advance_one(0, *last)
    d_mem_came = core_swap(after(d_mem_far, *last))
    while flows_side and not cross_sum.summed():
        last = last + take_turns(flows_side, *last)
    last = last + take_turns(flows_self, *last)
    last = last + fc_sum.advance_one(1, *last)
    memory_grad = memory_part(info, items, after(d_near, *last), weight_kv, d_mem_came)
    fc_in_grad = fc_sum.whole(0, *last)
    last = last + (memory_grad, fc_in_grad)
    while not self_sum.gathered():
        last = last + take_turns(flows_self, *last)
    input_came = [after(came, *last) for came in input_came]
    for came in input_came:
        input_grad = input_grad + came.astype(f32)
    input_grad = to_low(input_grad).reshape(items, steps, local_width)
    final_came = core_swap(after(final_low, *last))
    block_output = jnp.concatenate(halves(core, final_low, final_came), axis=0)
    block_output = block_output.reshape(items, steps, width)
    if not upright:
        fc_in_grad = fc_in_grad.T
    fc_out_grad = fc_sum.whole(1, *last)
    last = (fc_in_grad, fc_out_grad)
    self_in_grad, self_out_grad = call(
        functools.partial(self_finish_kernel, at_one, at_two),
        info,
        [self_sum.values[0], after(self_sum.came[0], *last)]
        + [self_sum.values[1], self_sum.came[1]],
        [((3, width, local_width), f32), ((local_width, width), f32)],
        name="self_finish",
    )
    self_in_grad = jnp.transpose(self_in_grad, (1, 0, 2))
    rows = fc_sum.extra_sum()
    spot = (lax.axis_index("dp") * mem_size + place) * shard
    owned = columns(rows, spot, shard)
    gains_grad, shifts_grad, out_biases_grad = owned[0:3].T, owned[3:6].T, owned[6:9].T
    cross_bias_grad = owned[9:11].T
    fc_in_bias_grad = rows[11, :hidden_width]
    self_in_bias_grad = rows[12:14, :local_width]
    if simple:
        cross_sum.arrived((after(cross_sum.pending()[0], *last),))
        cross_rows = cross_sum.total()
        q_rows, back_rows, left, right = (
            cross_rows[at * shard : (at + 1) * shard] for at in range(4)
        )
    else:
        d_q = to_low(tn(first_low, d_query_cross))
        d_back = to_low(tn(cross_heads, d_two_low))
        q_rows, back_rows, left, right = general_cross_rows(d_q, d_back, d_kv, shard)
    cross_in_grad = jnp.concatenate(
        [q_rows, left[:, :half], right[:, :half], left[:, half:], right[:, half:]], axis=1
    )
    cross_out_grad = back_rows

    return (
        block_output,
        input_grad,
        memory_grad.reshape(memory.shape),
        self_in_grad,
        self_in_bias_grad,
        self_out_grad,
        cross_in_grad,
        cross_bias_grad,
        cross_out_grad,
        fc_in_grad,
        fc_in_bias_grad,
        fc_out_grad,
        out_biases_grad,
        gains_grad,
        shifts_grad,
    )


def solution(mesh):
    placed = (
        P("dp", None, None),
        P("dp", "mem", None),
        P("dp"),
        P("dp"),
        P(None, None, "mem"),
        P(None, "mem"),
        P("mem", None),
        P("mem", None),
        P("mem", None),
        P("mem", None),
        P(None, "mem"),
        P("mem"),
        P("mem", None),
        P(),
        P(),
        P(),
        P("dp", None, None),
    )
    return jax.shard_map(
        local,
        mesh=mesh,
        in_specs=placed,
        out_specs=(
            P("dp", None, None),
            P("dp", None, "mem"),
            P("dp", "mem", None),
            P(None, None, "mem"),
            P(None, "mem"),
            P("mem", None),
            P(("dp", "mem"), None),
            P(("dp", "mem"), None),
            P(("dp", "mem"), None),
            P(None, "mem"),
            P("mem"),
            P("mem", None),
            P(("dp", "mem"), None),
            P(("dp", "mem"), None),
            P(("dp", "mem"), None),
        ),
        check_vma=False,
    )
```

```python
import functools

import jax
import jax.numpy as jnp
from jax import lax
from jax.experimental import pallas as pl
from jax.experimental.pallas import tpu as pltpu
from jax.sharding import PartitionSpec as P

HEAD_DIM = 64
PAIR = 2 * HEAD_DIM
CORE = 1
SCALE = HEAD_DIM ** (-0.5)
MASKED = -1e30
EPSILON = 1e-05
TILE = 256
MEGA = 1024 * 1024

f32 = jnp.float32
bf16 = jnp.bfloat16


def to_low(values):
    return values.astype(bf16)


def nt(left, right):
    return lax.dot_general(left, right, (((1,), (1,)), ((), ())), preferred_element_type=f32)


def nn(left, right):
    return lax.dot_general(left, right, (((1,), (0,)), ((), ())), preferred_element_type=f32)


def tn(left, right):
    return lax.dot_general(left, right, (((0,), (0,)), ((), ())), preferred_element_type=f32)


def col_sum(values):
    return jnp.sum(values, axis=0, keepdims=True)


def swap(values, axis, bit):
    pairs = [(i, i ^ bit) for i in range(lax.axis_size(axis))]
    return lax.ppermute(values, axis, pairs)


def core_swap(values):
    return swap(values, "mem", CORE)


def bits_of(axis):
    size, bits, bit = lax.axis_size(axis), [], 1
    while bit < size:
        bits.append(bit)
        bit *= 2
    return bits


def chip_bits():
    return bits_of("mem")[1:]


def bit_at(axis, bit):
    return (lax.axis_index(axis) // bit % 2).astype(jnp.int32)


def after(values, *others):
    return lax.optimization_barrier((values,) + others)[0]


def add_low(first, second):
    return to_low(first.astype(f32) + second.astype(f32))


def chip_swap(values):
    bits = chip_bits()
    for bit in bits[:-1]:
        values = add_low(values, swap(values, "mem", bit))
    return values, swap(values, "mem", bits[-1])


def relative(pieces, bits):
    for bit in bits:
        pieces = pieces | {r ^ bit: swap(piece, "mem", bit) for r, piece in pieces.items()}
    return pieces


def whole(shape):
    return pl.BlockSpec(shape, lambda *_: (0,) * len(shape))


HBM = pl.BlockSpec(memory_space=pl.ANY)


def call(
    kernel, info, inputs, outputs, scratch=(), grid=(1,), out_specs=None, mega=8, cost=0.0, name=None
):
    arrays = [given[0] if isinstance(given, tuple) else given for given in inputs]
    specs = [given[1] if isinstance(given, tuple) else whole(given.shape) for given in inputs]
    return pl.pallas_call(
        kernel,
        out_shape=[jax.ShapeDtypeStruct(*out) for out in outputs],
        grid_spec=pltpu.PrefetchScalarGridSpec(
            num_scalar_prefetch=1,
            grid=grid,
            in_specs=specs,
            out_specs=out_specs or [whole(out[0]) for out in outputs],
            scratch_shapes=list(scratch),
        ),
        compiler_params=pltpu.CompilerParams(vmem_limit_bytes=mega * MEGA),
        cost_estimate=pl.CostEstimate(
            flops=1 + int(cost * 1.1e9), bytes_accessed=1, transcendentals=0
        ),
        name=name or kernel.__name__,
    )(info, *arrays)


def dp_position(bit):
    return DP_AT + bit.bit_length() - 1


def norm_parts(resid):
    centre = resid - jnp.mean(resid, axis=-1, keepdims=True)
    inverse = lax.rsqrt(jnp.mean(centre * centre, axis=-1, keepdims=True) + EPSILON)
    return (centre * inverse, inverse)


def norm_back(normed, inverse, gain, upstream):
    scaled = upstream * gain
    return inverse * (
        scaled
        - jnp.mean(scaled, axis=-1, keepdims=True)
        - normed * jnp.mean(scaled * normed, axis=-1, keepdims=True)
    )


def row(ref, at):
    return ref[at : at + 1, :]


def wide(ref):
    return ref[...].astype(f32)


def halves(core, mine, theirs):
    first = core == 0
    return jnp.where(first, mine, theirs), jnp.where(first, theirs, mine)


def dyn(start, size, unit=16):
    return pl.ds(pl.multiple_of(start, unit), size)


PLACE, CORE_AT, DP_AT, LENS = 0, 1, 3, 8
GAIN, SHIFT, BIAS = 0, 3, 6


def assemble_kernel(ids, parts, s_ref, *refs):
    sources, outs, sem = refs[: len(ids)], refs[len(ids) : -1], refs[-1]
    rows = sources[0].shape[0]
    copies = []
    for source, r in zip(sources, ids):
        at = dyn((s_ref[PLACE] ^ r) * rows, rows)
        for out, start, step, to, width in parts:
            columns = pl.ds(pl.multiple_of(start + s_ref[CORE_AT] * step, 128), width)
            copies.append(
                pltpu.make_async_copy(
                    source.at[:, columns],
                    outs[out].at[at, pl.ds(to, width)],
                    sem.at[len(copies)],
                )
            )
    for copy in copies:
        copy.start()
    for copy in copies:
        copy.wait()


def assemble(info, pieces, parts, outputs, name):
    return call(
        functools.partial(assemble_kernel, tuple(pieces), parts),
        info,
        [(piece, HBM) for piece in pieces.values()],
        outputs,
        scratch=[pltpu.SemaphoreType.DMA((len(pieces) * len(parts),))],
        out_specs=[HBM] * len(outputs),
        name=name,
    )


def first_norm_kernel(
    s_ref,
    x_ref,
    mine_ref,
    came_ref,
    vec_ref,
    shift_ref,
    wq_ref,
    normed_ref,
    inv_ref,
    low_ref,
    keep_ref,
    send_ref,
):
    resid = wide(x_ref) + (wide(mine_ref) + wide(came_ref)) + row(vec_ref, BIAS)
    normed, inverse = norm_parts(resid)
    normed_ref[...] = normed
    inv_ref[...] = inverse
    low = to_low(normed * row(vec_ref, GAIN) + row(vec_ref, SHIFT))
    low_ref[...] = low
    half = keep_ref.shape[1]
    left, right = (
        to_low(nn(low, wq_ref[:, part]) + shift_ref[:, part])
        for part in (slice(0, half), slice(half, 2 * half))
    )
    keep_ref[...], send_ref[...] = halves(s_ref[CORE_AT], left, right)


def middle_kernel(
    s_ref,
    normed_ref,
    mine_ref,
    came_ref,
    vec_ref,
    bias_ref,
    bias_far_ref,
    back_hbm,
    in_hbm,
    in_far_hbm,
    out_hbm,
    out_far_hbm,
    heads_ref,
    normed_two_ref,
    inv_ref,
    low_ref,
    hidden_ref,
    hidden_far_ref,
    slope_ref,
    slope_far_ref,
    fed_ref,
    back,
    w_in,
    w_in_far,
    w_out,
    w_out_far,
    sem,
):
    loads = []
    for i, (source, target) in enumerate(
        (
            (back_hbm, back),
            (in_hbm, w_in),
            (in_far_hbm, w_in_far),
            (out_hbm, w_out),
            (out_far_hbm, w_out_far),
        )
    ):
        loads.append(pltpu.make_async_copy(source, target, sem.at[i]))
        loads[i].start()
    heads = jnp.concatenate(halves(s_ref[CORE_AT], mine_ref[...], came_ref[...]), axis=1)
    heads_ref[...] = heads
    first = normed_ref[...] * row(vec_ref, GAIN) + row(vec_ref, SHIFT)
    loads[0].wait()
    normed, inverse = norm_parts(first + nn(heads, back[...]) + row(vec_ref, BIAS + 1))
    normed_two_ref[...] = normed
    inv_ref[...] = inverse
    low = to_low(normed * row(vec_ref, GAIN + 1) + row(vec_ref, SHIFT + 1))
    low_ref[...] = low
    for i, (weight, shift, hidden, slope) in enumerate(
        ((w_in, bias_ref, hidden_ref, slope_ref), (w_in_far, bias_far_ref, hidden_far_ref, slope_far_ref))
    ):
        loads[1 + i].wait()
        for at in range(0, weight.shape[1], TILE):
            part = slice(at, at + TILE)
            pre = nn(low, weight[:, part]) + shift[:, part]
            share = 0.5 * (1.0 + lax.erf(pre * (0.5**0.5)))
            hidden[:, part] = to_low(pre * share)
            density = jnp.exp(-0.5 * pre * pre) * (1.0 / (2.0 * jnp.pi) ** 0.5)
            slope[:, part] = to_low(share + pre * density)
    loads[3].wait()
    loads[4].wait()
    for at in range(0, fed_ref.shape[1], TILE):
        part = slice(at, at + TILE)
        fed_ref[:, part] = to_low(
            nn(hidden_ref[...], w_out[:, part]) + nn(hidden_far_ref[...], w_out_far[:, part])
        )


def turn_kernel(
    s_ref,
    normed_two_ref,
    mine_ref,
    came_ref,
    vec_ref,
    grad_ref,
    slope_ref,
    slope_far_ref,
    in_hbm,
    in_far_hbm,
    out_hbm,
    out_far_hbm,
    final_ref,
    d_ref,
    d_low_ref,
    pre_ref,
    pre_far_ref,
    part_ref,
    sums_ref,
    pre_sums_ref,
    w_in,
    w_in_far,
    w_out,
    w_out_far,
    sem,
):
    loads = []
    for i, (source, target) in enumerate(
        ((out_hbm, w_out), (out_far_hbm, w_out_far), (in_hbm, w_in), (in_far_hbm, w_in_far))
    ):
        loads.append(pltpu.make_async_copy(source, target, sem.at[i]))
        loads[i].start()
    second = normed_two_ref[...] * row(vec_ref, GAIN + 1) + row(vec_ref, SHIFT + 1)
    resid = second + (wide(mine_ref) + wide(came_ref)) + row(vec_ref, BIAS + 2)
    normed, inverse = norm_parts(resid)
    gain = row(vec_ref, GAIN + 2)
    final_ref[...] = to_low(normed * gain + row(vec_ref, SHIFT + 2))
    upstream = wide(grad_ref)
    d_resid = norm_back(normed, inverse, gain, upstream)
    d_ref[...] = d_resid
    d_low = to_low(d_resid)
    d_low_ref[...] = d_low
    sums_ref[...] = jnp.zeros_like(sums_ref)
    sums_ref[0:1, :] = col_sum(upstream * normed)
    sums_ref[1:2, :] = col_sum(upstream)
    sums_ref[2:3, :] = col_sum(d_resid)
    pre_sums_ref[...] = jnp.zeros_like(pre_sums_ref)
    for i, (weight, slope, pre) in enumerate(
        ((w_out, slope_ref, pre_ref), (w_out_far, slope_far_ref, pre_far_ref))
    ):
        loads[i].wait()
        for at in range(0, weight.shape[0], TILE):
            part = slice(at, at + TILE)
            d_pre = to_low(nt(d_low, weight[part, :]) * slope[:, part].astype(f32))
            pre[:, part] = d_pre
            pre_sums_ref[i : i + 1, part] = col_sum(d_pre.astype(f32))
    loads[2].wait()
    loads[3].wait()
    for at in range(0, part_ref.shape[1], TILE):
        part = slice(at, at + TILE)
        part_ref[:, part] = to_low(
            nt(pre_ref[...], w_in[part, :]) + nt(pre_far_ref[...], w_in_far[part, :])
        )


def second_back_kernel(
    s_ref,
    d_three_ref,
    mine_ref,
    came_ref,
    normed_ref,
    inv_ref,
    vec_ref,
    back_ref,
    d_ref,
    d_low_ref,
    keep_ref,
    send_ref,
    sums_ref,
):
    upstream = d_three_ref[...] + (wide(mine_ref) + wide(came_ref))
    normed = normed_ref[...]
    d_resid = norm_back(normed, inv_ref[...], row(vec_ref, GAIN + 1), upstream)
    d_ref[...] = d_resid
    d_low = to_low(d_resid)
    d_low_ref[...] = d_low
    half = keep_ref.shape[1]
    left = to_low(nt(d_low, back_ref[:half, :]))
    right = to_low(nt(d_low, back_ref[half:, :]))
    keep_ref[...], send_ref[...] = halves(s_ref[CORE_AT], left, right)
    sums_ref[...] = jnp.zeros_like(sums_ref)
    sums_ref[0:1, :] = col_sum(upstream * normed)
    sums_ref[1:2, :] = col_sum(upstream)
    sums_ref[2:3, :] = col_sum(d_resid)
    sums_ref[3:4, :half] = col_sum(left.astype(f32))
    sums_ref[3:4, half:] = col_sum(right.astype(f32))


def split_sum_kernel(s_ref, mine_ref, came_ref, keep_ref, send_ref):
    rows = keep_ref.shape[0]
    for out, core in ((send_ref, 1 - s_ref[CORE_AT]), (keep_ref, s_ref[CORE_AT])):
        part = dyn(core * rows, rows)
        out[...] = add_low(mine_ref[part, :], came_ref[part, :])


def first_back_kernel(
    s_ref,
    d_two_ref,
    mine_ref,
    came_ref,
    normed_ref,
    inv_ref,
    vec_ref,
    wq_ref,
    left_ref,
    right_ref,
    query_ref,
    sums_ref,
):
    d_query = jnp.concatenate(halves(s_ref[CORE_AT], mine_ref[...], came_ref[...]), axis=1)
    query_ref[...] = d_query
    upstream = d_two_ref[...] + nt(d_query, wq_ref[...])
    normed = normed_ref[...]
    d_resid = norm_back(normed, inv_ref[...], row(vec_ref, GAIN), upstream)
    half = left_ref.shape[1]
    left_ref[...] = to_low(d_resid[:, :half])
    right_ref[...] = to_low(d_resid[:, half:])
    sums_ref[...] = jnp.zeros_like(sums_ref)
    sums_ref[0:1, :] = col_sum(upstream * normed)
    sums_ref[1:2, :] = col_sum(upstream)
    sums_ref[2:3, :] = col_sum(d_resid)
    sums_ref[3:4, :] = col_sum(d_query.astype(f32))


def stacked(block, first_head):
    zero = jnp.zeros_like(block)
    return jnp.concatenate(
        [jnp.where(first_head, block, zero), jnp.where(first_head, zero, block)], axis=0
    )


def unstacked(both, first_head):
    rows = both.shape[0] // 2
    return jnp.where(first_head, both[:rows], both[rows:])


def first_lanes(rows):
    return lax.broadcasted_iota(jnp.int32, (rows, PAIR), 1) < HEAD_DIM


def row_sums(values):
    lanes = lax.broadcasted_iota(jnp.int32, (16, PAIR), 1)
    which = lax.broadcasted_iota(jnp.int32, (16, PAIR), 0)
    pick = to_low((lanes // HEAD_DIM == which).astype(f32))
    high = to_low(values)
    low = to_low(values - high.astype(f32))
    sums = nt(pick, high) + nt(pick, low)
    return jnp.concatenate([sums[0:1], sums[1:2]], axis=1)


def shown(length, place, rows):
    spot = lax.broadcasted_iota(jnp.int32, (rows, 1), 0)
    return jnp.concatenate(
        [place * rows + spot < length, (place ^ CORE) * rows + spot < length], axis=0
    )


def join_rows(core, mine_ref, came_ref, both):
    rows = mine_ref.shape[0]
    both[dyn(core * rows, rows), :] = mine_ref[...]
    both[dyn((1 - core) * rows, rows), :] = came_ref[...]


def cross_forward_kernel(s_ref, mine_ref, came_ref, near_ref, far_ref, o_ref, stat_ref, both):
    item = pl.program_id(0)

    @pl.when(item == 0)
    def _():
        join_rows(s_ref[CORE_AT], mine_ref, came_ref, both)

    steps, width = o_ref.shape
    rows = dyn(item * steps, steps)
    visible = shown(s_ref[LENS + item], s_ref[PLACE], near_ref.shape[0])
    first_head = first_lanes(steps)
    for pair in range(width // PAIR):
        lanes = slice(pair * PAIR, (pair + 1) * PAIR)
        values = slice(width + pair * PAIR, width + (pair + 1) * PAIR)
        query = stacked(both[rows, lanes] * SCALE, first_head)
        key = jnp.concatenate([near_ref[:, lanes], far_ref[:, lanes]], axis=0)
        value = jnp.concatenate([near_ref[:, values], far_ref[:, values]], axis=0)
        scores = jnp.where(visible, nt(key, query), MASKED)
        top = jnp.max(scores, axis=0, keepdims=True)
        grown = jnp.exp(scores - top)
        total = jnp.sum(grown, axis=0, keepdims=True)
        weights = to_low(grown * (1.0 / total))
        o_ref[:, lanes] = to_low(unstacked(tn(weights, value), first_head))
        stat = top + jnp.log(total)
        stat_ref[0, 2 * pair : 2 * pair + 1, :] = stat[:, :steps]
        stat_ref[0, 2 * pair + 1 : 2 * pair + 2, :] = stat[:, steps:]


def cross_forward(info, items, mine, came, near, far):
    width, tokens = mine.shape[1], 2 * mine.shape[0]
    rows, steps = near.shape[0] // items, tokens // items
    heads = width // HEAD_DIM
    keys = pl.BlockSpec((rows, 2 * width), lambda i, *_: (i, 0))
    return call(
        cross_forward_kernel,
        info,
        [mine, came, (near, keys), (far, keys)],
        [((tokens, width), bf16), ((items, heads, steps), f32)],
        scratch=[pltpu.VMEM((tokens, width), bf16)],
        grid=(items,),
        mega=14,
        out_specs=[
            pl.BlockSpec((steps, width), lambda i, *_: (i, 0)),
            pl.BlockSpec((1, heads, steps), lambda i, *_: (i, 0, 0)),
        ],
    )


def merge_kernel(bit, s_ref, a_ref, sa_ref, b_ref, sb_ref, o_ref, stat_ref):
    flip = (s_ref[PLACE] & bit) != 0
    items, heads, steps = sa_ref.shape
    width = a_ref.shape[1]
    pick = lax.broadcasted_iota(jnp.int32, (heads, width), 1) // HEAD_DIM
    pick = to_low((pick == lax.broadcasted_iota(jnp.int32, (heads, width), 0)).astype(f32))

    def spread(share):
        high = to_low(share)
        return tn(high, pick) + tn(to_low(share - high.astype(f32)), pick)

    for item in range(items):
        rows = slice(item * steps, (item + 1) * steps)
        mine, theirs = sa_ref[item], sb_ref[item]
        first, second = jnp.where(flip, theirs, mine), jnp.where(flip, mine, theirs)
        top = jnp.maximum(first, second)
        grown_first, grown_second = jnp.exp(first - top), jnp.exp(second - top)
        total = grown_first + grown_second
        stat_ref[item] = top + jnp.log(total)
        low_values = jnp.where(flip, b_ref[rows, :], a_ref[rows, :]).astype(f32)
        high_values = jnp.where(flip, a_ref[rows, :], b_ref[rows, :]).astype(f32)
        o_ref[rows, :] = to_low(
            spread(grown_first / total) * low_values + spread(grown_second / total) * high_values
        )


def merge(info, bit, mine, stat_mine, theirs, stat_theirs):
    return call(
        functools.partial(merge_kernel, bit),
        info,
        [mine, stat_mine, theirs, stat_theirs],
        [(mine.shape, bf16), (stat_mine.shape, f32)],
        name="merge",
    )


def cross_backward_kernel(
    s_ref, q_ref, q_came_ref, do_mine_ref, do_came_ref, o_ref, stat_ref, near_ref, far_ref,
    dq_ref, dnear_ref, dfar_ref, q_both, do_both,
):
    item = pl.program_id(0)

    @pl.when(item == 0)
    def _():
        join_rows(s_ref[CORE_AT], q_ref, q_came_ref, q_both)
        join_rows(s_ref[CORE_AT], do_mine_ref, do_came_ref, do_both)

    steps, width = dq_ref.shape
    rows = near_ref.shape[0]
    tokens = dyn(item * steps, steps)
    visible = shown(s_ref[LENS + item], s_ref[PLACE], rows)
    first_head = first_lanes(steps)
    for pair in range(width // PAIR):
        lanes = slice(pair * PAIR, (pair + 1) * PAIR)
        values = slice(width + pair * PAIR, width + (pair + 1) * PAIR)
        d_out = do_both[tokens, lanes]
        dots = row_sums(d_out.astype(f32) * o_ref[:, lanes].astype(f32))
        stat = jnp.concatenate(
            [stat_ref[0, 2 * pair : 2 * pair + 1, :], stat_ref[0, 2 * pair + 1 : 2 * pair + 2, :]],
            axis=1,
        )
        query = stacked(q_both[tokens, lanes] * SCALE, first_head)
        d_both = stacked(d_out, first_head)
        key = jnp.concatenate([near_ref[:, lanes], far_ref[:, lanes]], axis=0)
        value = jnp.concatenate([near_ref[:, values], far_ref[:, values]], axis=0)
        scores = jnp.where(visible, nt(key, query), MASKED)
        probs = jnp.exp(scores - stat)
        d_scores = to_low(probs * (nt(value, d_both) - dots))
        d_value = to_low(nn(to_low(probs), d_both))
        d_key = to_low(nn(d_scores, query))
        dnear_ref[:, lanes] = d_key[:rows]
        dfar_ref[:, lanes] = d_key[rows:]
        dnear_ref[:, values] = d_value[:rows]
        dfar_ref[:, values] = d_value[rows:]
        dq_ref[:, lanes] = to_low(unstacked(tn(d_scores, key), first_head) * SCALE)


def cross_backward(info, queries, d_outs, out, stat, near, far):
    items, heads, steps = stat.shape
    tokens, width = out.shape
    rows = near.shape[0] // items
    keys = pl.BlockSpec((rows, 2 * width), lambda i, *_: (i, 0))
    block = pl.BlockSpec((steps, width), lambda i, *_: (i, 0))
    return call(
        cross_backward_kernel,
        info,
        list(queries)
        + list(d_outs)
        + [
            (out, block),
            (stat, pl.BlockSpec((1, heads, steps), lambda i, *_: (i, 0, 0))),
            (near, keys),
            (far, keys),
        ],
        [(out.shape, bf16), (near.shape, bf16), (far.shape, bf16)],
        scratch=[pltpu.VMEM((tokens, width), bf16)] * 2,
        grid=(items,),
        mega=14,
        out_specs=[block, keys, keys],
    )


def self_weights(query_block, key_block, first_head, allowed):
    query = stacked(query_block * SCALE, first_head)
    scores = jnp.where(allowed, nt(key_block, query), MASKED)
    top = jnp.max(scores, axis=0, keepdims=True)
    grown = jnp.exp(scores - top)
    total = jnp.sum(grown, axis=0, keepdims=True)
    return query, grown * (1.0 / total)


def self_parts(len_ref, items, tokens, width):
    steps = tokens // items
    keys = lax.broadcasted_iota(jnp.int32, (steps, 2 * steps), 0)
    queries = lax.broadcasted_iota(jnp.int32, (steps, 2 * steps), 1) % steps
    causal = keys <= queries
    for item in range(items):
        allowed = jnp.logical_and(causal, keys < len_ref[LENS + items + item])
        for pair in range(width // PAIR):
            yield (
                slice(item * steps, (item + 1) * steps),
                slice(pair * PAIR, (pair + 1) * PAIR),
                allowed,
            )


def self_forward_kernel(items, len_ref, q_ref, k_ref, v_ref, o_ref):
    tokens, width = q_ref.shape
    first_head = first_lanes(tokens // items)
    for rows, lanes, allowed in self_parts(len_ref, items, tokens, width):
        _, probs = self_weights(q_ref[rows, lanes], k_ref[rows, lanes], first_head, allowed)
        o_ref[rows, lanes] = to_low(unstacked(tn(to_low(probs), v_ref[rows, lanes]), first_head))


def self_backward_kernel(
    items, s_ref, q_ref, k_ref, v_ref, left_ref, right_ref, left_came, right_came, out_ref,
    d_low_ref, dq_ref, dk_ref, dv_ref, sums_ref, do_both,
):
    tokens, width = q_ref.shape
    half = left_ref.shape[1]
    for at, mine, came in ((0, left_ref, left_came), (half, right_ref, right_came)):
        part = slice(at, at + half)
        rows = mine.shape[0]
        d_low_ref[dyn(s_ref[CORE_AT] * rows, rows), part] = mine[...]
        d_low_ref[dyn((1 - s_ref[CORE_AT]) * rows, rows), part] = came[...]
    do_both[...] = to_low(nt(d_low_ref[...], out_ref[...]))
    first_head = first_lanes(tokens // items)
    for rows, lanes, allowed in self_parts(s_ref, items, tokens, width):
        key = k_ref[rows, lanes]
        query, probs = self_weights(q_ref[rows, lanes], key, first_head, allowed)
        d_both = stacked(do_both[rows, lanes], first_head)
        d_probs = nt(v_ref[rows, lanes], d_both)
        dots = jnp.sum(probs * d_probs, axis=0, keepdims=True)
        d_scores = to_low(probs * (d_probs - dots))
        dv_ref[rows, lanes] = to_low(nn(to_low(probs), d_both))
        dk_ref[rows, lanes] = to_low(nn(d_scores, query))
        dq_ref[rows, lanes] = to_low(unstacked(tn(d_scores, key), first_head) * SCALE)
    sums_ref[...] = jnp.zeros_like(sums_ref)
    sums_ref[0:1, :] = col_sum(dq_ref[...].astype(f32))
    sums_ref[1:2, :] = col_sum(do_both[...].astype(f32))


def grad_half_kernel(count, s_ref, *refs):
    for at in range(0, refs[-1].shape[1], TILE):
        part = slice(at, at + TILE)
        total = tn(refs[0][...], refs[count][:, part])
        for i in range(1, count):
            total = total + tn(refs[i][...], refs[count + i][:, part])
        refs[-1][:, part] = to_low(total)


def grad_half(info, index, lefts, rights):
    rows, columns = lefts[0].shape[1] // 2, rights[0].shape[1]
    spec = lambda left: pl.BlockSpec((left.shape[0], rows), lambda i, s: (0, index(s)))
    return call(
        functools.partial(grad_half_kernel, len(lefts)),
        info,
        [(left, spec(left)) for left in lefts] + list(rights),
        [((rows, columns), bf16)],
        cost=5.0,
        name="grad_half",
    )[0]


def self_grad_kernel(s_ref, x0_ref, x1_ref, d0_ref, d1_ref, q_ref, k_ref, v_ref, h_ref, *outs):
    width = q_ref.shape[1]
    for x_ref, d_ref, out in ((x0_ref, d0_ref, outs[0]), (x1_ref, d1_ref, outs[1])):
        for i, ref in enumerate((q_ref, k_ref, v_ref)):
            out[:, i * width : (i + 1) * width] = to_low(tn(x_ref[...], ref[...]))
        out[:, 3 * width :] = to_low(tn(d_ref[...], h_ref[...]))


def self_grad(info, first, second, x, d_low, query, key, value, heads):
    rows, tokens, width = x.shape[1] // 4, x.shape[0], query.shape[1]
    at = lambda index: pl.BlockSpec((tokens, rows), lambda i, s: (0, index(s)))
    return call(
        self_grad_kernel,
        info,
        [(x, at(first)), (x, at(second)), (d_low, at(first)), (d_low, at(second)), query, key, value, heads],
        [((rows, 4 * width), bf16)] * 2,
    )


def put_wide(out, at, values):
    rows = values.shape[0]
    high = to_low(values)
    out[at : at + rows, :] = high
    out[at + rows : at + 2 * rows, :] = to_low(values - high.astype(f32))


def get_wide(ref, at, rows):
    return ref[at : at + rows, :].astype(f32) + ref[at + rows : at + 2 * rows, :].astype(f32)


def split_kernel(positions, joint, s_ref, *refs):
    count = len(positions)
    mine, came, outs = refs[:count], refs[count : 2 * count], refs[2 * count :]
    sends, keeps = outs[:-count], outs[-count:]
    rows = keeps[0].shape[0]
    for k, position in enumerate(positions):
        base = 2 * rows * k if joint[0] else 0
        for send in (True, False):
            half = 1 - s_ref[position] if send else s_ref[position]
            total = add_low(
                mine[k][dyn(half * rows, rows), :], came[k][dyn(base + half * rows, rows), :]
            )
            if not send:
                keeps[k][...] = total
            elif joint[1]:
                sends[0][k * rows : (k + 1) * rows, :] = total
            else:
                sends[k][...] = total


def split(info, bits, mine, came, joint):
    rows, columns = mine[0].shape[0] // 2, mine[0].shape[1]
    sends = [2 * rows] if joint[1] else [rows] * len(bits)
    return call(
        functools.partial(split_kernel, [dp_position(bit) for bit in bits], joint),
        info,
        list(mine) + list(came),
        [((size, columns), bf16) for size in sends + [rows] * len(bits)],
        name="split_sums",
    )


def total_kernel(joint, extra, s_ref, *refs):
    mine, came, outs = refs[:2], refs[2:4], refs[4 + extra :]
    rows = mine[0].shape[0]
    for k in range(2):
        base = rows * k if joint[0] else 0
        total = add_low(mine[k][...], came[k][base : base + rows, :])
        if joint[1]:
            outs[0][k * rows : (k + 1) * rows, :] = total
        else:
            outs[k][...] = total
    if extra:
        put_wide(outs[0], 2 * rows, refs[4][...])


def total_pair(info, mine, came, joint, extra=None):
    rows, columns = mine[0].shape
    extras = [] if extra is None else [extra]
    more = 2 * sum(v.shape[0] for v in extras)
    outputs = [2 * rows + more] if joint[1] else [rows, rows]
    return call(
        functools.partial(total_kernel, joint, len(extras)),
        info,
        list(mine) + list(came) + extras,
        [((size, columns), bf16) for size in outputs],
        name="total_sums",
    )


def join_pair_kernel(positions, given, extra, s_ref, *refs):
    mine, came, outs = refs[:given], refs[given : 2 * given], refs[2 * given :]
    joint = given < len(positions)
    rows = mine[0].shape[0] - 2 * extra
    rows = rows // 2 if joint else rows
    for k, position in enumerate(positions):
        part = slice(k * rows, (k + 1) * rows) if joint else slice(0, rows)
        own, other = mine[k % given][part, :], came[k % given][part, :]
        base = 2 * rows * k if len(outs) < len(positions) else 0
        out = outs[k % len(outs)]
        out[dyn(base + s_ref[position] * rows, rows), :] = own
        out[dyn(base + (1 - s_ref[position]) * rows, rows), :] = other
    if extra:
        at = mine[0].shape[0] - 2 * extra
        total = get_wide(mine[0], at, extra) + get_wide(came[0], at, extra)
        put_wide(outs[0], outs[0].shape[0] - 2 * extra, total)


def join_pair(info, bits, mine, came, joint, extra=0, cost=8.0):
    given, columns = len(mine), mine[0].shape[1]
    rows = mine[0].shape[0] - 2 * extra
    rows = (rows if given == len(bits) else rows // 2) * 2
    more = 2 * extra
    outputs = [len(bits) * rows + more] if joint else [rows + more] + [rows] * (len(bits) - 1)
    return call(
        functools.partial(
            join_pair_kernel, [dp_position(bit) for bit in bits], given, extra
        ),
        info,
        list(mine) + list(came),
        [((size, columns), bf16) for size in outputs],
        cost=cost,
        name="join_pair",
    )


def join_kernel(position, s_ref, mine_ref, came_ref, out_ref):
    @pl.when(pl.program_id(1) == s_ref[position])
    def _():
        out_ref[...] = mine_ref[...].astype(out_ref.dtype)

    @pl.when(pl.program_id(1) != s_ref[position])
    def _():
        out_ref[...] = came_ref[...].astype(out_ref.dtype)


def join(info, bit, mine, came, rows):
    columns = mine.shape[1]
    spec = pl.BlockSpec((rows, columns), lambda i, j, s: (0, 0))
    return call(
        functools.partial(join_kernel, dp_position(bit)),
        info,
        [(mine, spec), (came, spec)],
        [((2 * rows, columns), f32)],
        grid=(1, 2),
        out_specs=[pl.BlockSpec((rows, columns), lambda i, j, s: (j, 0))],
        name="join",
    )[0]


class PairSum:
    def __init__(self, info, orders, keeps, cames):
        self.info, self.step = info, 1
        self.bits = list(zip(*orders))
        self.back = self.bits[::-1]
        self.mine, self.came, self.extra = tuple(keeps), tuple(cames), None
        self.joint, self.gathering = False, False

    def pending(self):
        return self.came

    def arrived(self, came):
        self.came = came

    def exchange(self, values, bits):
        if len(values) == 1:
            self.came = (swap(values[0], "dp", bits[0]),)
        else:
            self.came = tuple(swap(value, "dp", bit) for value, bit in zip(values, bits))

    def advance(self):
        same = lambda bits: bits[0] == bits[1]
        came = self.came if len(self.came) == 2 else self.came * 2
        if self.step < len(self.bits):
            bits = self.bits[self.step]
            joint = (self.joint, same(bits))
            result = split(self.info, bits, self.mine, came, joint)
            sent, self.mine, self.joint = tuple(result[:-2]), tuple(result[-2:]), joint[1]
            self.step += 1
            self.exchange(sent, bits)
            return sent
        if not self.gathering:
            joint = (self.joint, same(self.back[0]))
            self.values = total_pair(self.info, self.mine, came, joint, self.extra)
            self.gathering = True
        else:
            bits = self.back.pop(0)
            extra = 0 if self.extra is None else self.extra.shape[0]
            joint = same(self.back[0])
            self.values = tuple(
                join_pair(
                    self.info,
                    bits,
                    self.values,
                    self.came,
                    joint,
                    extra,
                    0.0 if len(self.back) == 1 else 8.0,
                )
            )
        self.exchange(self.values, self.back[0])
        return tuple(self.values)

    def advance_one(self, k, *points):
        bit, last = self.back[0][k], self.back[1][k]
        extra = 0 if k or self.extra is None else self.extra.shape[0]
        mine, came = self.values[k], after(self.came[k], *points) if points else self.came[k]
        cost = 8.0 if k else 8.0
        (values,) = join_pair(self.info, [bit], [mine], [came], False, extra, cost)
        self.values = self.values[:k] + (values,) + self.values[k + 1 :]
        self.came = self.came[:k] + (swap(values, "dp", last),) + self.came[k + 1 :]
        if k:
            self.back.pop(0)
        return (values,)

    def gathered(self):
        return self.gathering and len(self.back) == 1

    def whole(self, k, *points):
        self.came = self.came[:k] + (after(self.came[k], *points),) + self.came[k + 1 :]
        rows = self.values[1].shape[0]
        return join(self.info, self.back[0][k], self.values[k], self.came[k], rows)

    def extra_sum(self):
        extra = self.extra.shape[0]
        at = self.values[0].shape[0] - 2 * extra
        total = self.values[0][at:].astype(f32) + self.came[0][at:].astype(f32)
        return total[:extra] + total[extra:]


class BlockSum:
    def __init__(self, info, keep, came):
        self.info, self.order = info, bits_of("dp")[1:]
        self.mine, self.came = keep, (came,)

    def pending(self):
        return self.came

    def arrived(self, came):
        self.came = came

    def summed(self):
        return not self.order

    def advance(self):
        bit = self.order.pop(0)
        sent, self.mine = split(self.info, [bit], [self.mine], self.came, (False, False))
        self.came = (swap(sent, "dp", bit),)
        return (sent,)

    def total(self):
        return self.mine.astype(f32) + self.came[0].astype(f32)


def take_turns(flows, *points):
    if not flows:
        return ()
    came = lax.optimization_barrier((tuple(flow.pending() for flow in flows), points))[0]
    for flow, values in zip(flows, came):
        flow.arrived(values)
    return sum((flow.advance() for flow in flows), ())


def self_finish_kernel(first, second, s_ref, upper_ref, upper_came_ref, lower_ref, lower_came_ref, in_ref, out_ref):
    rows, width = upper_ref.shape[0], in_ref.shape[2]
    blocks = halves(s_ref[first], upper_ref[...], upper_came_ref[...])
    blocks = blocks + halves(s_ref[second], lower_ref[...], lower_came_ref[...])
    for at, block in enumerate(blocks):
        block = block.astype(f32)
        part = slice(at * rows, (at + 1) * rows)
        for i in range(3):
            in_ref[i, part, :] = block[:, i * width : (i + 1) * width]
        out_ref[:, part] = block[:, 3 * width :].T


def second_order(bits):
    return bits[1:2] + bits[:1] + bits[2:]


def spot_of(block, blocks):
    order = [1 << i for i in range(blocks.bit_length() - 1)]
    return sum((block // bit % 2) << (len(order) - 1 - i) for i, bit in enumerate(order))


def cross_grad_kernel(blocks, s_ref, *refs):
    scratch = refs[10]
    for k in range(2):
        left, right = refs[2 * k], refs[2 * k + 1]
        keep, first, second = refs[4 + 3 * k : 7 + 3 * k]
        rows, half = keep.shape[0] // blocks, first.shape[1]
        for at in range(0, right.shape[1], TILE):
            part = slice(at, at + TILE)
            scratch[...] = to_low(tn(left[...], right[:, part]))
            size = scratch.shape[0] // blocks
            send, column = (first, at) if at < half else (second, at - half)
            sent = slice(column, column + TILE)
            for block in range(blocks):
                turned = spot_of(block, blocks)
                to = slice(turned * rows, (turned + 1) * rows)
                own = dyn(block * size + s_ref[PLACE] * rows, rows)
                other = dyn(block * size + (s_ref[PLACE] ^ CORE) * rows, rows)
                keep[to, part] = scratch[own, :]
                send[to, sent] = scratch[other, :]


def cross_grad(info, blocks, shard, pairs):
    width = pairs[0][0].shape[1]
    rows = blocks * shard
    outputs = [((rows, width), bf16), ((rows, width // 2), bf16), ((rows, width // 2), bf16)]
    return call(
        functools.partial(cross_grad_kernel, blocks),
        info,
        [array for pair in pairs for array in pair],
        outputs * 2,
        scratch=[pltpu.VMEM((width, TILE), bf16)],
        name="cross_grad",
    )


def input_part_kernel(s_ref, q_ref, k_ref, v_ref, weight_ref, keep_ref, send_ref):
    width = q_ref.shape[1]
    for out, core in ((send_ref, 1 - s_ref[CORE_AT]), (keep_ref, s_ref[CORE_AT])):
        for i in range(out.shape[1] // width):
            rows = dyn((2 * i + core) * width, width)
            total = nt(q_ref[...], weight_ref[0, rows, :])
            total = total + nt(k_ref[...], weight_ref[1, rows, :])
            total = total + nt(v_ref[...], weight_ref[2, rows, :])
            out[:, i * width : (i + 1) * width] = to_low(total)


def input_sum_kernel(s_ref, mine_ref, came_ref, d_ref, keep_ref, send_ref):
    width = keep_ref.shape[1]
    chip = s_ref[PLACE] // 2
    other = dyn((1 - chip) * width, width, 128)
    send_ref[...] = add_low(mine_ref[:, other], came_ref[:, other])
    own = dyn(chip * width, width, 128)
    keep_ref[...] = (
        mine_ref[:, own].astype(f32)
        + came_ref[:, own].astype(f32)
        + d_ref[:, dyn(s_ref[PLACE] * width, width, 128)].astype(f32)
    )


def memory_kernel(s_ref, d_ref, weight_ref, *refs):
    total = nt(d_ref[...], weight_ref[...])
    if len(refs) == 2:
        total = total + wide(refs[0])
    refs[-1][...] = to_low(total)


def memory_part(info, items, d_ref, weight, *came):
    rows = pl.BlockSpec((d_ref.shape[0] // items, d_ref.shape[1]), lambda i, s: (i, 0))
    return call(
        memory_kernel,
        info,
        [(d_ref, rows), weight] + [(array, rows) for array in came],
        [(d_ref.shape, bf16)],
        grid=(items,),
        out_specs=[rows],
        mega=12,
        name="memory_grad",
    )[0]


def stack_kernel(s_ref, one_ref, two_ref, three_ref, pre_ref, out_ref):
    out_ref[...] = jnp.zeros_like(out_ref)
    out_ref[0:8, :], out_ref[8:16, :], out_ref[16:24, :] = one_ref[...], two_ref[...], three_ref[...]
    out_ref[24:32, : pre_ref.shape[1]] = pre_ref[...]


SMALL = (0, 8, 16, 1, 9, 17, 2, 10, 18, 3, 11)


def small_kernel(s_ref, mine_ref, came_ref, self_ref, out_ref):
    out_ref[...] = jnp.zeros_like(out_ref)
    for to, at in enumerate(SMALL):
        out_ref[to : to + 1, :] = mine_ref[at : at + 1, :] + came_ref[at : at + 1, :]
    to = len(SMALL)
    out_ref[to : to + 1, :] = mine_ref[24:25, :] + came_ref[25:26, :]
    out_ref[to + 1 : to + 3, : self_ref.shape[1]] = self_ref[0:2, :]


def other_chip_kernel(blocks, s_ref, values, out):
    size, rows = values.shape[0] // blocks, out.shape[0] // blocks
    for block in range(blocks):
        to = spot_of(block, blocks) * rows
        start = block * size + (1 - s_ref[PLACE] // 2) * rows
        out[to : to + rows, :] = values[dyn(start, rows), :]


def chip_rows_kernel(blocks, s_ref, values, came, keep, first, second):
    size, rows = values.shape[0] // blocks, keep.shape[0] // blocks
    half = first.shape[1]
    for block in range(blocks):
        turned = spot_of(block, blocks)
        to = slice(turned * rows, (turned + 1) * rows)
        own = values[dyn(block * size + s_ref[PLACE] * rows, rows), :]
        keep[to, :] = add_low(own, came[dyn((2 * turned + s_ref[CORE_AT]) * rows, rows), :])
        other = values[dyn(block * size + (s_ref[PLACE] ^ CORE) * rows, rows), :]
        other = add_low(other, came[dyn((2 * turned + 1 - s_ref[CORE_AT]) * rows, rows), :])
        first[to, :] = other[:, :half]
        second[to, :] = other[:, half:]


def cross_rows_kernel(blocks, s_ref, *refs):
    send, keep = refs[9:]
    rows = refs[0].shape[0] // blocks
    for block in range(blocks):
        part = slice(block * rows, (block + 1) * rows)
        came = [
            jnp.concatenate([refs[3 * k + 1][part, :], refs[3 * k + 2][part, :]], axis=1)
            for k in range(3)
        ]
        values = [add_low(refs[0][part, :], came[0]), add_low(refs[3][part, :], came[1])]
        values.extend(halves(s_ref[CORE_AT], refs[6][part, :], came[2]))
        base = 4 * rows * (block % (blocks // 2))
        mine = s_ref[DP_AT] == block // (blocks // 2)
        for out, chosen in ((keep, mine), (send, jnp.logical_not(mine))):

            @pl.when(chosen)
            def _():
                for i, value in enumerate(values):
                    out[base + i * rows : base + (i + 1) * rows, :] = value


def general_cross_rows(d_q, d_back, d_kv, shard):
    dp_size, mem_size = lax.axis_size("dp"), lax.axis_size("mem")
    width = d_q.shape[1]

    def split(values, axis, bit, dim):
        mine = bit_at(axis, bit)
        entry = lambda at: lax.dynamic_index_in_dim(values, at, dim, keepdims=False)
        return entry(mine), entry(1 - mine)

    mem_dims = (2,) * len(bits_of("mem"))
    own = []
    for grad in (d_q, d_back):
        grad = grad.reshape((dp_size,) + mem_dims + (shard, width))
        for bit in chip_bits()[::-1]:
            grad = split(grad, "mem", bit, 1)[0]
        keep, send = split(grad, "mem", CORE, 1)
        own.append(add_low(keep, core_swap(send)))
    grad = d_kv.reshape((dp_size,) + mem_dims + (shard, width))
    for bit in chip_bits()[::-1]:
        keep, send = split(grad, "mem", bit, 1)
        grad = add_low(keep, swap(send, "mem", bit))
    keep, send = split(grad, "mem", CORE, 1)
    own = jnp.stack(own + list(halves(bit_at("mem", CORE), keep, core_swap(send))), axis=1)
    own = own.reshape((2,) * len(bits_of("dp")) + own.shape[1:])
    for bit in bits_of("dp")[::-1]:
        keep, send = split(own, "dp", bit, 0)
        own = add_low(keep, swap(send, "dp", bit))
    return own.astype(f32)


def local(
    dec_input,
    memory,
    dec_len,
    mem_len,
    self_in,
    self_in_bias,
    self_out,
    cross_in,
    cross_bias,
    cross_out,
    fc_in,
    fc_in_bias,
    fc_out,
    out_biases,
    norm_gains,
    norm_shifts,
    grad_out,
):
    items, steps, width = dec_input.shape
    mem_rows = memory.shape[1]
    local_width, hidden_width = self_in.shape[2], fc_in.shape[1]
    tokens = items * steps
    half, share = width // 2, tokens // 2
    dp_size, mem_size = lax.axis_size("dp"), lax.axis_size("mem")
    dp_bits = bits_of("dp")
    place = lax.axis_index("mem").astype(jnp.int32)
    core = bit_at("mem", CORE)
    numbers = [place, core, place * 0] + [bit_at("dp", bit) for bit in dp_bits]
    info = jnp.stack(numbers + [place * 0] * (LENS - len(numbers)))
    info = jnp.concatenate([info, mem_len, dec_len])

    x_low = dec_input.reshape(tokens, width)
    mem_low = memory.reshape(items * mem_rows, width)
    own_rows = pl.BlockSpec((share, width), lambda i, s: (s[CORE_AT], 0))
    columns = lambda values, at, size: lax.dynamic_slice_in_dim(values, at, size, 1)

    cross_pieces = relative({0: cross_in}, chip_bits())
    mem_far = core_swap(mem_low)
    bias_pair = jnp.concatenate([cross_bias.T, core_swap(cross_bias.T)], axis=0)
    bias_pieces = relative({0: bias_pair}, chip_bits())

    weight_self = jnp.transpose(self_in, (1, 0, 2))
    bias_self = self_in_bias.astype(f32)
    query_self = to_low(nn(x_low, weight_self[0]) + bias_self[0])
    key_self = to_low(nn(x_low, weight_self[1]))
    value_self = to_low(nn(x_low, weight_self[2]) + bias_self[1])
    (heads_self,) = call(
        functools.partial(self_forward_kernel, items),
        info,
        [query_self, key_self, value_self],
        [((tokens, local_width), bf16)],
        name="self_forward",
    )
    part_of = lambda core: lax.dynamic_slice_in_dim(heads_self, core * share, share, 0)
    came = core_swap(to_low(nn(part_of(1 - core), self_out)))
    attended = to_low(nn(part_of(core), self_out) + came.astype(f32))
    attended, attended_came = chip_swap(attended)

    points = (attended,) + tuple(bias_pieces.values())
    cross_pieces = {r: after(v, *points) if r else v for r, v in cross_pieces.items()}
    low_weight = [((width, width), bf16)]
    weight_kv, weight_query = assemble(
        info,
        relative(cross_pieces, [CORE]),
        ((0, width, half, 0, half), (0, 2 * width, half, half, half), (1, 0, 0, 0, width)),
        low_weight * 2,
        "cross_weights",
    )
    bias_pieces = {r: v[:2] for r, v in bias_pieces.items()} | {
        r ^ CORE: v[2:] for r, v in bias_pieces.items()
    }
    block = jnp.arange(width)[None, :] // local_width
    cross_shift = sum(
        jnp.where(block == (place ^ r), jnp.tile(v, (1, mem_size)).astype(f32), 0.0)
        for r, v in bias_pieces.items()
    )
    value_shift = lax.dynamic_slice_in_dim(cross_shift[1], core * half, half, 0)
    value_shift = jnp.concatenate([jnp.zeros((half,), f32), value_shift])
    vectors = jnp.concatenate(
        [
            norm_gains.astype(f32).T,
            norm_shifts.astype(f32).T,
            out_biases.astype(f32).T,
            jnp.zeros((7, width), f32),
        ],
        axis=0,
    )
    kv_near = to_low(nn(mem_low, weight_kv) + value_shift)
    kv_far = to_low(nn(mem_far, weight_kv) + value_shift)
    fc_in_far, fc_out_far = core_swap(after(fc_in, attended)), core_swap(after(fc_out, attended))
    fc_bias = fc_in_bias[None].astype(f32)
    fc_bias_far = core_swap(fc_in_bias)[None].astype(f32)

    token_f32, token_low = ((share, width), f32), ((share, width), bf16)
    token_half, one_each = ((share, half), bf16), ((share, 1), f32)
    normed_one, inverse_one, first_low, query_keep, query_send = call(
        first_norm_kernel,
        info,
        [(x_low, own_rows), attended, after(attended_came, kv_near, kv_far), vectors]
        + [cross_shift[:1], weight_query],
        [token_f32, one_each, token_low, token_half, token_half],
    )
    back_pieces = relative({0: after(cross_out, kv_near)}, chip_bits())
    back_pieces = {r: after(v, first_low) if r else v for r, v in back_pieces.items()}
    query_came = core_swap(query_send)
    (cross_back,) = assemble(
        info,
        relative(back_pieces, [CORE]),
        ((0, 0, 0, 0, width),),
        low_weight,
        "cross_back",
    )

    out, stat = cross_forward(info, items, query_keep, query_came, kv_near, kv_far)
    out = after(out, *back_pieces.values())
    for bit in chip_bits():
        out, stat = merge(info, bit, out, stat, swap(out, "mem", bit), swap(stat, "mem", bit))
    part_of_out = lambda core: lax.dynamic_slice_in_dim(out, core * share, share, 0)
    out_keep, out_came = part_of_out(core), core_swap(part_of_out(1 - core))

    units_low = ((share, hidden_width), bf16)
    weight = pltpu.VMEM((width, hidden_width), bf16)
    weight_out = pltpu.VMEM((hidden_width, width), bf16)
    cross_heads, normed_two, inverse_two, second_low, hidden, hidden_far, slope, slope_far, fed = call(
        middle_kernel,
        info,
        [normed_one, out_keep, out_came, vectors, fc_bias, fc_bias_far]
        + [(v, HBM) for v in (cross_back, fc_in, fc_in_far, fc_out, fc_out_far)],
        [token_low, token_f32, one_each, token_low] + [units_low] * 4 + [token_low],
        scratch=[
            pltpu.VMEM((width, width), bf16),
            weight,
            weight,
            weight_out,
            weight_out,
            pltpu.SemaphoreType.DMA((5,)),
        ],
        mega=20,
    )
    fed, fed_came = chip_swap(fed)
    second_other, hidden_other = core_swap(second_low), core_swap(hidden_far)
    final_low, d_three, d_three_low, d_pre, d_pre_far, d_fed, sums_three, pre_sums = call(
        turn_kernel,
        info,
        [normed_two, fed, fed_came, vectors, (grad_out.reshape(tokens, width), own_rows)]
        + [slope, slope_far]
        + [(v, HBM) for v in (fc_in, fc_in_far, fc_out, fc_out_far)],
        [token_low, token_f32, token_low, units_low, units_low, token_low]
        + [((8, width), f32), ((8, hidden_width), f32)],
        scratch=[weight, weight, weight_out, weight_out, pltpu.SemaphoreType.DMA((4,))],
        mega=20,
    )
    d_fed, d_fed_came = chip_swap(d_fed)

    order_one = dp_bits
    order_two = second_order(dp_bits)
    at_one, at_two = dp_position(order_one[0]), dp_position(order_two[0])
    d_three_other, d_pre_other = core_swap(d_three_low), core_swap(d_pre_far)
    fc_in_args = ([second_low, second_other], [d_pre, d_pre_other])
    fc_out_args = ([hidden, hidden_other], [d_three_low, d_three_other])
    upright = hidden_width == width
    if not upright:
        fc_in_args = fc_in_args[::-1]
    fc_in_send = grad_half(info, lambda s: 1 - s[at_one], *fc_in_args)
    fc_in_came = swap(fc_in_send, "dp", order_one[0])
    fc_out_send = grad_half(info, lambda s: 1 - s[at_two], *fc_out_args)
    fc_out_came = swap(fc_out_send, "dp", order_two[0])
    fc_in_keep = grad_half(info, lambda s: s[at_one], *fc_in_args)
    fc_out_keep = grad_half(info, lambda s: s[at_two], *fc_out_args)
    orders = (order_one, order_two)
    fc_sum = PairSum(
        info, orders, (fc_in_keep, fc_out_keep), (fc_in_came, fc_out_came)
    )

    d_fed_came = after(d_fed_came, fc_in_send, fc_out_send, fc_in_keep, fc_out_keep)
    d_two, d_two_low, d_keep, d_send, sums_two = call(
        second_back_kernel,
        info,
        [d_three, d_fed, d_fed_came, normed_two, inverse_two, vectors, cross_back],
        [token_f32, token_low, token_half, token_half, ((8, width), f32)],
    )
    d_came = core_swap(d_send)

    d_query_part, d_near, d_far = cross_backward(
        info, (query_keep, query_came), (d_keep, d_came), out, stat, kv_near, kv_far
    )
    d_query_part, d_query_came = chip_swap(d_query_part)
    flows_fc = [fc_sum]
    last = take_turns(flows_fc, d_query_part)

    d_kv = to_low(tn(mem_low, after(d_near, *last)) + tn(mem_far, d_far))
    shard = width // (dp_size * mem_size)
    simple = shard % 16 == 0 and mem_size == 4
    d_query_came = after(d_query_came, *take_turns(flows_fc, d_kv))
    if simple:
        (d_kv_send,) = call(
            functools.partial(other_chip_kernel, dp_size),
            info,
            [d_kv],
            [((width // 2, width), bf16)],
            name="other_chip",
        )
        d_kv_came = swap(d_kv_send, "mem", chip_bits()[0])
        d_query_came = after(d_query_came, d_kv_send)
    d_query_keep, d_query_send = call(
        split_sum_kernel, info, [d_query_part, d_query_came], [token_half, token_half]
    )
    d_query_send_came = core_swap(d_query_send)
    d_one_left, d_one_right, d_query_cross, sums_one = call(
        first_back_kernel,
        info,
        [d_two, d_query_keep, d_query_send_came, normed_one, inverse_one]
        + [vectors, weight_query],
        [token_half, token_half, token_low, ((8, width), f32)],
    )

    local_low = ((tokens, local_width), bf16)
    d_one_all, d_query, d_key, d_value, sums_self = call(
        functools.partial(self_backward_kernel, items),
        info,
        [query_self, key_self, value_self, d_one_left, d_one_right]
        + [core_swap(d_one_left), core_swap(d_one_right), self_out],
        [((tokens, width), bf16), local_low, local_low, local_low, ((8, local_width), f32)],
        scratch=[pltpu.VMEM((tokens, local_width), bf16)],
        name="self_backward",
    )

    self_args = (x_low, d_one_all, d_query, d_key, d_value, heads_self)
    self_one_send, self_two_send = self_grad(
        info, lambda s: 1 - s[at_one], lambda s: 3 - s[at_two], *self_args
    )
    self_one_came = swap(self_one_send, "dp", order_one[0])
    self_two_came = swap(self_two_send, "dp", order_two[0])
    last = (self_one_send, self_two_send)

    (small,) = call(
        stack_kernel,
        info,
        [sums_one, sums_two, after(sums_three, *last), pre_sums],
        [((32, width), f32)],
    )
    small_came = core_swap(small)
    self_one_keep, self_two_keep = self_grad(
        info, lambda s: s[at_one], lambda s: 2 + s[at_two], after(x_low, *last), *self_args[1:]
    )
    self_sum = PairSum(
        info, orders, (self_one_keep, self_two_keep), (self_one_came, self_two_came)
    )
    flows_self = [self_sum]
    last = (self_one_keep, self_two_keep)
    (fc_sum.extra,) = call(
        small_kernel, info, [small, after(small_came, *last), sums_self], [((16, width), f32)]
    )
    flows_self = [self_sum]

    chips = mem_size // 2
    shares = ((tokens, chips * local_width), bf16)
    partial, partial_send = call(
        input_part_kernel,
        info,
        [after(d_query, *last), d_key, d_value, weight_self],
        [shares, shares],
    )
    partial_came = core_swap(partial_send)

    if simple:
        q_keep, q_first, q_second, back_keep, back_first, back_second = cross_grad(
            info,
            dp_size,
            shard,
            [(after(first_low, *last), d_query_cross), (cross_heads, d_two_low)],
        )
        cross_parts = [q_keep, core_swap(q_first), core_swap(q_second)]
        cross_parts += [back_keep, core_swap(back_first), core_swap(back_second)]
        last = (q_keep,)
    last = take_turns(flows_fc, *last, partial)
    last = last + take_turns(flows_self, *last)
    if simple:
        rows = dp_size * shard
        d_kv_keep, d_kv_first, d_kv_second = call(
            functools.partial(chip_rows_kernel, dp_size),
            info,
            [d_kv, after(d_kv_came, *last)],
            [((rows, width), bf16), ((rows, half), bf16), ((rows, half), bf16)],
            name="chip_rows",
        )
        cross_parts += [d_kv_keep, core_swap(d_kv_first), core_swap(d_kv_second)]
        cross_send, cross_keep = call(
            functools.partial(cross_rows_kernel, dp_size),
            info,
            cross_parts,
            [((2 * rows, width), bf16)] * 2,
            name="cross_rows",
        )
        cross_sum = BlockSum(info, cross_keep, swap(cross_send, "dp", dp_bits[0]))
        last = last + (cross_send,)
    if chips == 2:
        input_grad, partial_send = call(
            input_sum_kernel,
            info,
            [partial, after(partial_came, *last), d_one_all],
            [((tokens, local_width), f32), local_low],
        )
        input_came = [swap(partial_send, "mem", chip_bits()[0])]
    else:
        partial = add_low(partial, partial_came)
        piece = lambda i: columns(partial, (place // 2 ^ i) * local_width, local_width)
        input_grad = columns(d_one_all, place * local_width, local_width).astype(f32)
        input_grad = input_grad + piece(0).astype(f32)
        input_came = [swap(piece(i), "mem", 2 * i) for i in range(1, chips)]
    flows_side = [cross_sum] if simple else []
    d_mem_far = memory_part(info, items, after(d_far, *last), weight_kv)
    last = take_turns(flows_self + flows_fc, *last, d_mem_far)
    last = last + take_turns(flows_side, *last)
    while len(fc_sum.back) > 2:
        last = take_turns(flows_self + flows_fc, *last)
    last = take_turns(flows_self, *last, *fc_sum.came) + fc_sum.advance_one(0, *last)
    d_mem_came = core_swap(after(d_mem_far, *last))
    last = last + take_turns(flows_self, *last)
    last = last + fc_sum.advance_one(1, *last)
    memory_grad = memory_part(info, items, after(d_near, *last), weight_kv, d_mem_came)
    fc_in_grad = fc_sum.whole(0, *last)
    while flows_side and not cross_sum.summed():
        last = last + take_turns(flows_side, *last)
    last = last + (memory_grad, fc_in_grad)
    while not self_sum.gathered():
        last = last + take_turns(flows_self, *last)
    input_came = [after(came, *last) for came in input_came]
    for came in input_came:
        input_grad = input_grad + came.astype(f32)
    input_grad = to_low(input_grad).reshape(items, steps, local_width)
    final_came = core_swap(after(final_low, *last))
    block_output = jnp.concatenate(halves(core, final_low, final_came), axis=0)
    block_output = block_output.reshape(items, steps, width)
    if not upright:
        fc_in_grad = fc_in_grad.T
    fc_out_grad = fc_sum.whole(1, *last)
    last = (fc_in_grad, fc_out_grad)
    self_in_grad, self_out_grad = call(
        functools.partial(self_finish_kernel, at_one, at_two),
        info,
        [self_sum.values[0], after(self_sum.came[0], *last)]
        + [self_sum.values[1], self_sum.came[1]],
        [((3, width, local_width), f32), ((local_width, width), f32)],
        name="self_finish",
    )
    self_in_grad = jnp.transpose(self_in_grad, (1, 0, 2))
    rows = fc_sum.extra_sum()
    spot = (lax.axis_index("dp") * mem_size + place) * shard
    owned = columns(rows, spot, shard)
    gains_grad, shifts_grad, out_biases_grad = owned[0:3].T, owned[3:6].T, owned[6:9].T
    cross_bias_grad = owned[9:11].T
    fc_in_bias_grad = rows[11, :hidden_width]
    self_in_bias_grad = rows[12:14, :local_width]
    if simple:
        cross_sum.arrived((after(cross_sum.pending()[0], *last),))
        cross_rows = cross_sum.total()
        q_rows, back_rows, left, right = (
            cross_rows[at * shard : (at + 1) * shard] for at in range(4)
        )
    else:
        d_q = to_low(tn(first_low, d_query_cross))
        d_back = to_low(tn(cross_heads, d_two_low))
        q_rows, back_rows, left, right = general_cross_rows(d_q, d_back, d_kv, shard)
    cross_in_grad = jnp.concatenate(
        [q_rows, left[:, :half], right[:, :half], left[:, half:], right[:, half:]], axis=1
    )
    cross_out_grad = back_rows

    return (
        block_output,
        input_grad,
        memory_grad.reshape(memory.shape),
        self_in_grad,
        self_in_bias_grad,
        self_out_grad,
        cross_in_grad,
        cross_bias_grad,
        cross_out_grad,
        fc_in_grad,
        fc_in_bias_grad,
        fc_out_grad,
        out_biases_grad,
        gains_grad,
        shifts_grad,
    )


def solution(mesh):
    placed = (
        P("dp", None, None),
        P("dp", "mem", None),
        P("dp"),
        P("dp"),
        P(None, None, "mem"),
        P(None, "mem"),
        P("mem", None),
        P("mem", None),
        P("mem", None),
        P("mem", None),
        P(None, "mem"),
        P("mem"),
        P("mem", None),
        P(),
        P(),
        P(),
        P("dp", None, None),
    )
    return jax.shard_map(
        local,
        mesh=mesh,
        in_specs=placed,
        out_specs=(
            P("dp", None, None),
            P("dp", None, "mem"),
            P("dp", "mem", None),
            P(None, None, "mem"),
            P(None, "mem"),
            P("mem", None),
            P(("dp", "mem"), None),
            P(("dp", "mem"), None),
            P(("dp", "mem"), None),
            P(None, "mem"),
            P("mem"),
            P("mem", None),
            P(("dp", "mem"), None),
            P(("dp", "mem"), None),
            P(("dp", "mem"), None),
        ),
        check_vma=False,
    )
```

```python
import functools

import jax
import jax.numpy as jnp
from jax import lax
from jax.experimental import pallas as pl
from jax.experimental.pallas import tpu as pltpu
from jax.sharding import PartitionSpec as P

HEAD_DIM = 64
PAIR = 2 * HEAD_DIM
CORE = 1
SCALE = HEAD_DIM ** (-0.5)
MASKED = -1e30
EPSILON = 1e-05
TILE = 256
MEGA = 1024 * 1024

f32 = jnp.float32
bf16 = jnp.bfloat16


def to_low(values):
    return values.astype(bf16)


def nt(left, right):
    return lax.dot_general(left, right, (((1,), (1,)), ((), ())), preferred_element_type=f32)


def nn(left, right):
    return lax.dot_general(left, right, (((1,), (0,)), ((), ())), preferred_element_type=f32)


def tn(left, right):
    return lax.dot_general(left, right, (((0,), (0,)), ((), ())), preferred_element_type=f32)


def col_sum(values):
    return jnp.sum(values, axis=0, keepdims=True)


def swap(values, axis, bit):
    pairs = [(i, i ^ bit) for i in range(lax.axis_size(axis))]
    return lax.ppermute(values, axis, pairs)


def core_swap(values):
    return swap(values, "mem", CORE)


def bits_of(axis):
    size, bits, bit = lax.axis_size(axis), [], 1
    while bit < size:
        bits.append(bit)
        bit *= 2
    return bits


def chip_bits():
    return bits_of("mem")[1:]


def bit_at(axis, bit):
    return (lax.axis_index(axis) // bit % 2).astype(jnp.int32)


def after(values, *others):
    return lax.optimization_barrier((values,) + others)[0]


def add_low(first, second):
    return to_low(first.astype(f32) + second.astype(f32))


def chip_swap(values):
    bits = chip_bits()
    for bit in bits[:-1]:
        values = add_low(values, swap(values, "mem", bit))
    return values, swap(values, "mem", bits[-1])


def relative(pieces, bits):
    for bit in bits:
        pieces = pieces | {r ^ bit: swap(piece, "mem", bit) for r, piece in pieces.items()}
    return pieces


def whole(shape):
    return pl.BlockSpec(shape, lambda *_: (0,) * len(shape))


HBM = pl.BlockSpec(memory_space=pl.ANY)


def call(
    kernel, info, inputs, outputs, scratch=(), grid=(1,), out_specs=None, mega=8, cost=0.0, name=None
):
    arrays = [given[0] if isinstance(given, tuple) else given for given in inputs]
    specs = [given[1] if isinstance(given, tuple) else whole(given.shape) for given in inputs]
    return pl.pallas_call(
        kernel,
        out_shape=[jax.ShapeDtypeStruct(*out) for out in outputs],
        grid_spec=pltpu.PrefetchScalarGridSpec(
            num_scalar_prefetch=1,
            grid=grid,
            in_specs=specs,
            out_specs=out_specs or [whole(out[0]) for out in outputs],
            scratch_shapes=list(scratch),
        ),
        compiler_params=pltpu.CompilerParams(vmem_limit_bytes=mega * MEGA),
        cost_estimate=pl.CostEstimate(
            flops=1 + int(cost * 1.1e9), bytes_accessed=1, transcendentals=0
        ),
        name=name or kernel.__name__,
    )(info, *arrays)


def dp_position(bit):
    return DP_AT + bit.bit_length() - 1


def norm_parts(resid):
    centre = resid - jnp.mean(resid, axis=-1, keepdims=True)
    inverse = lax.rsqrt(jnp.mean(centre * centre, axis=-1, keepdims=True) + EPSILON)
    return (centre * inverse, inverse)


def norm_back(normed, inverse, gain, upstream):
    scaled = upstream * gain
    return inverse * (
        scaled
        - jnp.mean(scaled, axis=-1, keepdims=True)
        - normed * jnp.mean(scaled * normed, axis=-1, keepdims=True)
    )


def row(ref, at):
    return ref[at : at + 1, :]


def wide(ref):
    return ref[...].astype(f32)


def halves(core, mine, theirs):
    first = core == 0
    return jnp.where(first, mine, theirs), jnp.where(first, theirs, mine)


def dyn(start, size, unit=16):
    return pl.ds(pl.multiple_of(start, unit), size)


PLACE, CORE_AT, DP_AT, LENS = 0, 1, 3, 8
GAIN, SHIFT, BIAS = 0, 3, 6


def assemble_kernel(ids, parts, s_ref, *refs):
    sources, outs, sem = refs[: len(ids)], refs[len(ids) : -1], refs[-1]
    rows = sources[0].shape[0]
    copies = []
    for source, r in zip(sources, ids):
        at = dyn((s_ref[PLACE] ^ r) * rows, rows)
        for out, start, step, to, width in parts:
            columns = pl.ds(pl.multiple_of(start + s_ref[CORE_AT] * step, 128), width)
            copies.append(
                pltpu.make_async_copy(
                    source.at[:, columns],
                    outs[out].at[at, pl.ds(to, width)],
                    sem.at[len(copies)],
                )
            )
    for copy in copies:
        copy.start()
    for copy in copies:
        copy.wait()


def assemble(info, pieces, parts, outputs, name):
    return call(
        functools.partial(assemble_kernel, tuple(pieces), parts),
        info,
        [(piece, HBM) for piece in pieces.values()],
        outputs,
        scratch=[pltpu.SemaphoreType.DMA((len(pieces) * len(parts),))],
        out_specs=[HBM] * len(outputs),
        name=name,
    )


def first_norm_kernel(
    s_ref,
    x_ref,
    mine_ref,
    came_ref,
    vec_ref,
    shift_ref,
    wq_ref,
    normed_ref,
    inv_ref,
    low_ref,
    keep_ref,
    send_ref,
):
    resid = wide(x_ref) + (wide(mine_ref) + wide(came_ref)) + row(vec_ref, BIAS)
    normed, inverse = norm_parts(resid)
    normed_ref[...] = normed
    inv_ref[...] = inverse
    low = to_low(normed * row(vec_ref, GAIN) + row(vec_ref, SHIFT))
    low_ref[...] = low
    half = keep_ref.shape[1]
    left, right = (
        to_low(nn(low, wq_ref[:, part]) + shift_ref[:, part])
        for part in (slice(0, half), slice(half, 2 * half))
    )
    keep_ref[...], send_ref[...] = halves(s_ref[CORE_AT], left, right)


def middle_kernel(
    s_ref,
    normed_ref,
    mine_ref,
    came_ref,
    vec_ref,
    bias_ref,
    bias_far_ref,
    back_hbm,
    in_hbm,
    in_far_hbm,
    out_hbm,
    out_far_hbm,
    heads_ref,
    normed_two_ref,
    inv_ref,
    low_ref,
    hidden_ref,
    hidden_far_ref,
    slope_ref,
    slope_far_ref,
    fed_ref,
    back,
    w_in,
    w_in_far,
    w_out,
    w_out_far,
    sem,
):
    loads = []
    for i, (source, target) in enumerate(
        (
            (back_hbm, back),
            (in_hbm, w_in),
            (in_far_hbm, w_in_far),
            (out_hbm, w_out),
            (out_far_hbm, w_out_far),
        )
    ):
        loads.append(pltpu.make_async_copy(source, target, sem.at[i]))
        loads[i].start()
    heads = jnp.concatenate(halves(s_ref[CORE_AT], mine_ref[...], came_ref[...]), axis=1)
    heads_ref[...] = heads
    first = normed_ref[...] * row(vec_ref, GAIN) + row(vec_ref, SHIFT)
    loads[0].wait()
    normed, inverse = norm_parts(first + nn(heads, back[...]) + row(vec_ref, BIAS + 1))
    normed_two_ref[...] = normed
    inv_ref[...] = inverse
    low = to_low(normed * row(vec_ref, GAIN + 1) + row(vec_ref, SHIFT + 1))
    low_ref[...] = low
    for i, (weight, shift, hidden, slope) in enumerate(
        ((w_in, bias_ref, hidden_ref, slope_ref), (w_in_far, bias_far_ref, hidden_far_ref, slope_far_ref))
    ):
        loads[1 + i].wait()
        for at in range(0, weight.shape[1], TILE):
            part = slice(at, at + TILE)
            pre = nn(low, weight[:, part]) + shift[:, part]
            share = 0.5 * (1.0 + lax.erf(pre * (0.5**0.5)))
            hidden[:, part] = to_low(pre * share)
            density = jnp.exp(-0.5 * pre * pre) * (1.0 / (2.0 * jnp.pi) ** 0.5)
            slope[:, part] = to_low(share + pre * density)
    loads[3].wait()
    loads[4].wait()
    for at in range(0, fed_ref.shape[1], TILE):
        part = slice(at, at + TILE)
        fed_ref[:, part] = to_low(
            nn(hidden_ref[...], w_out[:, part]) + nn(hidden_far_ref[...], w_out_far[:, part])
        )


def turn_kernel(
    s_ref,
    normed_two_ref,
    mine_ref,
    came_ref,
    vec_ref,
    grad_ref,
    slope_ref,
    slope_far_ref,
    in_hbm,
    in_far_hbm,
    out_hbm,
    out_far_hbm,
    final_ref,
    d_ref,
    d_low_ref,
    pre_ref,
    pre_far_ref,
    part_ref,
    sums_ref,
    pre_sums_ref,
    w_in,
    w_in_far,
    w_out,
    w_out_far,
    sem,
):
    loads = []
    for i, (source, target) in enumerate(
        ((out_hbm, w_out), (out_far_hbm, w_out_far), (in_hbm, w_in), (in_far_hbm, w_in_far))
    ):
        loads.append(pltpu.make_async_copy(source, target, sem.at[i]))
        loads[i].start()
    second = normed_two_ref[...] * row(vec_ref, GAIN + 1) + row(vec_ref, SHIFT + 1)
    resid = second + (wide(mine_ref) + wide(came_ref)) + row(vec_ref, BIAS + 2)
    normed, inverse = norm_parts(resid)
    gain = row(vec_ref, GAIN + 2)
    final_ref[...] = to_low(normed * gain + row(vec_ref, SHIFT + 2))
    upstream = wide(grad_ref)
    d_resid = norm_back(normed, inverse, gain, upstream)
    d_ref[...] = d_resid
    d_low = to_low(d_resid)
    d_low_ref[...] = d_low
    sums_ref[...] = jnp.zeros_like(sums_ref)
    sums_ref[0:1, :] = col_sum(upstream * normed)
    sums_ref[1:2, :] = col_sum(upstream)
    sums_ref[2:3, :] = col_sum(d_resid)
    pre_sums_ref[...] = jnp.zeros_like(pre_sums_ref)
    for i, (weight, slope, pre) in enumerate(
        ((w_out, slope_ref, pre_ref), (w_out_far, slope_far_ref, pre_far_ref))
    ):
        loads[i].wait()
        for at in range(0, weight.shape[0], TILE):
            part = slice(at, at + TILE)
            d_pre = to_low(nt(d_low, weight[part, :]) * slope[:, part].astype(f32))
            pre[:, part] = d_pre
            pre_sums_ref[i : i + 1, part] = col_sum(d_pre.astype(f32))
    loads[2].wait()
    loads[3].wait()
    for at in range(0, part_ref.shape[1], TILE):
        part = slice(at, at + TILE)
        part_ref[:, part] = to_low(
            nt(pre_ref[...], w_in[part, :]) + nt(pre_far_ref[...], w_in_far[part, :])
        )


def second_back_kernel(
    s_ref,
    d_three_ref,
    mine_ref,
    came_ref,
    normed_ref,
    inv_ref,
    vec_ref,
    back_ref,
    d_ref,
    d_low_ref,
    keep_ref,
    send_ref,
    sums_ref,
):
    upstream = d_three_ref[...] + (wide(mine_ref) + wide(came_ref))
    normed = normed_ref[...]
    d_resid = norm_back(normed, inv_ref[...], row(vec_ref, GAIN + 1), upstream)
    d_ref[...] = d_resid
    d_low = to_low(d_resid)
    d_low_ref[...] = d_low
    half = keep_ref.shape[1]
    left = to_low(nt(d_low, back_ref[:half, :]))
    right = to_low(nt(d_low, back_ref[half:, :]))
    keep_ref[...], send_ref[...] = halves(s_ref[CORE_AT], left, right)
    sums_ref[...] = jnp.zeros_like(sums_ref)
    sums_ref[0:1, :] = col_sum(upstream * normed)
    sums_ref[1:2, :] = col_sum(upstream)
    sums_ref[2:3, :] = col_sum(d_resid)
    sums_ref[3:4, :half] = col_sum(left.astype(f32))
    sums_ref[3:4, half:] = col_sum(right.astype(f32))


def split_sum_kernel(s_ref, mine_ref, came_ref, keep_ref, send_ref):
    rows = keep_ref.shape[0]
    for out, core in ((send_ref, 1 - s_ref[CORE_AT]), (keep_ref, s_ref[CORE_AT])):
        part = dyn(core * rows, rows)
        out[...] = add_low(mine_ref[part, :], came_ref[part, :])


def first_back_kernel(
    s_ref,
    d_two_ref,
    mine_ref,
    came_ref,
    normed_ref,
    inv_ref,
    vec_ref,
    wq_ref,
    left_ref,
    right_ref,
    query_ref,
    sums_ref,
):
    d_query = jnp.concatenate(halves(s_ref[CORE_AT], mine_ref[...], came_ref[...]), axis=1)
    query_ref[...] = d_query
    upstream = d_two_ref[...] + nt(d_query, wq_ref[...])
    normed = normed_ref[...]
    d_resid = norm_back(normed, inv_ref[...], row(vec_ref, GAIN), upstream)
    half = left_ref.shape[1]
    left_ref[...] = to_low(d_resid[:, :half])
    right_ref[...] = to_low(d_resid[:, half:])
    sums_ref[...] = jnp.zeros_like(sums_ref)
    sums_ref[0:1, :] = col_sum(upstream * normed)
    sums_ref[1:2, :] = col_sum(upstream)
    sums_ref[2:3, :] = col_sum(d_resid)
    sums_ref[3:4, :] = col_sum(d_query.astype(f32))


def stacked(block, first_head):
    zero = jnp.zeros_like(block)
    return jnp.concatenate(
        [jnp.where(first_head, block, zero), jnp.where(first_head, zero, block)], axis=0
    )


def unstacked(both, first_head):
    rows = both.shape[0] // 2
    return jnp.where(first_head, both[:rows], both[rows:])


def first_lanes(rows):
    return lax.broadcasted_iota(jnp.int32, (rows, PAIR), 1) < HEAD_DIM


def row_sums(values):
    lanes = lax.broadcasted_iota(jnp.int32, (16, PAIR), 1)
    which = lax.broadcasted_iota(jnp.int32, (16, PAIR), 0)
    pick = to_low((lanes // HEAD_DIM == which).astype(f32))
    high = to_low(values)
    low = to_low(values - high.astype(f32))
    sums = nt(pick, high) + nt(pick, low)
    return jnp.concatenate([sums[0:1], sums[1:2]], axis=1)


def shown(length, place, rows):
    spot = lax.broadcasted_iota(jnp.int32, (rows, 1), 0)
    return jnp.concatenate(
        [place * rows + spot < length, (place ^ CORE) * rows + spot < length], axis=0
    )


def join_rows(core, mine_ref, came_ref, both):
    rows = mine_ref.shape[0]
    both[dyn(core * rows, rows), :] = mine_ref[...]
    both[dyn((1 - core) * rows, rows), :] = came_ref[...]


def cross_forward_kernel(s_ref, mine_ref, came_ref, near_ref, far_ref, o_ref, stat_ref, both):
    item = pl.program_id(0)

    @pl.when(item == 0)
    def _():
        join_rows(s_ref[CORE_AT], mine_ref, came_ref, both)

    steps, width = o_ref.shape
    rows = dyn(item * steps, steps)
    visible = shown(s_ref[LENS + item], s_ref[PLACE], near_ref.shape[0])
    first_head = first_lanes(steps)
    for pair in range(width // PAIR):
        lanes = slice(pair * PAIR, (pair + 1) * PAIR)
        values = slice(width + pair * PAIR, width + (pair + 1) * PAIR)
        query = stacked(both[rows, lanes] * SCALE, first_head)
        key = jnp.concatenate([near_ref[:, lanes], far_ref[:, lanes]], axis=0)
        value = jnp.concatenate([near_ref[:, values], far_ref[:, values]], axis=0)
        scores = jnp.where(visible, nt(key, query), MASKED)
        top = jnp.max(scores, axis=0, keepdims=True)
        grown = jnp.exp(scores - top)
        total = jnp.sum(grown, axis=0, keepdims=True)
        weights = to_low(grown * (1.0 / total))
        o_ref[:, lanes] = to_low(unstacked(tn(weights, value), first_head))
        stat = top + jnp.log(total)
        stat_ref[0, 2 * pair : 2 * pair + 1, :] = stat[:, :steps]
        stat_ref[0, 2 * pair + 1 : 2 * pair + 2, :] = stat[:, steps:]


def cross_forward(info, items, mine, came, near, far):
    width, tokens = mine.shape[1], 2 * mine.shape[0]
    rows, steps = near.shape[0] // items, tokens // items
    heads = width // HEAD_DIM
    keys = pl.BlockSpec((rows, 2 * width), lambda i, *_: (i, 0))
    return call(
        cross_forward_kernel,
        info,
        [mine, came, (near, keys), (far, keys)],
        [((tokens, width), bf16), ((items, heads, steps), f32)],
        scratch=[pltpu.VMEM((tokens, width), bf16)],
        grid=(items,),
        mega=14,
        out_specs=[
            pl.BlockSpec((steps, width), lambda i, *_: (i, 0)),
            pl.BlockSpec((1, heads, steps), lambda i, *_: (i, 0, 0)),
        ],
    )


def merge_kernel(bit, s_ref, a_ref, sa_ref, b_ref, sb_ref, o_ref, stat_ref):
    flip = (s_ref[PLACE] & bit) != 0
    items, heads, steps = sa_ref.shape
    width = a_ref.shape[1]
    pick = lax.broadcasted_iota(jnp.int32, (heads, width), 1) // HEAD_DIM
    pick = to_low((pick == lax.broadcasted_iota(jnp.int32, (heads, width), 0)).astype(f32))

    def spread(share):
        high = to_low(share)
        return tn(high, pick) + tn(to_low(share - high.astype(f32)), pick)

    for item in range(items):
        rows = slice(item * steps, (item + 1) * steps)
        mine, theirs = sa_ref[item], sb_ref[item]
        first, second = jnp.where(flip, theirs, mine), jnp.where(flip, mine, theirs)
        top = jnp.maximum(first, second)
        grown_first, grown_second = jnp.exp(first - top), jnp.exp(second - top)
        total = grown_first + grown_second
        stat_ref[item] = top + jnp.log(total)
        low_values = jnp.where(flip, b_ref[rows, :], a_ref[rows, :]).astype(f32)
        high_values = jnp.where(flip, a_ref[rows, :], b_ref[rows, :]).astype(f32)
        o_ref[rows, :] = to_low(
            spread(grown_first / total) * low_values + spread(grown_second / total) * high_values
        )


def merge(info, bit, mine, stat_mine, theirs, stat_theirs):
    return call(
        functools.partial(merge_kernel, bit),
        info,
        [mine, stat_mine, theirs, stat_theirs],
        [(mine.shape, bf16), (stat_mine.shape, f32)],
        name="merge",
    )


def cross_backward_kernel(
    s_ref, q_ref, q_came_ref, do_mine_ref, do_came_ref, o_ref, stat_ref, near_ref, far_ref,
    dq_ref, dnear_ref, dfar_ref, q_both, do_both,
):
    item = pl.program_id(0)

    @pl.when(item == 0)
    def _():
        join_rows(s_ref[CORE_AT], q_ref, q_came_ref, q_both)
        join_rows(s_ref[CORE_AT], do_mine_ref, do_came_ref, do_both)

    steps, width = dq_ref.shape
    rows = near_ref.shape[0]
    tokens = dyn(item * steps, steps)
    visible = shown(s_ref[LENS + item], s_ref[PLACE], rows)
    first_head = first_lanes(steps)
    for pair in range(width // PAIR):
        lanes = slice(pair * PAIR, (pair + 1) * PAIR)
        values = slice(width + pair * PAIR, width + (pair + 1) * PAIR)
        d_out = do_both[tokens, lanes]
        dots = row_sums(d_out.astype(f32) * o_ref[:, lanes].astype(f32))
        stat = jnp.concatenate(
            [stat_ref[0, 2 * pair : 2 * pair + 1, :], stat_ref[0, 2 * pair + 1 : 2 * pair + 2, :]],
            axis=1,
        )
        query = stacked(q_both[tokens, lanes] * SCALE, first_head)
        d_both = stacked(d_out, first_head)
        key = jnp.concatenate([near_ref[:, lanes], far_ref[:, lanes]], axis=0)
        value = jnp.concatenate([near_ref[:, values], far_ref[:, values]], axis=0)
        scores = jnp.where(visible, nt(key, query), MASKED)
        probs = jnp.exp(scores - stat)
        d_scores = to_low(probs * (nt(value, d_both) - dots))
        d_value = to_low(nn(to_low(probs), d_both))
        d_key = to_low(nn(d_scores, query))
        dnear_ref[:, lanes] = d_key[:rows]
        dfar_ref[:, lanes] = d_key[rows:]
        dnear_ref[:, values] = d_value[:rows]
        dfar_ref[:, values] = d_value[rows:]
        dq_ref[:, lanes] = to_low(unstacked(tn(d_scores, key), first_head) * SCALE)


def cross_backward(info, queries, d_outs, out, stat, near, far):
    items, heads, steps = stat.shape
    tokens, width = out.shape
    rows = near.shape[0] // items
    keys = pl.BlockSpec((rows, 2 * width), lambda i, *_: (i, 0))
    block = pl.BlockSpec((steps, width), lambda i, *_: (i, 0))
    return call(
        cross_backward_kernel,
        info,
        list(queries)
        + list(d_outs)
        + [
            (out, block),
            (stat, pl.BlockSpec((1, heads, steps), lambda i, *_: (i, 0, 0))),
            (near, keys),
            (far, keys),
        ],
        [(out.shape, bf16), (near.shape, bf16), (far.shape, bf16)],
        scratch=[pltpu.VMEM((tokens, width), bf16)] * 2,
        grid=(items,),
        mega=14,
        out_specs=[block, keys, keys],
    )


def self_weights(query_block, key_block, first_head, allowed):
    query = stacked(query_block * SCALE, first_head)
    scores = jnp.where(allowed, nt(key_block, query), MASKED)
    top = jnp.max(scores, axis=0, keepdims=True)
    grown = jnp.exp(scores - top)
    total = jnp.sum(grown, axis=0, keepdims=True)
    return query, grown * (1.0 / total)


def self_parts(len_ref, items, tokens, width):
    steps = tokens // items
    keys = lax.broadcasted_iota(jnp.int32, (steps, 2 * steps), 0)
    queries = lax.broadcasted_iota(jnp.int32, (steps, 2 * steps), 1) % steps
    causal = keys <= queries
    for item in range(items):
        allowed = jnp.logical_and(causal, keys < len_ref[LENS + items + item])
        for pair in range(width // PAIR):
            yield (
                slice(item * steps, (item + 1) * steps),
                slice(pair * PAIR, (pair + 1) * PAIR),
                allowed,
            )


def self_forward_kernel(items, len_ref, q_ref, k_ref, v_ref, o_ref):
    tokens, width = q_ref.shape
    first_head = first_lanes(tokens // items)
    for rows, lanes, allowed in self_parts(len_ref, items, tokens, width):
        _, probs = self_weights(q_ref[rows, lanes], k_ref[rows, lanes], first_head, allowed)
        o_ref[rows, lanes] = to_low(unstacked(tn(to_low(probs), v_ref[rows, lanes]), first_head))


def self_backward_kernel(
    items, s_ref, q_ref, k_ref, v_ref, left_ref, right_ref, left_came, right_came, out_ref,
    d_low_ref, dq_ref, dk_ref, dv_ref, sums_ref, do_both,
):
    tokens, width = q_ref.shape
    half = left_ref.shape[1]
    for at, mine, came in ((0, left_ref, left_came), (half, right_ref, right_came)):
        part = slice(at, at + half)
        rows = mine.shape[0]
        d_low_ref[dyn(s_ref[CORE_AT] * rows, rows), part] = mine[...]
        d_low_ref[dyn((1 - s_ref[CORE_AT]) * rows, rows), part] = came[...]
    do_both[...] = to_low(nt(d_low_ref[...], out_ref[...]))
    first_head = first_lanes(tokens // items)
    for rows, lanes, allowed in self_parts(s_ref, items, tokens, width):
        key = k_ref[rows, lanes]
        query, probs = self_weights(q_ref[rows, lanes], key, first_head, allowed)
        d_both = stacked(do_both[rows, lanes], first_head)
        d_probs = nt(v_ref[rows, lanes], d_both)
        dots = jnp.sum(probs * d_probs, axis=0, keepdims=True)
        d_scores = to_low(probs * (d_probs - dots))
        dv_ref[rows, lanes] = to_low(nn(to_low(probs), d_both))
        dk_ref[rows, lanes] = to_low(nn(d_scores, query))
        dq_ref[rows, lanes] = to_low(unstacked(tn(d_scores, key), first_head) * SCALE)
    sums_ref[...] = jnp.zeros_like(sums_ref)
    sums_ref[0:1, :] = col_sum(dq_ref[...].astype(f32))
    sums_ref[1:2, :] = col_sum(do_both[...].astype(f32))


def grad_half_kernel(count, s_ref, *refs):
    for at in range(0, refs[-1].shape[1], TILE):
        part = slice(at, at + TILE)
        total = tn(refs[0][...], refs[count][:, part])
        for i in range(1, count):
            total = total + tn(refs[i][...], refs[count + i][:, part])
        refs[-1][:, part] = to_low(total)


def grad_half(info, index, lefts, rights):
    rows, columns = lefts[0].shape[1] // 2, rights[0].shape[1]
    spec = lambda left: pl.BlockSpec((left.shape[0], rows), lambda i, s: (0, index(s)))
    return call(
        functools.partial(grad_half_kernel, len(lefts)),
        info,
        [(left, spec(left)) for left in lefts] + list(rights),
        [((rows, columns), bf16)],
        cost=5.0,
        name="grad_half",
    )[0]


def self_grad_kernel(s_ref, x0_ref, x1_ref, d0_ref, d1_ref, q_ref, k_ref, v_ref, h_ref, *outs):
    width = q_ref.shape[1]
    for x_ref, d_ref, out in ((x0_ref, d0_ref, outs[0]), (x1_ref, d1_ref, outs[1])):
        for i, ref in enumerate((q_ref, k_ref, v_ref)):
            out[:, i * width : (i + 1) * width] = to_low(tn(x_ref[...], ref[...]))
        out[:, 3 * width :] = to_low(tn(d_ref[...], h_ref[...]))


def self_grad(info, first, second, x, d_low, query, key, value, heads):
    rows, tokens, width = x.shape[1] // 4, x.shape[0], query.shape[1]
    at = lambda index: pl.BlockSpec((tokens, rows), lambda i, s: (0, index(s)))
    return call(
        self_grad_kernel,
        info,
        [(x, at(first)), (x, at(second)), (d_low, at(first)), (d_low, at(second)), query, key, value, heads],
        [((rows, 4 * width), bf16)] * 2,
    )


def put_wide(out, at, values):
    rows = values.shape[0]
    high = to_low(values)
    out[at : at + rows, :] = high
    out[at + rows : at + 2 * rows, :] = to_low(values - high.astype(f32))


def get_wide(ref, at, rows):
    return ref[at : at + rows, :].astype(f32) + ref[at + rows : at + 2 * rows, :].astype(f32)


def split_kernel(positions, joint, s_ref, *refs):
    count = len(positions)
    mine, came, outs = refs[:count], refs[count : 2 * count], refs[2 * count :]
    sends, keeps = outs[:-count], outs[-count:]
    rows = keeps[0].shape[0]
    for k, position in enumerate(positions):
        base = 2 * rows * k if joint[0] else 0
        for send in (True, False):
            half = 1 - s_ref[position] if send else s_ref[position]
            total = add_low(
                mine[k][dyn(half * rows, rows), :], came[k][dyn(base + half * rows, rows), :]
            )
            if not send:
                keeps[k][...] = total
            elif joint[1]:
                sends[0][k * rows : (k + 1) * rows, :] = total
            else:
                sends[k][...] = total


def split(info, bits, mine, came, joint):
    rows, columns = mine[0].shape[0] // 2, mine[0].shape[1]
    sends = [2 * rows] if joint[1] else [rows] * len(bits)
    return call(
        functools.partial(split_kernel, [dp_position(bit) for bit in bits], joint),
        info,
        list(mine) + list(came),
        [((size, columns), bf16) for size in sends + [rows] * len(bits)],
        name="split_sums",
    )


def total_kernel(joint, extra, s_ref, *refs):
    mine, came, outs = refs[:2], refs[2:4], refs[4 + extra :]
    rows = mine[0].shape[0]
    for k in range(2):
        base = rows * k if joint[0] else 0
        total = add_low(mine[k][...], came[k][base : base + rows, :])
        if joint[1]:
            outs[0][k * rows : (k + 1) * rows, :] = total
        else:
            outs[k][...] = total
    if extra:
        put_wide(outs[0], 2 * rows, refs[4][...])


def total_pair(info, mine, came, joint, extra=None):
    rows, columns = mine[0].shape
    extras = [] if extra is None else [extra]
    more = 2 * sum(v.shape[0] for v in extras)
    outputs = [2 * rows + more] if joint[1] else [rows, rows]
    return call(
        functools.partial(total_kernel, joint, len(extras)),
        info,
        list(mine) + list(came) + extras,
        [((size, columns), bf16) for size in outputs],
        name="total_sums",
    )


def join_pair_kernel(positions, given, extra, s_ref, *refs):
    mine, came, outs = refs[:given], refs[given : 2 * given], refs[2 * given :]
    joint = given < len(positions)
    rows = mine[0].shape[0] - 2 * extra
    rows = rows // 2 if joint else rows
    for k, position in enumerate(positions):
        part = slice(k * rows, (k + 1) * rows) if joint else slice(0, rows)
        own, other = mine[k % given][part, :], came[k % given][part, :]
        base = 2 * rows * k if len(outs) < len(positions) else 0
        out = outs[k % len(outs)]
        out[dyn(base + s_ref[position] * rows, rows), :] = own
        out[dyn(base + (1 - s_ref[position]) * rows, rows), :] = other
    if extra:
        at = mine[0].shape[0] - 2 * extra
        total = get_wide(mine[0], at, extra) + get_wide(came[0], at, extra)
        put_wide(outs[0], outs[0].shape[0] - 2 * extra, total)


def join_pair(info, bits, mine, came, joint, extra=0, cost=8.0):
    given, columns = len(mine), mine[0].shape[1]
    rows = mine[0].shape[0] - 2 * extra
    rows = (rows if given == len(bits) else rows // 2) * 2
    more = 2 * extra
    outputs = [len(bits) * rows + more] if joint else [rows + more] + [rows] * (len(bits) - 1)
    return call(
        functools.partial(
            join_pair_kernel, [dp_position(bit) for bit in bits], given, extra
        ),
        info,
        list(mine) + list(came),
        [((size, columns), bf16) for size in outputs],
        cost=cost,
        name="join_pair",
    )


def join_kernel(position, s_ref, mine_ref, came_ref, out_ref):
    @pl.when(pl.program_id(1) == s_ref[position])
    def _():
        out_ref[...] = mine_ref[...].astype(out_ref.dtype)

    @pl.when(pl.program_id(1) != s_ref[position])
    def _():
        out_ref[...] = came_ref[...].astype(out_ref.dtype)


def join(info, bit, mine, came, rows):
    columns = mine.shape[1]
    spec = pl.BlockSpec((rows, columns), lambda i, j, s: (0, 0))
    return call(
        functools.partial(join_kernel, dp_position(bit)),
        info,
        [(mine, spec), (came, spec)],
        [((2 * rows, columns), f32)],
        grid=(1, 2),
        out_specs=[pl.BlockSpec((rows, columns), lambda i, j, s: (j, 0))],
        name="join",
    )[0]


class PairSum:
    def __init__(self, info, orders, keeps, cames):
        self.info, self.step = info, 1
        self.bits = list(zip(*orders))
        self.back = self.bits[::-1]
        self.mine, self.came, self.extra = tuple(keeps), tuple(cames), None
        self.joint, self.gathering = False, False

    def pending(self):
        return self.came

    def arrived(self, came):
        self.came = came

    def exchange(self, values, bits):
        if len(values) == 1:
            self.came = (swap(values[0], "dp", bits[0]),)
        else:
            self.came = tuple(swap(value, "dp", bit) for value, bit in zip(values, bits))

    def advance(self):
        same = lambda bits: bits[0] == bits[1]
        came = self.came if len(self.came) == 2 else self.came * 2
        if self.step < len(self.bits):
            bits = self.bits[self.step]
            joint = (self.joint, same(bits))
            result = split(self.info, bits, self.mine, came, joint)
            sent, self.mine, self.joint = tuple(result[:-2]), tuple(result[-2:]), joint[1]
            self.step += 1
            self.exchange(sent, bits)
            return sent
        if not self.gathering:
            joint = (self.joint, same(self.back[0]))
            self.values = total_pair(self.info, self.mine, came, joint, self.extra)
            self.gathering = True
        else:
            bits = self.back.pop(0)
            extra = 0 if self.extra is None else self.extra.shape[0]
            joint = same(self.back[0])
            self.values = tuple(
                join_pair(
                    self.info,
                    bits,
                    self.values,
                    self.came,
                    joint,
                    extra,
                    0.0 if len(self.back) == 1 else 8.0,
                )
            )
        self.exchange(self.values, self.back[0])
        return tuple(self.values)

    def advance_one(self, k, *points):
        bit, last = self.back[0][k], self.back[1][k]
        extra = 0 if k or self.extra is None else self.extra.shape[0]
        mine, came = self.values[k], after(self.came[k], *points) if points else self.came[k]
        cost = 8.0 if k else 8.0
        (values,) = join_pair(self.info, [bit], [mine], [came], False, extra, cost)
        self.values = self.values[:k] + (values,) + self.values[k + 1 :]
        self.came = self.came[:k] + (swap(values, "dp", last),) + self.came[k + 1 :]
        if k:
            self.back.pop(0)
        return (values,)

    def gathered(self):
        return self.gathering and len(self.back) == 1

    def whole(self, k, *points):
        self.came = self.came[:k] + (after(self.came[k], *points),) + self.came[k + 1 :]
        rows = self.values[1].shape[0]
        return join(self.info, self.back[0][k], self.values[k], self.came[k], rows)

    def extra_sum(self):
        extra = self.extra.shape[0]
        at = self.values[0].shape[0] - 2 * extra
        total = self.values[0][at:].astype(f32) + self.came[0][at:].astype(f32)
        return total[:extra] + total[extra:]


class BlockSum:
    def __init__(self, info, keep, came):
        self.info, self.order = info, bits_of("dp")[1:]
        self.mine, self.came = keep, (came,)

    def pending(self):
        return self.came

    def arrived(self, came):
        self.came = came

    def summed(self):
        return not self.order

    def advance(self):
        bit = self.order.pop(0)
        sent, self.mine = split(self.info, [bit], [self.mine], self.came, (False, False))
        self.came = (swap(sent, "dp", bit),)
        return (sent,)

    def total(self):
        return self.mine.astype(f32) + self.came[0].astype(f32)


def take_turns(flows, *points):
    if not flows:
        return ()
    came = lax.optimization_barrier((tuple(flow.pending() for flow in flows), points))[0]
    for flow, values in zip(flows, came):
        flow.arrived(values)
    return sum((flow.advance() for flow in flows), ())


def self_finish_kernel(first, second, s_ref, upper_ref, upper_came_ref, lower_ref, lower_came_ref, in_ref, out_ref):
    rows, width = upper_ref.shape[0], in_ref.shape[2]
    blocks = halves(s_ref[first], upper_ref[...], upper_came_ref[...])
    blocks = blocks + halves(s_ref[second], lower_ref[...], lower_came_ref[...])
    for at, block in enumerate(blocks):
        block = block.astype(f32)
        part = slice(at * rows, (at + 1) * rows)
        for i in range(3):
            in_ref[i, part, :] = block[:, i * width : (i + 1) * width]
        out_ref[:, part] = block[:, 3 * width :].T


def second_order(bits):
    return bits[1:2] + bits[:1] + bits[2:]


def spot_of(block, blocks):
    order = [1 << i for i in range(blocks.bit_length() - 1)]
    return sum((block // bit % 2) << (len(order) - 1 - i) for i, bit in enumerate(order))


def cross_grad_kernel(blocks, s_ref, *refs):
    scratch = refs[10]
    for k in range(2):
        left, right = refs[2 * k], refs[2 * k + 1]
        keep, first, second = refs[4 + 3 * k : 7 + 3 * k]
        rows, half = keep.shape[0] // blocks, first.shape[1]
        for at in range(0, right.shape[1], TILE):
            part = slice(at, at + TILE)
            scratch[...] = to_low(tn(left[...], right[:, part]))
            size = scratch.shape[0] // blocks
            send, column = (first, at) if at < half else (second, at - half)
            sent = slice(column, column + TILE)
            for block in range(blocks):
                turned = spot_of(block, blocks)
                to = slice(turned * rows, (turned + 1) * rows)
                own = dyn(block * size + s_ref[PLACE] * rows, rows)
                other = dyn(block * size + (s_ref[PLACE] ^ CORE) * rows, rows)
                keep[to, part] = scratch[own, :]
                send[to, sent] = scratch[other, :]


def cross_grad(info, blocks, shard, pairs):
    width = pairs[0][0].shape[1]
    rows = blocks * shard
    outputs = [((rows, width), bf16), ((rows, width // 2), bf16), ((rows, width // 2), bf16)]
    return call(
        functools.partial(cross_grad_kernel, blocks),
        info,
        [array for pair in pairs for array in pair],
        outputs * 2,
        scratch=[pltpu.VMEM((width, TILE), bf16)],
        name="cross_grad",
    )


def input_part_kernel(s_ref, q_ref, k_ref, v_ref, weight_ref, keep_ref, send_ref):
    width = q_ref.shape[1]
    for out, core in ((send_ref, 1 - s_ref[CORE_AT]), (keep_ref, s_ref[CORE_AT])):
        for i in range(out.shape[1] // width):
            rows = dyn((2 * i + core) * width, width)
            total = nt(q_ref[...], weight_ref[0, rows, :])
            total = total + nt(k_ref[...], weight_ref[1, rows, :])
            total = total + nt(v_ref[...], weight_ref[2, rows, :])
            out[:, i * width : (i + 1) * width] = to_low(total)


def input_sum_kernel(s_ref, mine_ref, came_ref, d_ref, keep_ref, send_ref):
    width = keep_ref.shape[1]
    chip = s_ref[PLACE] // 2
    other = dyn((1 - chip) * width, width, 128)
    send_ref[...] = add_low(mine_ref[:, other], came_ref[:, other])
    own = dyn(chip * width, width, 128)
    keep_ref[...] = (
        mine_ref[:, own].astype(f32)
        + came_ref[:, own].astype(f32)
        + d_ref[:, dyn(s_ref[PLACE] * width, width, 128)].astype(f32)
    )


def memory_kernel(s_ref, d_ref, weight_ref, *refs):
    total = nt(d_ref[...], weight_ref[...])
    if len(refs) == 2:
        total = total + wide(refs[0])
    refs[-1][...] = to_low(total)


def memory_part(info, items, d_ref, weight, *came):
    rows = pl.BlockSpec((d_ref.shape[0] // items, d_ref.shape[1]), lambda i, s: (i, 0))
    return call(
        memory_kernel,
        info,
        [(d_ref, rows), weight] + [(array, rows) for array in came],
        [(d_ref.shape, bf16)],
        grid=(items,),
        out_specs=[rows],
        mega=12,
        name="memory_grad",
    )[0]


def stack_kernel(s_ref, one_ref, two_ref, three_ref, pre_ref, out_ref):
    out_ref[...] = jnp.zeros_like(out_ref)
    out_ref[0:8, :], out_ref[8:16, :], out_ref[16:24, :] = one_ref[...], two_ref[...], three_ref[...]
    out_ref[24:32, : pre_ref.shape[1]] = pre_ref[...]


SMALL = (0, 8, 16, 1, 9, 17, 2, 10, 18, 3, 11)


def small_kernel(s_ref, mine_ref, came_ref, self_ref, out_ref):
    out_ref[...] = jnp.zeros_like(out_ref)
    for to, at in enumerate(SMALL):
        out_ref[to : to + 1, :] = mine_ref[at : at + 1, :] + came_ref[at : at + 1, :]
    to = len(SMALL)
    out_ref[to : to + 1, :] = mine_ref[24:25, :] + came_ref[25:26, :]
    out_ref[to + 1 : to + 3, : self_ref.shape[1]] = self_ref[0:2, :]


def other_chip_kernel(blocks, s_ref, values, out):
    size, rows = values.shape[0] // blocks, out.shape[0] // blocks
    for block in range(blocks):
        to = spot_of(block, blocks) * rows
        start = block * size + (1 - s_ref[PLACE] // 2) * rows
        out[to : to + rows, :] = values[dyn(start, rows), :]


def chip_rows_kernel(blocks, s_ref, values, came, keep, first, second):
    size, rows = values.shape[0] // blocks, keep.shape[0] // blocks
    half = first.shape[1]
    for block in range(blocks):
        turned = spot_of(block, blocks)
        to = slice(turned * rows, (turned + 1) * rows)
        own = values[dyn(block * size + s_ref[PLACE] * rows, rows), :]
        keep[to, :] = add_low(own, came[dyn((2 * turned + s_ref[CORE_AT]) * rows, rows), :])
        other = values[dyn(block * size + (s_ref[PLACE] ^ CORE) * rows, rows), :]
        other = add_low(other, came[dyn((2 * turned + 1 - s_ref[CORE_AT]) * rows, rows), :])
        first[to, :] = other[:, :half]
        second[to, :] = other[:, half:]


def cross_rows_kernel(blocks, s_ref, *refs):
    send, keep = refs[9:]
    rows = refs[0].shape[0] // blocks
    for block in range(blocks):
        part = slice(block * rows, (block + 1) * rows)
        came = [
            jnp.concatenate([refs[3 * k + 1][part, :], refs[3 * k + 2][part, :]], axis=1)
            for k in range(3)
        ]
        values = [add_low(refs[0][part, :], came[0]), add_low(refs[3][part, :], came[1])]
        values.extend(halves(s_ref[CORE_AT], refs[6][part, :], came[2]))
        base = 4 * rows * (block % (blocks // 2))
        mine = s_ref[DP_AT] == block // (blocks // 2)
        for out, chosen in ((keep, mine), (send, jnp.logical_not(mine))):

            @pl.when(chosen)
            def _():
                for i, value in enumerate(values):
                    out[base + i * rows : base + (i + 1) * rows, :] = value


def general_cross_rows(d_q, d_back, d_kv, shard):
    dp_size, mem_size = lax.axis_size("dp"), lax.axis_size("mem")
    width = d_q.shape[1]

    def split(values, axis, bit, dim):
        mine = bit_at(axis, bit)
        entry = lambda at: lax.dynamic_index_in_dim(values, at, dim, keepdims=False)
        return entry(mine), entry(1 - mine)

    mem_dims = (2,) * len(bits_of("mem"))
    own = []
    for grad in (d_q, d_back):
        grad = grad.reshape((dp_size,) + mem_dims + (shard, width))
        for bit in chip_bits()[::-1]:
            grad = split(grad, "mem", bit, 1)[0]
        keep, send = split(grad, "mem", CORE, 1)
        own.append(add_low(keep, core_swap(send)))
    grad = d_kv.reshape((dp_size,) + mem_dims + (shard, width))
    for bit in chip_bits()[::-1]:
        keep, send = split(grad, "mem", bit, 1)
        grad = add_low(keep, swap(send, "mem", bit))
    keep, send = split(grad, "mem", CORE, 1)
    own = jnp.stack(own + list(halves(bit_at("mem", CORE), keep, core_swap(send))), axis=1)
    own = own.reshape((2,) * len(bits_of("dp")) + own.shape[1:])
    for bit in bits_of("dp")[::-1]:
        keep, send = split(own, "dp", bit, 0)
        own = add_low(keep, swap(send, "dp", bit))
    return own.astype(f32)


def local(
    dec_input,
    memory,
    dec_len,
    mem_len,
    self_in,
    self_in_bias,
    self_out,
    cross_in,
    cross_bias,
    cross_out,
    fc_in,
    fc_in_bias,
    fc_out,
    out_biases,
    norm_gains,
    norm_shifts,
    grad_out,
):
    items, steps, width = dec_input.shape
    mem_rows = memory.shape[1]
    local_width, hidden_width = self_in.shape[2], fc_in.shape[1]
    tokens = items * steps
    half, share = width // 2, tokens // 2
    dp_size, mem_size = lax.axis_size("dp"), lax.axis_size("mem")
    dp_bits = bits_of("dp")
    place = lax.axis_index("mem").astype(jnp.int32)
    core = bit_at("mem", CORE)
    numbers = [place, core, place * 0] + [bit_at("dp", bit) for bit in dp_bits]
    info = jnp.stack(numbers + [place * 0] * (LENS - len(numbers)))
    info = jnp.concatenate([info, mem_len, dec_len])

    x_low = dec_input.reshape(tokens, width)
    mem_low = memory.reshape(items * mem_rows, width)
    own_rows = pl.BlockSpec((share, width), lambda i, s: (s[CORE_AT], 0))
    columns = lambda values, at, size: lax.dynamic_slice_in_dim(values, at, size, 1)

    cross_pieces = relative({0: cross_in}, chip_bits())
    mem_far = core_swap(mem_low)
    bias_pair = jnp.concatenate([cross_bias.T, core_swap(cross_bias.T)], axis=0)
    bias_pieces = relative({0: bias_pair}, chip_bits())

    weight_self = jnp.transpose(self_in, (1, 0, 2))
    bias_self = self_in_bias.astype(f32)
    query_self = to_low(nn(x_low, weight_self[0]) + bias_self[0])
    key_self = to_low(nn(x_low, weight_self[1]))
    value_self = to_low(nn(x_low, weight_self[2]) + bias_self[1])
    (heads_self,) = call(
        functools.partial(self_forward_kernel, items),
        info,
        [query_self, key_self, value_self],
        [((tokens, local_width), bf16)],
        name="self_forward",
    )
    part_of = lambda core: lax.dynamic_slice_in_dim(heads_self, core * share, share, 0)
    came = core_swap(to_low(nn(part_of(1 - core), self_out)))
    attended = to_low(nn(part_of(core), self_out) + came.astype(f32))
    attended, attended_came = chip_swap(attended)

    points = (attended,) + tuple(bias_pieces.values())
    cross_pieces = {r: after(v, *points) if r else v for r, v in cross_pieces.items()}
    low_weight = [((width, width), bf16)]
    weight_kv, weight_query = assemble(
        info,
        relative(cross_pieces, [CORE]),
        ((0, width, half, 0, half), (0, 2 * width, half, half, half), (1, 0, 0, 0, width)),
        low_weight * 2,
        "cross_weights",
    )
    bias_pieces = {r: v[:2] for r, v in bias_pieces.items()} | {
        r ^ CORE: v[2:] for r, v in bias_pieces.items()
    }
    block = jnp.arange(width)[None, :] // local_width
    cross_shift = sum(
        jnp.where(block == (place ^ r), jnp.tile(v, (1, mem_size)).astype(f32), 0.0)
        for r, v in bias_pieces.items()
    )
    value_shift = lax.dynamic_slice_in_dim(cross_shift[1], core * half, half, 0)
    value_shift = jnp.concatenate([jnp.zeros((half,), f32), value_shift])
    vectors = jnp.concatenate(
        [
            norm_gains.astype(f32).T,
            norm_shifts.astype(f32).T,
            out_biases.astype(f32).T,
            jnp.zeros((7, width), f32),
        ],
        axis=0,
    )
    kv_near = to_low(nn(mem_low, weight_kv) + value_shift)
    kv_far = to_low(nn(mem_far, weight_kv) + value_shift)
    fc_in_far, fc_out_far = core_swap(after(fc_in, attended)), core_swap(after(fc_out, attended))
    fc_bias = fc_in_bias[None].astype(f32)
    fc_bias_far = core_swap(fc_in_bias)[None].astype(f32)

    token_f32, token_low = ((share, width), f32), ((share, width), bf16)
    token_half, one_each = ((share, half), bf16), ((share, 1), f32)
    normed_one, inverse_one, first_low, query_keep, query_send = call(
        first_norm_kernel,
        info,
        [(x_low, own_rows), attended, after(attended_came, kv_near, kv_far), vectors]
        + [cross_shift[:1], weight_query],
        [token_f32, one_each, token_low, token_half, token_half],
    )
    back_pieces = relative({0: after(cross_out, kv_near)}, chip_bits())
    back_pieces = {r: after(v, first_low) if r else v for r, v in back_pieces.items()}
    query_came = core_swap(query_send)
    (cross_back,) = assemble(
        info,
        relative(back_pieces, [CORE]),
        ((0, 0, 0, 0, width),),
        low_weight,
        "cross_back",
    )

    out, stat = cross_forward(info, items, query_keep, query_came, kv_near, kv_far)
    out = after(out, *back_pieces.values())
    for bit in chip_bits():
        out, stat = merge(info, bit, out, stat, swap(out, "mem", bit), swap(stat, "mem", bit))
    part_of_out = lambda core: lax.dynamic_slice_in_dim(out, core * share, share, 0)
    out_keep, out_came = part_of_out(core), core_swap(part_of_out(1 - core))

    units_low = ((share, hidden_width), bf16)
    weight = pltpu.VMEM((width, hidden_width), bf16)
    weight_out = pltpu.VMEM((hidden_width, width), bf16)
    cross_heads, normed_two, inverse_two, second_low, hidden, hidden_far, slope, slope_far, fed = call(
        middle_kernel,
        info,
        [normed_one, out_keep, out_came, vectors, fc_bias, fc_bias_far]
        + [(v, HBM) for v in (cross_back, fc_in, fc_in_far, fc_out, fc_out_far)],
        [token_low, token_f32, one_each, token_low] + [units_low] * 4 + [token_low],
        scratch=[
            pltpu.VMEM((width, width), bf16),
            weight,
            weight,
            weight_out,
            weight_out,
            pltpu.SemaphoreType.DMA((5,)),
        ],
        mega=20,
    )
    fed, fed_came = chip_swap(fed)
    second_other, hidden_other = core_swap(second_low), core_swap(hidden_far)
    final_low, d_three, d_three_low, d_pre, d_pre_far, d_fed, sums_three, pre_sums = call(
        turn_kernel,
        info,
        [normed_two, fed, fed_came, vectors, (grad_out.reshape(tokens, width), own_rows)]
        + [slope, slope_far]
        + [(v, HBM) for v in (fc_in, fc_in_far, fc_out, fc_out_far)],
        [token_low, token_f32, token_low, units_low, units_low, token_low]
        + [((8, width), f32), ((8, hidden_width), f32)],
        scratch=[weight, weight, weight_out, weight_out, pltpu.SemaphoreType.DMA((4,))],
        mega=20,
    )
    d_fed, d_fed_came = chip_swap(d_fed)

    order_one = dp_bits
    order_two = second_order(dp_bits)
    at_one, at_two = dp_position(order_one[0]), dp_position(order_two[0])
    d_three_other, d_pre_other = core_swap(d_three_low), core_swap(d_pre_far)
    fc_in_args = ([second_low, second_other], [d_pre, d_pre_other])
    fc_out_args = ([hidden, hidden_other], [d_three_low, d_three_other])
    upright = hidden_width == width
    if not upright:
        fc_in_args = fc_in_args[::-1]
    fc_in_send = grad_half(info, lambda s: 1 - s[at_one], *fc_in_args)
    fc_in_came = swap(fc_in_send, "dp", order_one[0])
    fc_out_send = grad_half(info, lambda s: 1 - s[at_two], *fc_out_args)
    fc_out_came = swap(fc_out_send, "dp", order_two[0])
    fc_in_keep = grad_half(info, lambda s: s[at_one], *fc_in_args)
    fc_out_keep = grad_half(info, lambda s: s[at_two], *fc_out_args)
    orders = (order_one, order_two)
    fc_sum = PairSum(
        info, orders, (fc_in_keep, fc_out_keep), (fc_in_came, fc_out_came)
    )

    final_came = core_swap(after(final_low, fc_out_send))
    block_output = jnp.concatenate(halves(core, final_low, final_came), axis=0)
    block_output = block_output.reshape(items, steps, width)
    d_fed_came = after(d_fed_came, fc_in_send, fc_out_send, fc_in_keep, fc_out_keep, block_output)
    d_two, d_two_low, d_keep, d_send, sums_two = call(
        second_back_kernel,
        info,
        [d_three, d_fed, d_fed_came, normed_two, inverse_two, vectors, cross_back],
        [token_f32, token_low, token_half, token_half, ((8, width), f32)],
    )
    d_came = core_swap(d_send)

    d_query_part, d_near, d_far = cross_backward(
        info, (query_keep, query_came), (d_keep, d_came), out, stat, kv_near, kv_far
    )
    d_query_part, d_query_came = chip_swap(d_query_part)
    flows_fc = [fc_sum]
    last = take_turns(flows_fc, d_query_part)

    d_kv = to_low(tn(mem_low, after(d_near, *last)) + tn(mem_far, d_far))
    shard = width // (dp_size * mem_size)
    simple = shard % 16 == 0 and mem_size == 4
    d_query_came = after(d_query_came, *take_turns(flows_fc, d_kv))
    if simple:
        (d_kv_send,) = call(
            functools.partial(other_chip_kernel, dp_size),
            info,
            [d_kv],
            [((width // 2, width), bf16)],
            name="other_chip",
        )
        d_kv_came = swap(d_kv_send, "mem", chip_bits()[0])
        d_query_came = after(d_query_came, d_kv_send)
    d_query_keep, d_query_send = call(
        split_sum_kernel, info, [d_query_part, d_query_came], [token_half, token_half]
    )
    d_query_send_came = core_swap(d_query_send)
    d_one_left, d_one_right, d_query_cross, sums_one = call(
        first_back_kernel,
        info,
        [d_two, d_query_keep, d_query_send_came, normed_one, inverse_one]
        + [vectors, weight_query],
        [token_half, token_half, token_low, ((8, width), f32)],
    )

    local_low = ((tokens, local_width), bf16)
    d_one_all, d_query, d_key, d_value, sums_self = call(
        functools.partial(self_backward_kernel, items),
        info,
        [query_self, key_self, value_self, d_one_left, d_one_right]
        + [core_swap(d_one_left), core_swap(d_one_right), self_out],
        [((tokens, width), bf16), local_low, local_low, local_low, ((8, local_width), f32)],
        scratch=[pltpu.VMEM((tokens, local_width), bf16)],
        name="self_backward",
    )

    self_args = (x_low, d_one_all, d_query, d_key, d_value, heads_self)
    self_one_send, self_two_send = self_grad(
        info, lambda s: 1 - s[at_one], lambda s: 3 - s[at_two], *self_args
    )
    self_one_came = swap(self_one_send, "dp", order_one[0])
    self_two_came = swap(self_two_send, "dp", order_two[0])
    last = (self_one_send, self_two_send)

    (small,) = call(
        stack_kernel,
        info,
        [sums_one, sums_two, after(sums_three, *last), pre_sums],
        [((32, width), f32)],
    )
    small_came = core_swap(small)
    self_one_keep, self_two_keep = self_grad(
        info, lambda s: s[at_one], lambda s: 2 + s[at_two], after(x_low, *last), *self_args[1:]
    )
    self_sum = PairSum(
        info, orders, (self_one_keep, self_two_keep), (self_one_came, self_two_came)
    )
    flows_self = [self_sum]
    last = (self_one_keep, self_two_keep)
    (fc_sum.extra,) = call(
        small_kernel, info, [small, after(small_came, *last), sums_self], [((16, width), f32)]
    )
    flows_self = [self_sum]

    chips = mem_size // 2
    shares = ((tokens, chips * local_width), bf16)
    partial, partial_send = call(
        input_part_kernel,
        info,
        [after(d_query, *last), d_key, d_value, weight_self],
        [shares, shares],
    )
    partial_came = core_swap(partial_send)

    if simple:
        q_keep, q_first, q_second, back_keep, back_first, back_second = cross_grad(
            info,
            dp_size,
            shard,
            [(after(first_low, *last), d_query_cross), (cross_heads, d_two_low)],
        )
        cross_parts = [q_keep, core_swap(q_first), core_swap(q_second)]
        cross_parts += [back_keep, core_swap(back_first), core_swap(back_second)]
        last = (q_keep,)
    last = take_turns(flows_fc, *last, partial)
    last = last + take_turns(flows_self, *last)
    if simple:
        rows = dp_size * shard
        d_kv_keep, d_kv_first, d_kv_second = call(
            functools.partial(chip_rows_kernel, dp_size),
            info,
            [d_kv, after(d_kv_came, *last)],
            [((rows, width), bf16), ((rows, half), bf16), ((rows, half), bf16)],
            name="chip_rows",
        )
        cross_parts += [d_kv_keep, core_swap(d_kv_first), core_swap(d_kv_second)]
        cross_send, cross_keep = call(
            functools.partial(cross_rows_kernel, dp_size),
            info,
            cross_parts,
            [((2 * rows, width), bf16)] * 2,
            name="cross_rows",
        )
        cross_sum = BlockSum(info, cross_keep, swap(cross_send, "dp", dp_bits[0]))
        last = last + (cross_send,)
    if chips == 2:
        input_grad, partial_send = call(
            input_sum_kernel,
            info,
            [partial, after(partial_came, *last), d_one_all],
            [((tokens, local_width), f32), local_low],
        )
        input_came = [swap(partial_send, "mem", chip_bits()[0])]
    else:
        partial = add_low(partial, partial_came)
        piece = lambda i: columns(partial, (place // 2 ^ i) * local_width, local_width)
        input_grad = columns(d_one_all, place * local_width, local_width).astype(f32)
        input_grad = input_grad + piece(0).astype(f32)
        input_came = [swap(piece(i), "mem", 2 * i) for i in range(1, chips)]
    flows_side = [cross_sum] if simple else []
    d_mem_far = memory_part(info, items, after(d_far, *last), weight_kv)
    last = take_turns(flows_self + flows_fc, *last, d_mem_far)
    last = last + take_turns(flows_side, *last)
    while len(fc_sum.back) > 2:
        last = take_turns(flows_self + flows_fc, *last)
    last = take_turns(flows_self, *last, *fc_sum.came) + fc_sum.advance_one(0, *last)
    d_mem_came = core_swap(after(d_mem_far, *last))
    last = last + take_turns(flows_self, *last)
    last = last + fc_sum.advance_one(1, *last)
    memory_grad = memory_part(info, items, after(d_near, *last), weight_kv, d_mem_came)
    fc_in_grad = fc_sum.whole(0, *last)
    while flows_side and not cross_sum.summed():
        last = last + take_turns(flows_side, *last)
    last = last + (memory_grad, fc_in_grad)
    while not self_sum.gathered():
        last = last + take_turns(flows_self, *last)
    input_came = [after(came, *last) for came in input_came]
    for came in input_came:
        input_grad = input_grad + came.astype(f32)
    input_grad = to_low(input_grad).reshape(items, steps, local_width)
    if not upright:
        fc_in_grad = fc_in_grad.T
    fc_out_grad = fc_sum.whole(1, *last)
    last = (fc_in_grad, fc_out_grad)
    self_in_grad, self_out_grad = call(
        functools.partial(self_finish_kernel, at_one, at_two),
        info,
        [self_sum.values[0], after(self_sum.came[0], *last)]
        + [self_sum.values[1], self_sum.came[1]],
        [((3, width, local_width), f32), ((local_width, width), f32)],
        name="self_finish",
    )
    self_in_grad = jnp.transpose(self_in_grad, (1, 0, 2))
    rows = fc_sum.extra_sum()
    spot = (lax.axis_index("dp") * mem_size + place) * shard
    owned = columns(rows, spot, shard)
    gains_grad, shifts_grad, out_biases_grad = owned[0:3].T, owned[3:6].T, owned[6:9].T
    cross_bias_grad = owned[9:11].T
    fc_in_bias_grad = rows[11, :hidden_width]
    self_in_bias_grad = rows[12:14, :local_width]
    if simple:
        cross_sum.arrived((after(cross_sum.pending()[0], *last),))
        cross_rows = cross_sum.total()
        q_rows, back_rows, left, right = (
            cross_rows[at * shard : (at + 1) * shard] for at in range(4)
        )
    else:
        d_q = to_low(tn(first_low, d_query_cross))
        d_back = to_low(tn(cross_heads, d_two_low))
        q_rows, back_rows, left, right = general_cross_rows(d_q, d_back, d_kv, shard)
    cross_in_grad = jnp.concatenate(
        [q_rows, left[:, :half], right[:, :half], left[:, half:], right[:, half:]], axis=1
    )
    cross_out_grad = back_rows

    return (
        block_output,
        input_grad,
        memory_grad.reshape(memory.shape),
        self_in_grad,
        self_in_bias_grad,
        self_out_grad,
        cross_in_grad,
        cross_bias_grad,
        cross_out_grad,
        fc_in_grad,
        fc_in_bias_grad,
        fc_out_grad,
        out_biases_grad,
        gains_grad,
        shifts_grad,
    )


def solution(mesh):
    placed = (
        P("dp", None, None),
        P("dp", "mem", None),
        P("dp"),
        P("dp"),
        P(None, None, "mem"),
        P(None, "mem"),
        P("mem", None),
        P("mem", None),
        P("mem", None),
        P("mem", None),
        P(None, "mem"),
        P("mem"),
        P("mem", None),
        P(),
        P(),
        P(),
        P("dp", None, None),
    )
    return jax.shard_map(
        local,
        mesh=mesh,
        in_specs=placed,
        out_specs=(
            P("dp", None, None),
            P("dp", None, "mem"),
            P("dp", "mem", None),
            P(None, None, "mem"),
            P(None, "mem"),
            P("mem", None),
            P(("dp", "mem"), None),
            P(("dp", "mem"), None),
            P(("dp", "mem"), None),
            P(None, "mem"),
            P("mem"),
            P("mem", None),
            P(("dp", "mem"), None),
            P(("dp", "mem"), None),
            P(("dp", "mem"), None),
        ),
        check_vma=False,
    )
```
